32 devices in a mesh: lev: 2 (over y), lat: 16 (over z, x, core).
Axes of the slice: x: 2, y: 2, z: 4, core: 2. Of those that a mesh axis runs over, the one named last changes fastest.
Arguments:
- tl_pert: float32 [8, 8, 32, 1440], P(None, 'lev', 'lat'), may hold values from -6 to 6
- adj_in: float32 [8, 8, 32, 1440], P(None, 'lev', 'lat'), may hold values from -6 to 6
- zonal_wind: float32 [8, 32, 1440], P('lev', 'lat'), may hold values from -3 to 3
- merid_wind: float32 [8, 32, 1440], P('lev', 'lat'), may hold values from -3 to 3
- vert_wind: float32 [8, 32, 1440], P('lev', 'lat'), may hold values from -3 to 3
- cutoffs: int32 [32], P('lat'), may hold values from 540 to 720
- remap: float32 [8, 8, 8], replicated, may hold values from -1.5 to 1.5
- phys_op: float32 [8, 8, 8], replicated, may hold values from -1 to 1
- phys_state: float32 [8, 32, 1440], P(None, 'lat', 'lev'), may hold values from 0.6 to 1.4
- column_cost: int32 [32, 2], P('lat', 'lev'), may hold values from 1 to 8, as said below
Outputs:
- tl_out: float32 [8, 8, 32, 1440], P(None, 'lev', 'lat')
- adj_out: float32 [8, 8, 32, 1440], P(None, 'lev', 'lat')
The draws below stay inside these ranges and needn't reach their ends.
Inputs may be any that keep to these rules, and one draw needn't show every extreme that they name: `column_cost`: the value 8 occurs in every draw.
All inputs are finite; a program needn't handle non-finite values.
Results may differ from the reference program's by a relative error of at most 0.0003.
Values sent between devices are 32-bit elements; how exact they have to be, the bound alone decides.
A program may use at most 64 MiB of HBM per device.

```python
import math
import jax
import jax.numpy as jnp
from jax import lax

LON = 1440
FIELDS = 8
LAT_DEV = 2
SUBS = 8
LEV = 8
LAT = 32
BCOL = 720
N_LEV = 2
N_LAT = 16


def level_matrix(key, diag_low, diag_high, off_scale):
    diag_key, off_key = jax.random.split(key)
    diagonal = jax.random.uniform(diag_key, (FIELDS, LEV), jnp.float32, diag_low, diag_high)
    spread = jax.random.normal(off_key, (FIELDS, LEV, LEV), jnp.float32)
    identity = (lax.broadcasted_iota(jnp.int32, (LEV, LEV), 0) == lax.broadcasted_iota(jnp.int32, (LEV, LEV), 1)).astype(jnp.float32)
    return spread * (off_scale * LEV ** (-0.5)) * (1.0 - identity) + identity * diagonal[:, :, None]


def draw_remap(key, part):
    return level_matrix(jax.random.fold_in(key, 3), 0.8, 1.2, 0.4)


def draw_phys_op(key, part):
    return level_matrix(jax.random.fold_in(key, 5), 0.6, 1.0, 0.25)


def draw_column_cost(key, part):
    band_row = lax.broadcasted_iota(jnp.int32, (LAT, N_LEV), 0)
    block_col = lax.broadcasted_iota(jnp.int32, (LAT, N_LEV), 1)
    latitude_band = band_row // LAT_DEV
    heavy_band = (latitude_band >= 3 * N_LAT // 8) & (latitude_band < 5 * N_LAT // 8)
    first_key, second_key = jax.random.split(jax.random.fold_in(key, 11))
    heavy_cost = jax.random.randint(first_key, (LAT, N_LEV), SUBS - 2, SUBS + 1)
    light_cost = jax.random.randint(second_key, (LAT, N_LEV), 1, 3)
    chosen = jnp.where(heavy_band, heavy_cost, light_cost)
    pinned = (band_row == 3 * N_LAT // 8 * LAT_DEV) & (block_col == 0)
    return jnp.where(pinned, SUBS, chosen).astype(jnp.int32)


def plant(entries, stream_key, least, largest):
    shape = entries.shape
    index_at = [jax.random.randint(jax.random.fold_in(stream_key, axis), (), 0, shape[axis]) for axis in range(len(shape))]
    entries = entries.at[tuple(index_at)].set(least)
    longest = shape.index(max(shape))
    index_at[longest] = (index_at[longest] + 1) % shape[longest]
    return entries.at[tuple(index_at)].set(largest)


def level_of(stream_key, shape, shards, least, largest):
    factor_of, own = 1.0, jax.random.fold_in(stream_key, 6)
    for position, parts in shards:
        draws = jnp.exp(jax.random.uniform(jax.random.fold_in(own, position), (parts,), jnp.float32, least / len(shards), largest / len(shards)))
        factor_of = factor_of * jnp.repeat(draws, shape[position] // parts).reshape([-1 if axis == position else 1 for axis in range(len(shape))])
    return factor_of


def noise(key, extent, deviation, limit, pieces=(), kind=jnp.bfloat16):
    result = deviation * jax.random.normal(key, extent, jnp.float32)
    if pieces:
        result = result * level_of(key, extent, pieces, -0.22, 0.18)
    return jnp.clip(result, -limit, limit).astype(kind)


def setup_inputs(seed: int = 0) -> dict:
    key_list = jax.random.split(jax.random.key(seed), 11)
    tl_pert = noise(key_list[0], (FIELDS, LEV, LAT, LON), 1.0, 6.0, ((1, 2), (2, 16)), jnp.float32)
    adj_in = noise(key_list[1], (FIELDS, LEV, LAT, LON), 1.0, 6.0, ((1, 2), (2, 16)), jnp.float32)
    zonal_wind = noise(key_list[2], (LEV, LAT, LON), 0.5, 3.0, ((0, 2), (1, 16)), jnp.float32)
    merid_wind = noise(key_list[3], (LEV, LAT, LON), 0.5, 3.0, ((0, 2), (1, 16)), jnp.float32)
    vert_wind = noise(key_list[4], (LEV, LAT, LON), 0.5, 3.0, ((0, 2), (1, 16)), jnp.float32)
    cutoffs = plant(jax.random.randint(key_list[5], (LAT,), 3 * LON // 8, LON // 2 + 1), jax.random.fold_in(key_list[5], 1), 3 * LON // 8, (LON // 2 + 1) - 1).astype(jnp.int32)
    remap = draw_remap(jax.random.fold_in(key_list[10], 71), 0)
    phys_op = draw_phys_op(jax.random.fold_in(key_list[10], 71), 0)
    phys_state = jnp.clip(jnp.exp(math.log(1.4) - 0.8472978 * jax.random.uniform(key_list[8], (LEV, LAT, LON), jnp.float32) ** level_of(key_list[8], (LEV, LAT, LON), ((1, 16), (2, 2)), -0.2, 0.2)), 0.6, 1.4)
    column_cost = draw_column_cost(jax.random.fold_in(key_list[10], 71), 0)
    return dict(tl_pert=tl_pert, adj_in=adj_in, zonal_wind=zonal_wind, merid_wind=merid_wind, vert_wind=vert_wind, cutoffs=cutoffs, remap=remap, phys_op=phys_op, phys_state=phys_state, column_cost=column_cost)


HIGHEST = lax.Precision.HIGHEST

def fourier_basis(length):
    sample = jnp.arange(length, dtype=jnp.int32)[:, None]
    column = jnp.arange(length, dtype=jnp.int32)[None, :]
    nyquist = length // 2
    wavenumber = jnp.where(column <= nyquist, column, column - nyquist)
    angles = (sample * wavenumber % length).astype(jnp.float32) * (2.0 * math.pi / length)
    weights = jnp.where((wavenumber == 0) | (wavenumber == nyquist), 1.0 / math.sqrt(length), math.sqrt(2.0 / length))
    basis_table = jnp.where(column <= nyquist, jnp.cos(angles), jnp.sin(angles)) * weights
    return (basis_table, wavenumber[0])

def polar_filter(grid_field, keep_mask, basis_table):
    coeffs = jnp.einsum('kix,xc->kic', grid_field, basis_table, precision=HIGHEST)
    return jnp.einsum('kic,xc->kix', coeffs * keep_mask, basis_table, precision=HIGHEST)

def tangent_advect(grid_field, zonal_wind, merid_wind, vert_wind):
    padded = jnp.pad(grid_field, ((1, 1), (1, 1), (0, 0)))
    lat_diff = padded[1:-1, 2:] - padded[1:-1, :-2]
    lev_diff = padded[2:, 1:-1] - padded[:-2, 1:-1]
    lon_diff = jnp.roll(grid_field, -1, axis=2) - jnp.roll(grid_field, 1, axis=2)
    return grid_field - 0.5 * (zonal_wind * lon_diff + merid_wind * lat_diff + vert_wind * lev_diff)

def adjoint_advect(grid_field, zonal_wind, merid_wind, vert_wind):
    zonal_part = zonal_wind * grid_field
    merid_pad = jnp.pad(merid_wind * grid_field, ((1, 1), (1, 1), (0, 0)))
    vert_pad = jnp.pad(vert_wind * grid_field, ((1, 1), (1, 1), (0, 0)))
    lon_term = jnp.roll(zonal_part, -1, axis=2) - jnp.roll(zonal_part, 1, axis=2)
    lat_term = merid_pad[1:-1, 2:] - merid_pad[1:-1, :-2]
    lev_term = vert_pad[2:, 1:-1] - vert_pad[:-2, 1:-1]
    return grid_field + 0.5 * (lon_term + lat_term + lev_term)

def physics_steps(grid_field, operator, state_factor, steps_map, adjoint):
    for sub_step in range(SUBS):
        if adjoint:
            advanced = state_factor * jnp.einsum('kl,lix->kix', operator, grid_field, precision=HIGHEST)
        else:
            advanced = jnp.einsum('kl,lix->kix', operator, state_factor * grid_field, precision=HIGHEST)
        grid_field = jnp.where(sub_step < steps_map, advanced, grid_field)
    return grid_field

def reference(tl_pert, adj_in, zonal_wind, merid_wind, vert_wind, cutoffs, remap, phys_op, phys_state, column_cost):
    basis_table, wavenumber = fourier_basis(LON)
    keep_mask = (wavenumber[None, :] <= cutoffs[:, None]).astype(jnp.float32)
    steps_map = jnp.repeat(column_cost, BCOL, axis=1)

    def per_field(inputs):
        pert_field, adj_field, remap_field, phys_field = inputs
        tl_advected = tangent_advect(pert_field, zonal_wind, merid_wind, vert_wind)
        tl_filtered = polar_filter(tl_advected, keep_mask, basis_table)
        tl_remapped = jnp.einsum('kl,lix->kix', remap_field, tl_filtered, precision=HIGHEST)
        tl_result = physics_steps(tl_remapped, phys_field, phys_state, steps_map, False)
        adj_physics = physics_steps(adj_field, phys_field.T, phys_state, steps_map, True)
        adj_remapped = jnp.einsum('lk,lix->kix', remap_field, adj_physics, precision=HIGHEST)
        adj_filtered = polar_filter(adj_remapped, keep_mask, basis_table)
        adj_result = adjoint_advect(adj_filtered, zonal_wind, merid_wind, vert_wind)
        return (tl_result, adj_result)
    tl_out, adj_out = lax.map(per_field, (tl_pert, adj_in, remap, phys_op))
    return (tl_out, adj_out)
```

```python
import functools
import math

import jax
import jax.numpy as jnp
import ml_dtypes
import numpy as np
from jax import lax
from jax.experimental import pallas as pl
from jax.experimental.pallas import tpu as pltpu
from jax.sharding import PartitionSpec as P

SUBS = 8


HIGHEST = lax.Precision.HIGHEST


def with_halo(cells, sides, width):
    for axis, dim in sides:
        count = lax.axis_size(axis)
        ends = count - 1
        head = lax.slice_in_dim(cells, 0, width, axis=dim)
        tail = lax.slice_in_dim(cells, cells.shape[dim] - width, cells.shape[dim], axis=dim)
        cells = jnp.concatenate(
            [
                lax.ppermute(tail, axis, [(i, (i + 1) % count) for i in range(ends)]),
                cells,
                lax.ppermute(head, axis, [((i + 1) % count, i) for i in range(ends)]),
            ],
            axis=dim,
        )
    return cells


def fourier_basis(length):
    sample = jnp.arange(length, dtype=jnp.int32)[:, None]
    column = jnp.arange(length, dtype=jnp.int32)[None, :]
    nyquist = length // 2
    wavenumber = jnp.where(column <= nyquist, column, column - nyquist)
    angles = (sample * wavenumber % length).astype(jnp.float32) * (2.0 * math.pi / length)
    weights = jnp.where(
        (wavenumber == 0) | (wavenumber == nyquist),
        1.0 / math.sqrt(length),
        math.sqrt(2.0 / length),
    )
    basis_table = jnp.where(column <= nyquist, jnp.cos(angles), jnp.sin(angles)) * weights
    return (basis_table, wavenumber[0])


def upper_modes(length):
    basis_table, wavenumber = fourier_basis(length)
    nyquist = length // 2
    lowest = 3 * length // 8 + 1
    cosine_part = basis_table[:, lowest : nyquist + 1]
    sine_part = basis_table[:, nyquist + lowest :]
    modes = jnp.concatenate([cosine_part, sine_part], axis=1)
    mode_numbers = jnp.concatenate(
        [wavenumber[lowest : nyquist + 1], wavenumber[nyquist + lowest :]]
    )
    return (modes, mode_numbers)


def polar_filter(grid_field, drop_mask, modes):
    coeffs = jnp.einsum("fkix,xc->fkic", grid_field, modes, precision=HIGHEST)
    return grid_field - jnp.einsum("fkic,xc->fkix", coeffs * drop_mask, modes, precision=HIGHEST)


def tangent_advect(grid_field, zonal_wind, merid_wind, vert_wind):
    padded = with_halo(grid_field, (("lev", 1), ("lat", 2)), 1)
    lat_diff = padded[:, 1:-1, 2:] - padded[:, 1:-1, :-2]
    lev_diff = padded[:, 2:, 1:-1] - padded[:, :-2, 1:-1]
    lon_diff = jnp.roll(grid_field, -1, axis=3) - jnp.roll(grid_field, 1, axis=3)
    return grid_field - 0.5 * (zonal_wind * lon_diff + merid_wind * lat_diff + vert_wind * lev_diff)


def adjoint_advect(grid_field, zonal_wind, merid_wind, vert_wind):
    merid_padded = with_halo(merid_wind * grid_field, (("lat", 2),), 1)
    vert_padded = with_halo(vert_wind * grid_field, (("lev", 1),), 1)
    zonal_part = zonal_wind * grid_field
    lon_term = jnp.roll(zonal_part, -1, axis=3) - jnp.roll(zonal_part, 1, axis=3)
    lat_term = merid_padded[:, :, 2:] - merid_padded[:, :, :-2]
    lev_term = vert_padded[:, 2:] - vert_padded[:, :-2]
    return grid_field + 0.5 * (lon_term + lat_term + lev_term)


def to_columns(stacked):
    return lax.all_to_all(stacked, "lev", split_axis=4, concat_axis=2, tiled=True)


def to_bands(stacked):
    return lax.all_to_all(stacked, "lev", split_axis=2, concat_axis=4, tiled=True)


def column_physics(operators, state_rows, fields_all, row_counts):
    unit_rows = jnp.ones_like(state_rows)
    before = jnp.stack([state_rows, unit_rows])[:, None]
    after = jnp.stack([unit_rows, state_rows])[:, None]
    counts_view = row_counts[None, None, None, :, None]
    current = fields_all
    for sub_step in range(SUBS):
        advanced = after * jnp.einsum(
            "sfkl,sflix->sfkix", operators, before * current, precision=HIGHEST
        )
        current = jnp.where(sub_step < counts_view, advanced, current)
    return current


def local(
    tl_pert,
    adj_in,
    zonal_wind,
    merid_wind,
    vert_wind,
    cutoffs,
    remap,
    phys_op,
    phys_state,
    column_cost,
):
    modes, mode_numbers = upper_modes(tl_pert.shape[3])
    drop_mask = (mode_numbers[None, :] > cutoffs[:, None]).astype(jnp.float32)
    operators = jnp.stack([phys_op, jnp.swapaxes(phys_op, 1, 2)])
    row_counts = column_cost[:, 0]
    adj_columns = to_columns(adj_in[None])
    tl_advected = tangent_advect(tl_pert, zonal_wind, merid_wind, vert_wind)
    tl_filtered = polar_filter(tl_advected, drop_mask, modes)
    tl_columns = to_columns(tl_filtered[None])
    tl_remapped = jnp.einsum("fkl,sflix->sfkix", remap, tl_columns, precision=HIGHEST)
    fields_all = jnp.concatenate([tl_remapped, adj_columns], axis=0)
    physics_done = column_physics(operators, phys_state, fields_all, row_counts)
    tl_finished = physics_done[0:1]
    adj_remapped = jnp.einsum("flk,sflix->sfkix", remap, physics_done[1:2], precision=HIGHEST)
    tl_result = to_bands(tl_finished)[0]
    adj_bands = to_bands(adj_remapped)[0]
    adj_filtered = polar_filter(adj_bands, drop_mask, modes)
    adj_result = adjoint_advect(adj_filtered, zonal_wind, merid_wind, vert_wind)
    return (tl_result, adj_result)

BF16 = jnp.bfloat16
F32 = jnp.float32
LANES = 128
MODES = 256
MESH_IDS = pl.DeviceIdType.MESH


def mode_tables(length, half, padded):
    nyquist = length // 2
    lowest = 3 * length // 8 + 1
    forward = np.zeros((2, 2, padded, MODES), ml_dtypes.bfloat16)
    backward = np.zeros((2, 2, MODES, padded), ml_dtypes.bfloat16)
    numbers = np.zeros((2, MODES), np.int32)
    sample = np.arange(half)
    for parity in range(2):
        cosines = [m for m in range(lowest, nyquist + 1) if m % 2 == parity]
        sines = [m for m in range(lowest, nyquist) if m % 2 == parity]
        waves = np.array(cosines + sines)
        count = len(waves)
        angles = 2.0 * np.pi / length * ((sample[:, None] * waves[None, :]) % length)
        is_cosine = (np.arange(count) < len(cosines))[None, :]
        weight = np.where(waves == nyquist, length**-0.5, (2.0 / length) ** 0.5)
        table = np.where(is_cosine, np.cos(angles), np.sin(angles)) * weight[None, :]
        high = table.astype(ml_dtypes.bfloat16)
        low = (table - high.astype(np.float64)).astype(ml_dtypes.bfloat16)
        for part, piece in enumerate((high, low)):
            forward[parity, part, :half, :count] = piece
            backward[parity, part, :count, :half] = piece.T
        numbers[parity, :count] = waves
    return forward, backward, numbers


def split_dot(rows, high, low):
    count = rows.shape[0]
    top = rows.astype(BF16)
    rest = (rows - top.astype(F32)).astype(BF16)
    both = jnp.dot(jnp.concatenate([top, rest], axis=0), high, preferred_element_type=F32)
    cross = jnp.dot(top, low, preferred_element_type=F32)
    return both[:count] + both[count:] + cross


def filter_in_place(buf, levels, mask, fwd, bwd):
    width = buf.shape[-1]
    rows = levels * 16
    first = buf[0].reshape(rows, width)
    second = buf[1].reshape(rows, width)
    dropped = []
    for parity, folded in enumerate((first + second, first - second)):
        coeffs = split_dot(folded, fwd[parity, 0], fwd[parity, 1])
        kept = coeffs.reshape(levels, 2, 8, MODES) * mask[parity][None]
        dropped.append(split_dot(kept.reshape(rows, MODES), bwd[parity, 0], bwd[parity, 1]))
    even, odd = dropped
    buf[0] = (first - (even + odd)).reshape(levels, 2, 8, width)
    buf[1] = (second - (even - odd)).reshape(levels, 2, 8, width)


def step_kernel(
    half,
    bands,
    tl,
    adj,
    winds,
    ops,
    counts,
    mask,
    fwd_hbm,
    bwd_hbm,
    out_tl,
    out_adj,
    fwd,
    bwd,
    qx,
    wext,
    acols,
    tbuf,
    tcols,
    aback,
    tback,
    abuf,
    mx,
    vx,
    mats,
    send_sem,
    recv_sem,
    load_sem,
):
    width = tl.shape[-1]
    tiles = width // LANES
    lev = lax.axis_index("lev")
    lat = lax.axis_index("lat")
    other = 1 - lev
    has_up = lat < bands - 1
    has_down = lat > 0

    loads = [
        pltpu.make_async_copy(fwd_hbm, fwd, load_sem.at[0]),
        pltpu.make_async_copy(bwd_hbm, bwd, load_sem.at[1]),
    ]

    barrier = pltpu.get_barrier_semaphore()
    pl.semaphore_signal(barrier, inc=1, device_id=(other, lat), device_id_type=MESH_IDS)

    @pl.when(has_up)
    def _():
        pl.semaphore_signal(barrier, inc=1, device_id=(lev, lat + 1), device_id_type=MESH_IDS)

    @pl.when(has_down)
    def _():
        pl.semaphore_signal(barrier, inc=1, device_id=(lev, lat - 1), device_id_type=MESH_IDS)

    inner = jnp.logical_and(has_up, has_down)

    @pl.when(inner)
    def _():
        pl.semaphore_wait(barrier, 3)

    @pl.when(jnp.logical_not(inner))
    def _():
        pl.semaphore_wait(barrier, 2)

    def remote(number, src, dst, to_lev, to_lat):
        return pltpu.make_async_remote_copy(
            src_ref=src,
            dst_ref=dst,
            send_sem=send_sem.at[number],
            recv_sem=recv_sem.at[number],
            device_id=(to_lev, to_lat),
            device_id_type=MESH_IDS,
        )

    edge = 3 * other
    lev_halo = remote(0, tl.at[:, edge], qx.at[:, 5 * lev, pl.ds(1, 2)], other, lat)
    lat_up = remote(1, tl.at[:, :, 1], qx.at[:, pl.ds(1, 4), 0], lev, lat + 1)
    lat_down = remote(2, tl.at[:, :, 0], qx.at[:, pl.ds(1, 4), 3], lev, lat - 1)
    wind_halo = remote(3, winds.at[edge, pl.ds(8, 8)], wext, other, lat)
    mine = pl.ds(4 * lev, 4)
    theirs = pl.ds(4 * other, 4)
    adj_out_cols = [
        remote(4 + i, adj.at[other, :, i], acols.at[mine, i], other, lat) for i in range(2)
    ]
    adj_in_bands = [
        remote(6 + i, aback.at[pl.ds(3 * other, 5), i], abuf.at[lev, :, i], other, lat)
        for i in range(2)
    ]
    tl_out_cols = [
        remote(8 + i, tbuf.at[other, :, i], tcols.at[mine, i], other, lat) for i in range(2)
    ]
    tl_in_bands = [
        remote(10 + i, tback.at[theirs, i], out_tl.at[lev, :, i], other, lat) for i in range(2)
    ]
    merid_up = remote(12, mx.at[:, :, 2], mx.at[:, :, 0], lev, lat + 1)
    merid_down = remote(13, mx.at[:, :, 1], mx.at[:, :, 3], lev, lat - 1)

    lev_halo.start()

    @pl.when(has_up)
    def _():
        lat_up.start()

    @pl.when(has_down)
    def _():
        lat_down.start()

    wind_halo.start()
    for copy in adj_out_cols:
        copy.start()
    for load in loads:
        load.start()

    zeros = jnp.zeros((8, width), F32)

    @pl.when(jnp.logical_not(has_down))
    def _():
        for h in range(2):
            for k in range(4):
                qx[h, 1 + k, 0] = zeros
                mx[h, k, 0] = zeros

    @pl.when(jnp.logical_not(has_up))
    def _():
        for h in range(2):
            for k in range(4):
                qx[h, 1 + k, 3] = zeros
                mx[h, k, 3] = zeros

    for h in range(2):
        for i in range(2):
            qx[h, 5 * lev, 1 + i] = zeros
            vx[h, 5 * lev, i] = zeros
    qx[:, 1:5, 1:3] = tl[...]
    acols[mine] = adj[lev]

    table = ops[...]
    for entry in range(128):
        mats[entry] = jnp.broadcast_to(table[:, entry : entry + 1], (8, LANES))

    lane = lax.broadcasted_iota(jnp.int32, (8, width), 1)

    def wind(ref_row):
        return jnp.broadcast_to(ref_row, (8, width))

    def lon_diff(z, across):
        after = jnp.where(lane == half - 1, across[:, 0:1], pltpu.roll(z, width - 1, 1))
        before = jnp.where(lane == 0, across[:, half - 1 : half], pltpu.roll(z, 1, 1))
        return after - before

    lev_halo.wait_recv()

    @pl.when(has_down)
    def _():
        lat_up.wait_recv()

    @pl.when(has_up)
    def _():
        lat_down.wait_recv()

    def advect(k, carry):
        for h in range(2):
            for i in range(2):
                row = 2 * h + i
                q = qx[h, k + 1, i + 1]
                zonal = wind(winds[k, row : row + 1]) * lon_diff(q, qx[1 - h, k + 1, i + 1])
                merid = wind(winds[k, 4 + row : 5 + row]) * (
                    qx[h, k + 1, i + 2] - qx[h, k + 1, i]
                )
                vert = wind(winds[k, 8 + row : 9 + row]) * (
                    qx[h, k + 2, i + 1] - qx[h, k, i + 1]
                )
                tbuf[h, k, i] = q - 0.5 * (zonal + merid + vert)
        return carry

    lax.fori_loop(0, 4, advect, 0)
    for load in loads:
        load.wait()
    filter_in_place(tbuf, 4, mask, fwd, bwd)
    for copy in tl_out_cols:
        copy.start()
    tcols[mine] = tbuf[lev]

    def product(base, transposed, vec):
        result = []
        for k in range(8):
            terms = [
                mats[base + (8 * l + k if transposed else 8 * k + l)] * vec[l] for l in range(8)
            ]
            while len(terms) > 1:
                terms = [a + b for a, b in zip(terms[::2], terms[1::2])]
            result.append(terms[0])
        return result

    def physics(src, dst, i, adjoint):
        steps = counts[i]

        def tile(t, carry):
            cols = pl.ds(pl.multiple_of(t * LANES, LANES), LANES)
            state = [
                jnp.broadcast_to(
                    winds[l // 2, 12 + 2 * (l % 2) + i : 13 + 2 * (l % 2) + i, cols], (8, LANES)
                )
                for l in range(8)
            ]
            vec = [src[l, i, :, cols] for l in range(8)]
            if not adjoint:
                vec = product(64, False, vec)

            def sub_step(s, vec):
                if adjoint:
                    new = [d * v for d, v in zip(state, product(0, True, vec))]
                else:
                    new = product(0, False, [d * v for d, v in zip(state, vec)])
                active = s < steps
                return [jnp.where(active, n, v) for n, v in zip(new, vec)]

            vec = lax.fori_loop(0, SUBS, sub_step, vec)
            if adjoint:
                vec = product(64, True, vec)
            for k in range(8):
                dst[k, i, :, cols] = vec[k]
            return carry

        lax.fori_loop(0, tiles, tile, 0)

    for i in range(2):
        adj_out_cols[i].wait_recv()
        physics(acols, aback, i, True)
        adj_in_bands[i].start()
    abuf[lev] = aback[pl.ds(3 * lev, 5)]

    for i in range(2):
        tl_out_cols[i].wait_recv()
        physics(tcols, tback, i, False)
        tl_in_bands[i].start()
    out_tl[lev] = tback[mine]

    wind_halo.wait_recv()
    for i in range(2):
        adj_in_bands[i].wait_recv()
    filter_in_place(abuf, 5, mask, fwd, bwd)

    def merid_parts(k, carry):
        for h in range(2):
            for i in range(2):
                row = 2 * h + i
                mx[h, k, i + 1] = wind(winds[k, 4 + row : 5 + row]) * abuf[h, k + lev, i]
        return carry

    lax.fori_loop(0, 4, merid_parts, 0)

    @pl.when(has_up)
    def _():
        merid_up.start()

    @pl.when(has_down)
    def _():
        merid_down.start()

    def vert_parts(k, carry):
        for h in range(2):
            for i in range(2):
                row = 2 * h + i
                vx[h, k + 1, i] = wind(winds[k, 8 + row : 9 + row]) * abuf[h, k + lev, i]
        return carry

    lax.fori_loop(0, 4, vert_parts, 0)
    for h in range(2):
        for i in range(2):
            row = 2 * h + i
            vx[h, 5 * other, i] = wind(wext[row : row + 1]) * abuf[h, 4 * other, i]

    def zonal_parts(k, carry):
        for i in range(2):
            p = [abuf[h, k + lev, i] for h in range(2)]
            z = [wind(winds[k, 2 * h + i : 2 * h + i + 1]) * p[h] for h in range(2)]
            for h in range(2):
                total = lon_diff(z[h], z[1 - h]) + (vx[h, k + 2, i] - vx[h, k, i])
                out_adj[h, k, i] = p[h] + 0.5 * total
        return carry

    lax.fori_loop(0, 4, zonal_parts, 0)

    @pl.when(has_down)
    def _():
        merid_up.wait_recv()

    @pl.when(has_up)
    def _():
        merid_down.wait_recv()

    def add_merid(k, carry):
        for h in range(2):
            for i in range(2):
                out_adj[h, k, i] = out_adj[h, k, i] + 0.5 * (mx[h, k, i + 2] - mx[h, k, i])
        return carry

    lax.fori_loop(0, 4, add_merid, 0)

    for copy in tl_in_bands:
        copy.wait_recv()
    for copy in [lev_halo, wind_halo] + adj_out_cols + adj_in_bands + tl_out_cols + tl_in_bands:
        copy.wait_send()

    @pl.when(has_up)
    def _():
        lat_up.wait_send()
        merid_up.wait_send()

    @pl.when(has_down)
    def _():
        lat_down.wait_send()
        merid_down.wait_send()


def one_kernel(
    tl_pert,
    adj_in,
    zonal_wind,
    merid_wind,
    vert_wind,
    cutoffs,
    remap,
    phys_op,
    phys_state,
    column_cost,
):
    length = tl_pert.shape[3]
    half = length // 2
    padded = -(-half // LANES) * LANES
    spare = padded - half
    bands = lax.axis_size("lat")
    forward, backward, numbers = mode_tables(length, half, padded)

    def to_kernel(field):
        halves = field.reshape(8, 4, 2, 2, half).transpose(3, 1, 2, 0, 4)
        return jnp.pad(halves, ((0, 0),) * 4 + ((0, spare),))

    def from_kernel(field):
        return field[..., :half].transpose(3, 1, 2, 0, 4).reshape(8, 4, 2, length)

    def wind_rows(field):
        return field.reshape(4, 2, 2, half).transpose(0, 2, 1, 3).reshape(4, 4, half)

    winds = jnp.concatenate(
        [
            wind_rows(zonal_wind),
            wind_rows(merid_wind),
            wind_rows(vert_wind),
            phys_state.reshape(4, 4, half),
        ],
        axis=1,
    )
    winds = jnp.pad(winds, ((0, 0), (0, 0), (0, spare)))
    ops = jnp.concatenate([phys_op.reshape(8, 64), remap.reshape(8, 64)], axis=1)
    counts = jnp.broadcast_to(column_cost[:, :, None], (2, 8, LANES))
    drop = (jnp.asarray(numbers)[:, None, None, :] > cutoffs[None, :, None, None]).astype(F32)
    mask = jnp.broadcast_to(drop, (2, 2, 8, MODES))

    vmem = pl.BlockSpec(memory_space=pltpu.VMEM)
    hbm = pl.BlockSpec(memory_space=pl.ANY)
    band_shape = (2, 4, 2, 8, padded)
    column_shape = (8, 2, 8, padded)
    outs = pl.pallas_call(
        functools.partial(step_kernel, half, bands),
        out_shape=[jax.ShapeDtypeStruct(band_shape, F32)] * 2,
        in_specs=[vmem] * 6 + [hbm] * 2,
        out_specs=[vmem] * 2,
        scratch_shapes=[
            pltpu.VMEM(forward.shape, BF16),
            pltpu.VMEM(backward.shape, BF16),
            pltpu.VMEM((2, 6, 4, 8, padded), F32),
            pltpu.VMEM((8, padded), F32),
            pltpu.VMEM(column_shape, F32),
            pltpu.VMEM(band_shape, F32),
            pltpu.VMEM(column_shape, F32),
            pltpu.VMEM(column_shape, F32),
            pltpu.VMEM(column_shape, F32),
            pltpu.VMEM((2, 5, 2, 8, padded), F32),
            pltpu.VMEM((2, 4, 4, 8, padded), F32),
            pltpu.VMEM((2, 6, 2, 8, padded), F32),
            pltpu.VMEM((128, 8, LANES), F32),
            pltpu.SemaphoreType.DMA((14,)),
            pltpu.SemaphoreType.DMA((14,)),
            pltpu.SemaphoreType.DMA((2,)),
        ],
        compiler_params=pltpu.CompilerParams(
            collective_id=0, has_side_effects=True, vmem_limit_bytes=40 * 1024 * 1024
        ),
        cost_estimate=pl.CostEstimate(
            flops=10**9, bytes_accessed=8 * 10**6, transcendentals=0
        ),
    )(
        to_kernel(tl_pert),
        to_kernel(adj_in),
        winds,
        ops,
        counts,
        mask,
        jnp.asarray(forward),
        jnp.asarray(backward),
    )
    return from_kernel(outs[0]), from_kernel(outs[1])


def fits_kernel(mesh):
    return mesh.shape["lev"] == 2 and mesh.shape["lat"] > 1


def solution(mesh):
    placed = (
        P(None, "lev", "lat", None),
        P(None, "lev", "lat", None),
        P("lev", "lat", None),
        P("lev", "lat", None),
        P("lev", "lat", None),
        P("lat"),
        P(),
        P(),
        P(None, "lat", "lev"),
        P("lat", "lev"),
    )
    return jax.shard_map(
        one_kernel if fits_kernel(mesh) else local,
        mesh=mesh,
        in_specs=placed,
        out_specs=(P(None, "lev", "lat", None), P(None, "lev", "lat", None)),
        check_vma=False,
    )
```

```python
import functools
import math

import jax
import jax.numpy as jnp
import ml_dtypes
import numpy as np
from jax import lax
from jax.experimental import pallas as pl
from jax.experimental.pallas import tpu as pltpu
from jax.sharding import PartitionSpec as P

SUBS = 8


HIGHEST = lax.Precision.HIGHEST


def with_halo(cells, sides, width):
    for axis, dim in sides:
        count = lax.axis_size(axis)
        ends = count - 1
        head = lax.slice_in_dim(cells, 0, width, axis=dim)
        tail = lax.slice_in_dim(cells, cells.shape[dim] - width, cells.shape[dim], axis=dim)
        cells = jnp.concatenate(
            [
                lax.ppermute(tail, axis, [(i, (i + 1) % count) for i in range(ends)]),
                cells,
                lax.ppermute(head, axis, [((i + 1) % count, i) for i in range(ends)]),
            ],
            axis=dim,
        )
    return cells


def fourier_basis(length):
    sample = jnp.arange(length, dtype=jnp.int32)[:, None]
    column = jnp.arange(length, dtype=jnp.int32)[None, :]
    nyquist = length // 2
    wavenumber = jnp.where(column <= nyquist, column, column - nyquist)
    angles = (sample * wavenumber % length).astype(jnp.float32) * (2.0 * math.pi / length)
    weights = jnp.where(
        (wavenumber == 0) | (wavenumber == nyquist),
        1.0 / math.sqrt(length),
        math.sqrt(2.0 / length),
    )
    basis_table = jnp.where(column <= nyquist, jnp.cos(angles), jnp.sin(angles)) * weights
    return (basis_table, wavenumber[0])


def upper_modes(length):
    basis_table, wavenumber = fourier_basis(length)
    nyquist = length // 2
    lowest = 3 * length // 8 + 1
    cosine_part = basis_table[:, lowest : nyquist + 1]
    sine_part = basis_table[:, nyquist + lowest :]
    modes = jnp.concatenate([cosine_part, sine_part], axis=1)
    mode_numbers = jnp.concatenate(
        [wavenumber[lowest : nyquist + 1], wavenumber[nyquist + lowest :]]
    )
    return (modes, mode_numbers)


def polar_filter(grid_field, drop_mask, modes):
    coeffs = jnp.einsum("fkix,xc->fkic", grid_field, modes, precision=HIGHEST)
    return grid_field - jnp.einsum("fkic,xc->fkix", coeffs * drop_mask, modes, precision=HIGHEST)


def tangent_advect(grid_field, zonal_wind, merid_wind, vert_wind):
    padded = with_halo(grid_field, (("lev", 1), ("lat", 2)), 1)
    lat_diff = padded[:, 1:-1, 2:] - padded[:, 1:-1, :-2]
    lev_diff = padded[:, 2:, 1:-1] - padded[:, :-2, 1:-1]
    lon_diff = jnp.roll(grid_field, -1, axis=3) - jnp.roll(grid_field, 1, axis=3)
    return grid_field - 0.5 * (zonal_wind * lon_diff + merid_wind * lat_diff + vert_wind * lev_diff)


def adjoint_advect(grid_field, zonal_wind, merid_wind, vert_wind):
    merid_padded = with_halo(merid_wind * grid_field, (("lat", 2),), 1)
    vert_padded = with_halo(vert_wind * grid_field, (("lev", 1),), 1)
    zonal_part = zonal_wind * grid_field
    lon_term = jnp.roll(zonal_part, -1, axis=3) - jnp.roll(zonal_part, 1, axis=3)
    lat_term = merid_padded[:, :, 2:] - merid_padded[:, :, :-2]
    lev_term = vert_padded[:, 2:] - vert_padded[:, :-2]
    return grid_field + 0.5 * (lon_term + lat_term + lev_term)


def to_columns(stacked):
    return lax.all_to_all(stacked, "lev", split_axis=4, concat_axis=2, tiled=True)


def to_bands(stacked):
    return lax.all_to_all(stacked, "lev", split_axis=2, concat_axis=4, tiled=True)


def column_physics(operators, state_rows, fields_all, row_counts):
    unit_rows = jnp.ones_like(state_rows)
    before = jnp.stack([state_rows, unit_rows])[:, None]
    after = jnp.stack([unit_rows, state_rows])[:, None]
    counts_view = row_counts[None, None, None, :, None]
    current = fields_all
    for sub_step in range(SUBS):
        advanced = after * jnp.einsum(
            "sfkl,sflix->sfkix", operators, before * current, precision=HIGHEST
        )
        current = jnp.where(sub_step < counts_view, advanced, current)
    return current


def local(
    tl_pert,
    adj_in,
    zonal_wind,
    merid_wind,
    vert_wind,
    cutoffs,
    remap,
    phys_op,
    phys_state,
    column_cost,
):
    modes, mode_numbers = upper_modes(tl_pert.shape[3])
    drop_mask = (mode_numbers[None, :] > cutoffs[:, None]).astype(jnp.float32)
    operators = jnp.stack([phys_op, jnp.swapaxes(phys_op, 1, 2)])
    row_counts = column_cost[:, 0]
    adj_columns = to_columns(adj_in[None])
    tl_advected = tangent_advect(tl_pert, zonal_wind, merid_wind, vert_wind)
    tl_filtered = polar_filter(tl_advected, drop_mask, modes)
    tl_columns = to_columns(tl_filtered[None])
    tl_remapped = jnp.einsum("fkl,sflix->sfkix", remap, tl_columns, precision=HIGHEST)
    fields_all = jnp.concatenate([tl_remapped, adj_columns], axis=0)
    physics_done = column_physics(operators, phys_state, fields_all, row_counts)
    tl_finished = physics_done[0:1]
    adj_remapped = jnp.einsum("flk,sflix->sfkix", remap, physics_done[1:2], precision=HIGHEST)
    tl_result = to_bands(tl_finished)[0]
    adj_bands = to_bands(adj_remapped)[0]
    adj_filtered = polar_filter(adj_bands, drop_mask, modes)
    adj_result = adjoint_advect(adj_filtered, zonal_wind, merid_wind, vert_wind)
    return (tl_result, adj_result)

BF16 = jnp.bfloat16
F32 = jnp.float32
LANES = 128
MODES = 256
MESH_IDS = pl.DeviceIdType.MESH


def mode_tables(length, half, padded):
    nyquist = length // 2
    lowest = 3 * length // 8 + 1
    forward = np.zeros((2, 2, padded, MODES), ml_dtypes.bfloat16)
    backward = np.zeros((2, 2, MODES, padded), ml_dtypes.bfloat16)
    layout = []
    sample = np.arange(half)
    for parity in range(2):
        cosines = [m for m in range(lowest, nyquist + 1) if m % 2 == parity]
        sines = [m for m in range(lowest, nyquist) if m % 2 == parity]
        waves = np.array(cosines + sines)
        count = len(waves)
        angles = 2.0 * np.pi / length * ((sample[:, None] * waves[None, :]) % length)
        is_cosine = (np.arange(count) < len(cosines))[None, :]
        weight = np.where(waves == nyquist, length**-0.5, (2.0 / length) ** 0.5)
        table = np.where(is_cosine, np.cos(angles), np.sin(angles)) * weight[None, :]
        high = table.astype(ml_dtypes.bfloat16)
        low = (table - high.astype(np.float64)).astype(ml_dtypes.bfloat16)
        for part, piece in enumerate((high, low)):
            forward[parity, part, :half, :count] = piece
            backward[parity, part, :count, :half] = piece.T
        layout.append((cosines[0], len(cosines), count))
    return forward, backward, tuple(layout)


def split_dot(rows, high, low):
    count = rows.shape[0]
    top = rows.astype(BF16)
    rest = (rows - top.astype(F32)).astype(BF16)
    both = jnp.dot(jnp.concatenate([top, rest], axis=0), high, preferred_element_type=F32)
    cross = jnp.dot(top, low, preferred_element_type=F32)
    return both[:count] + both[count:] + cross


def filter_in_place(buf, levels, mask, fwd, bwd):
    width = buf.shape[-1]
    rows = levels * 16
    first = buf[0].reshape(rows, width)
    second = buf[1].reshape(rows, width)
    dropped = []
    for parity, folded in enumerate((first + second, first - second)):
        coeffs = split_dot(folded, fwd[parity, 0], fwd[parity, 1])
        kept = coeffs.reshape(levels, 2, 8, MODES) * mask[parity][None]
        dropped.append(split_dot(kept.reshape(rows, MODES), bwd[parity, 0], bwd[parity, 1]))
    even, odd = dropped
    buf[0] = (first - (even + odd)).reshape(levels, 2, 8, width)
    buf[1] = (second - (even - odd)).reshape(levels, 2, 8, width)


def step_kernel(
    half,
    bands,
    layout,
    cutoffs,
    cost,
    tl_hbm,
    adj_hbm,
    zonal_hbm,
    merid_hbm,
    vert_hbm,
    state_hbm,
    op_hbm,
    remap_hbm,
    fwd_hbm,
    bwd_hbm,
    out_tl,
    out_adj,
    tl,
    adj,
    zonal_raw,
    merid_raw,
    vert_raw,
    state_raw,
    op_raw,
    remap_raw,
    fwd,
    bwd,
    winds,
    qx,
    wext,
    ah,
    acols,
    tbuf,
    tcols,
    aback,
    tback,
    tband,
    abuf,
    mx,
    vx,
    part,
    spread,
    mats,
    mask,
    send_sem,
    recv_sem,
    load_sem,
):
    width = qx.shape[-1]
    tiles = width // LANES
    lev = lax.axis_index("lev")
    lat = lax.axis_index("lat")
    other = 1 - lev
    has_up = lat < bands - 1
    has_down = lat > 0

    loads = [
        pltpu.make_async_copy(src, dst, load_sem.at[number])
        for number, (src, dst) in enumerate(
            [
                (tl_hbm, tl),
                (adj_hbm, adj),
                (zonal_hbm, zonal_raw),
                (merid_hbm, merid_raw),
                (vert_hbm, vert_raw),
                (state_hbm, state_raw),
                (op_hbm, op_raw),
                (remap_hbm, remap_raw),
                (fwd_hbm, fwd),
                (bwd_hbm, bwd),
            ]
        )
    ]
    for load in loads:
        load.start()

    barrier = pltpu.get_barrier_semaphore()
    pl.semaphore_signal(barrier, inc=1, device_id=(other, lat), device_id_type=MESH_IDS)

    @pl.when(has_up)
    def _():
        pl.semaphore_signal(barrier, inc=1, device_id=(lev, lat + 1), device_id_type=MESH_IDS)

    @pl.when(has_down)
    def _():
        pl.semaphore_signal(barrier, inc=1, device_id=(lev, lat - 1), device_id_type=MESH_IDS)

    inner = jnp.logical_and(has_up, has_down)

    @pl.when(inner)
    def _():
        pl.semaphore_wait(barrier, 3)

    @pl.when(jnp.logical_not(inner))
    def _():
        pl.semaphore_wait(barrier, 2)

    def remote(number, src, dst, to_lev, to_lat):
        return pltpu.make_async_remote_copy(
            src_ref=src,
            dst_ref=dst,
            send_sem=send_sem.at[number],
            recv_sem=recv_sem.at[number],
            device_id=(to_lev, to_lat),
            device_id_type=MESH_IDS,
        )

    edge = 3 * other
    lev_halo = remote(0, qx.at[:, 1 + edge, pl.ds(1, 2)], qx.at[:, 5 * lev, pl.ds(1, 2)], other, lat)
    lat_up = remote(1, qx.at[:, pl.ds(1, 4), 2], qx.at[:, pl.ds(1, 4), 0], lev, lat + 1)
    lat_down = remote(2, qx.at[:, pl.ds(1, 4), 1], qx.at[:, pl.ds(1, 4), 3], lev, lat - 1)
    wind_halo = remote(3, winds.at[edge, pl.ds(8, 8)], wext, other, lat)
    mine = pl.ds(4 * lev, 4)
    theirs = pl.ds(4 * other, 4)
    adj_out_cols = [
        remote(4 + i, ah.at[other, :, i], acols.at[mine, i], other, lat) for i in range(2)
    ]
    adj_in_bands = [
        remote(6 + i, aback.at[pl.ds(3 * other, 5), i], abuf.at[lev, :, i], other, lat)
        for i in range(2)
    ]
    tl_out_cols = [
        remote(8 + i, tbuf.at[other, :, i], tcols.at[mine, i], other, lat) for i in range(2)
    ]
    tl_in_bands = [
        remote(10 + i, tback.at[theirs, i], tband.at[lev, :, i], other, lat) for i in range(2)
    ]
    merid_up = remote(12, mx.at[:, :, 2], mx.at[:, :, 0], lev, lat + 1)
    merid_down = remote(13, mx.at[:, :, 1], mx.at[:, :, 3], lev, lat - 1)

    def halves(row):
        first = jnp.concatenate([row[:, :half], jnp.zeros((8, width - half), F32)], axis=1)
        second = jnp.concatenate([row[:, half:], jnp.zeros((8, width - half), F32)], axis=1)
        return first, second

    loads[0].wait()
    for k in range(4):
        for i in range(2):
            for h, block in enumerate(halves(tl[:, k, i, :])):
                qx[h, 1 + k, 1 + i] = block
    lev_halo.start()

    @pl.when(has_up)
    def _():
        lat_up.start()

    @pl.when(has_down)
    def _():
        lat_down.start()

    for load in loads[1:6]:
        load.wait()
    blank = jnp.zeros((4, width - half), F32)
    for k in range(4):
        for first, raw in ((0, zonal_raw), (4, merid_raw), (8, vert_raw)):
            for h in range(2):
                for i in range(2):
                    winds[k, first + 2 * h + i : first + 2 * h + i + 1, :half] = raw[
                        k, i : i + 1, h * half : (h + 1) * half
                    ]
            winds[k, first : first + 4, half:] = blank
        for l in range(2):
            winds[k, 12 + 2 * l : 14 + 2 * l, :half] = state_raw[2 * k + l]
        winds[k, 12:16, half:] = blank
    wind_halo.start()
    for i in range(2):
        for k in range(4):
            for h, block in enumerate(halves(adj[:, k, i, :])):
                ah[h, k, i] = block
        adj_out_cols[i].start()
    acols[mine] = ah[lev]

    zeros = jnp.zeros((8, width), F32)

    @pl.when(jnp.logical_not(has_down))
    def _():
        for h in range(2):
            for k in range(4):
                qx[h, 1 + k, 0] = zeros
                mx[h, k, 0] = zeros

    @pl.when(jnp.logical_not(has_up))
    def _():
        for h in range(2):
            for k in range(4):
                qx[h, 1 + k, 3] = zeros
                mx[h, k, 3] = zeros

    for h in range(2):
        for i in range(2):
            qx[h, 5 * lev, 1 + i] = zeros
            vx[h, 5 * lev, i] = zeros

    for load in loads[6:8]:
        load.wait()
    for base, raw in ((0, op_raw), (64, remap_raw)):
        for f in range(8):
            table = raw[f]
            for l in range(8):
                at = (f * 8 + l) * 8
                spread[at : at + 8, :] = jnp.broadcast_to(table[:, l : l + 1], (8, LANES))
        for k in range(8):
            for l in range(8):
                mats[base + 8 * k + l] = spread[pl.ds(8 * l + k, 8, stride=64), :]

    column = lax.broadcasted_iota(jnp.int32, (8, MODES), 1)
    for parity, (first, cosines, count) in enumerate(layout):
        number = first + 2 * jnp.where(column < cosines, column, column - cosines)
        for i in range(2):
            drop = jnp.logical_and(number > cutoffs[i], column < count)
            mask[parity, i] = jnp.where(drop, 1.0, 0.0).astype(F32)

    lane = lax.broadcasted_iota(jnp.int32, (8, width), 1)

    def wind(ref_row):
        return jnp.broadcast_to(ref_row, (8, width))

    def lon_diff(z, across):
        after = jnp.where(lane == half - 1, across[:, 0:1], pltpu.roll(z, width - 1, 1))
        before = jnp.where(lane == 0, across[:, half - 1 : half], pltpu.roll(z, 1, 1))
        return after - before

    lev_halo.wait_recv()

    @pl.when(has_down)
    def _():
        lat_up.wait_recv()

    @pl.when(has_up)
    def _():
        lat_down.wait_recv()

    def advect(k, carry):
        for h in range(2):
            for i in range(2):
                row = 2 * h + i
                q = qx[h, k + 1, i + 1]
                zonal = wind(winds[k, row : row + 1]) * lon_diff(q, qx[1 - h, k + 1, i + 1])
                merid = wind(winds[k, 4 + row : 5 + row]) * (
                    qx[h, k + 1, i + 2] - qx[h, k + 1, i]
                )
                vert = wind(winds[k, 8 + row : 9 + row]) * (
                    qx[h, k + 2, i + 1] - qx[h, k, i + 1]
                )
                tbuf[h, k, i] = q - 0.5 * (zonal + merid + vert)
        return carry

    lax.fori_loop(0, 4, advect, 0)
    for load in loads[8:]:
        load.wait()
    filter_in_place(tbuf, 4, mask, fwd, bwd)
    for copy in tl_out_cols:
        copy.start()
    tcols[mine] = tbuf[lev]

    def product(base, transposed, vec):
        result = []
        for k in range(8):
            terms = [
                mats[base + (8 * l + k if transposed else 8 * k + l)] * vec[l] for l in range(8)
            ]
            while len(terms) > 1:
                terms = [a + b for a, b in zip(terms[::2], terms[1::2])]
            result.append(terms[0])
        return result

    def physics(src, dst, i, adjoint):
        steps = jnp.full((8, LANES), cost[i, 0], jnp.int32)

        def tile(t, carry):
            cols = pl.ds(pl.multiple_of(t * LANES, LANES), LANES)
            state = [
                jnp.broadcast_to(
                    winds[l // 2, 12 + 2 * (l % 2) + i : 13 + 2 * (l % 2) + i, cols], (8, LANES)
                )
                for l in range(8)
            ]
            vec = [src[l, i, :, cols] for l in range(8)]
            if not adjoint:
                vec = product(64, False, vec)

            def sub_step(s, vec):
                if adjoint:
                    new = [d * v for d, v in zip(state, product(0, True, vec))]
                else:
                    new = product(0, False, [d * v for d, v in zip(state, vec)])
                active = s < steps
                return [jnp.where(active, n, v) for n, v in zip(new, vec)]

            vec = lax.fori_loop(0, SUBS, sub_step, vec)
            if adjoint:
                vec = product(64, True, vec)
            for k in range(8):
                dst[k, i, :, cols] = vec[k]
            return carry

        lax.fori_loop(0, tiles, tile, 0)

    for i in range(2):
        adj_out_cols[i].wait_recv()
        physics(acols, aback, i, True)
        adj_in_bands[i].start()
    abuf[lev] = aback[pl.ds(3 * lev, 5)]

    for i in range(2):
        tl_out_cols[i].wait_recv()
        physics(tcols, tback, i, False)
        tl_in_bands[i].start()
    tband[lev] = tback[mine]

    wind_halo.wait_recv()
    for i in range(2):
        adj_in_bands[i].wait_recv()
    filter_in_place(abuf, 5, mask, fwd, bwd)

    def merid_parts(k, carry):
        for h in range(2):
            for i in range(2):
                row = 2 * h + i
                mx[h, k, i + 1] = wind(winds[k, 4 + row : 5 + row]) * abuf[h, k + lev, i]
        return carry

    lax.fori_loop(0, 4, merid_parts, 0)

    @pl.when(has_up)
    def _():
        merid_up.start()

    @pl.when(has_down)
    def _():
        merid_down.start()

    def vert_parts(k, carry):
        for h in range(2):
            for i in range(2):
                row = 2 * h + i
                vx[h, k + 1, i] = wind(winds[k, 8 + row : 9 + row]) * abuf[h, k + lev, i]
        return carry

    lax.fori_loop(0, 4, vert_parts, 0)
    for h in range(2):
        for i in range(2):
            row = 2 * h + i
            vx[h, 5 * other, i] = wind(wext[row : row + 1]) * abuf[h, 4 * other, i]

    def zonal_parts(k, carry):
        for i in range(2):
            p = [abuf[h, k + lev, i] for h in range(2)]
            z = [wind(winds[k, 2 * h + i : 2 * h + i + 1]) * p[h] for h in range(2)]
            for h in range(2):
                total = lon_diff(z[h], z[1 - h]) + (vx[h, k + 2, i] - vx[h, k, i])
                part[h, k, i] = p[h] + 0.5 * total
        return carry

    lax.fori_loop(0, 4, zonal_parts, 0)

    def join(pair):
        return jnp.concatenate([block[:, :half] for block in pair], axis=1)

    for copy in tl_in_bands:
        copy.wait_recv()
    for k in range(4):
        for i in range(2):
            out_tl[:, k, i, :] = join([tband[h, k, i] for h in range(2)])

    @pl.when(has_down)
    def _():
        merid_up.wait_recv()

    @pl.when(has_up)
    def _():
        merid_down.wait_recv()

    for k in range(4):
        for i in range(2):
            out_adj[:, k, i, :] = join(
                [
                    part[h, k, i] + 0.5 * (mx[h, k, i + 2] - mx[h, k, i])
                    for h in range(2)
                ]
            )

    for copy in [lev_halo, wind_halo] + adj_out_cols + adj_in_bands + tl_out_cols + tl_in_bands:
        copy.wait_send()

    @pl.when(has_up)
    def _():
        lat_up.wait_send()
        merid_up.wait_send()

    @pl.when(has_down)
    def _():
        lat_down.wait_send()
        merid_down.wait_send()


def one_kernel(
    tl_pert,
    adj_in,
    zonal_wind,
    merid_wind,
    vert_wind,
    cutoffs,
    remap,
    phys_op,
    phys_state,
    column_cost,
):
    length = tl_pert.shape[3]
    half = length // 2
    padded = -(-half // LANES) * LANES
    bands = lax.axis_size("lat")
    forward, backward, layout = mode_tables(length, half, padded)
    vmem = pl.BlockSpec(memory_space=pltpu.VMEM)
    smem = pl.BlockSpec(memory_space=pltpu.SMEM)
    hbm = pl.BlockSpec(memory_space=pl.ANY)
    band_shape = (2, 4, 2, 8, padded)
    column_shape = (8, 2, 8, padded)
    fields = [tl_pert, adj_in, zonal_wind, merid_wind, vert_wind, phys_state, phys_op, remap]
    return pl.pallas_call(
        functools.partial(step_kernel, half, bands, layout),
        out_shape=[jax.ShapeDtypeStruct(tl_pert.shape, F32)] * 2,
        in_specs=[smem] * 2 + [hbm] * 10,
        out_specs=[vmem] * 2,
        scratch_shapes=[pltpu.VMEM(field.shape, F32) for field in fields]
        + [
            pltpu.VMEM(forward.shape, BF16),
            pltpu.VMEM(backward.shape, BF16),
            pltpu.VMEM((4, 16, padded), F32),
            pltpu.VMEM((2, 6, 4, 8, padded), F32),
            pltpu.VMEM((8, padded), F32),
            pltpu.VMEM(band_shape, F32),
            pltpu.VMEM(column_shape, F32),
            pltpu.VMEM(band_shape, F32),
            pltpu.VMEM(column_shape, F32),
            pltpu.VMEM(column_shape, F32),
            pltpu.VMEM(column_shape, F32),
            pltpu.VMEM(band_shape, F32),
            pltpu.VMEM((2, 5, 2, 8, padded), F32),
            pltpu.VMEM((2, 4, 4, 8, padded), F32),
            pltpu.VMEM((2, 6, 2, 8, padded), F32),
            pltpu.VMEM(band_shape, F32),
            pltpu.VMEM((512, LANES), F32),
            pltpu.VMEM((128, 8, LANES), F32),
            pltpu.VMEM((2, 2, 8, MODES), F32),
            pltpu.SemaphoreType.DMA((14,)),
            pltpu.SemaphoreType.DMA((14,)),
            pltpu.SemaphoreType.DMA((10,)),
        ],
        compiler_params=pltpu.CompilerParams(
            collective_id=0, has_side_effects=True, vmem_limit_bytes=56 * 1024 * 1024
        ),
        cost_estimate=pl.CostEstimate(
            flops=10**9, bytes_accessed=8 * 10**6, transcendentals=0
        ),
    )(cutoffs, column_cost, *fields, jnp.asarray(forward), jnp.asarray(backward))


def fits_kernel(mesh):
    return mesh.shape["lev"] == 2 and mesh.shape["lat"] > 1


def solution(mesh):
    placed = (
        P(None, "lev", "lat", None),
        P(None, "lev", "lat", None),
        P("lev", "lat", None),
        P("lev", "lat", None),
        P("lev", "lat", None),
        P("lat"),
        P(),
        P(),
        P(None, "lat", "lev"),
        P("lat", "lev"),
    )
    return jax.shard_map(
        one_kernel if fits_kernel(mesh) else local,
        mesh=mesh,
        in_specs=placed,
        out_specs=(P(None, "lev", "lat", None), P(None, "lev", "lat", None)),
        check_vma=False,
    )
```

```python
import functools
import math

import jax
import jax.numpy as jnp
import ml_dtypes
import numpy as np
from jax import lax
from jax.experimental import pallas as pl
from jax.experimental.pallas import tpu as pltpu
from jax.sharding import PartitionSpec as P

SUBS = 8


HIGHEST = lax.Precision.HIGHEST


def with_halo(cells, sides, width):
    for axis, dim in sides:
        count = lax.axis_size(axis)
        ends = count - 1
        head = lax.slice_in_dim(cells, 0, width, axis=dim)
        tail = lax.slice_in_dim(cells, cells.shape[dim] - width, cells.shape[dim], axis=dim)
        cells = jnp.concatenate(
            [
                lax.ppermute(tail, axis, [(i, (i + 1) % count) for i in range(ends)]),
                cells,
                lax.ppermute(head, axis, [((i + 1) % count, i) for i in range(ends)]),
            ],
            axis=dim,
        )
    return cells


def fourier_basis(length):
    sample = jnp.arange(length, dtype=jnp.int32)[:, None]
    column = jnp.arange(length, dtype=jnp.int32)[None, :]
    nyquist = length // 2
    wavenumber = jnp.where(column <= nyquist, column, column - nyquist)
    angles = (sample * wavenumber % length).astype(jnp.float32) * (2.0 * math.pi / length)
    weights = jnp.where(
        (wavenumber == 0) | (wavenumber == nyquist),
        1.0 / math.sqrt(length),
        math.sqrt(2.0 / length),
    )
    basis_table = jnp.where(column <= nyquist, jnp.cos(angles), jnp.sin(angles)) * weights
    return (basis_table, wavenumber[0])


def upper_modes(length):
    basis_table, wavenumber = fourier_basis(length)
    nyquist = length // 2
    lowest = 3 * length // 8 + 1
    cosine_part = basis_table[:, lowest : nyquist + 1]
    sine_part = basis_table[:, nyquist + lowest :]
    modes = jnp.concatenate([cosine_part, sine_part], axis=1)
    mode_numbers = jnp.concatenate(
        [wavenumber[lowest : nyquist + 1], wavenumber[nyquist + lowest :]]
    )
    return (modes, mode_numbers)


def polar_filter(grid_field, drop_mask, modes):
    coeffs = jnp.einsum("fkix,xc->fkic", grid_field, modes, precision=HIGHEST)
    return grid_field - jnp.einsum("fkic,xc->fkix", coeffs * drop_mask, modes, precision=HIGHEST)


def tangent_advect(grid_field, zonal_wind, merid_wind, vert_wind):
    padded = with_halo(grid_field, (("lev", 1), ("lat", 2)), 1)
    lat_diff = padded[:, 1:-1, 2:] - padded[:, 1:-1, :-2]
    lev_diff = padded[:, 2:, 1:-1] - padded[:, :-2, 1:-1]
    lon_diff = jnp.roll(grid_field, -1, axis=3) - jnp.roll(grid_field, 1, axis=3)
    return grid_field - 0.5 * (zonal_wind * lon_diff + merid_wind * lat_diff + vert_wind * lev_diff)


def adjoint_advect(grid_field, zonal_wind, merid_wind, vert_wind):
    merid_padded = with_halo(merid_wind * grid_field, (("lat", 2),), 1)
    vert_padded = with_halo(vert_wind * grid_field, (("lev", 1),), 1)
    zonal_part = zonal_wind * grid_field
    lon_term = jnp.roll(zonal_part, -1, axis=3) - jnp.roll(zonal_part, 1, axis=3)
    lat_term = merid_padded[:, :, 2:] - merid_padded[:, :, :-2]
    lev_term = vert_padded[:, 2:] - vert_padded[:, :-2]
    return grid_field + 0.5 * (lon_term + lat_term + lev_term)


def to_columns(stacked):
    return lax.all_to_all(stacked, "lev", split_axis=4, concat_axis=2, tiled=True)


def to_bands(stacked):
    return lax.all_to_all(stacked, "lev", split_axis=2, concat_axis=4, tiled=True)


def column_physics(operators, state_rows, fields_all, row_counts):
    unit_rows = jnp.ones_like(state_rows)
    before = jnp.stack([state_rows, unit_rows])[:, None]
    after = jnp.stack([unit_rows, state_rows])[:, None]
    counts_view = row_counts[None, None, None, :, None]
    current = fields_all
    for sub_step in range(SUBS):
        advanced = after * jnp.einsum(
            "sfkl,sflix->sfkix", operators, before * current, precision=HIGHEST
        )
        current = jnp.where(sub_step < counts_view, advanced, current)
    return current


def local(
    tl_pert,
    adj_in,
    zonal_wind,
    merid_wind,
    vert_wind,
    cutoffs,
    remap,
    phys_op,
    phys_state,
    column_cost,
):
    modes, mode_numbers = upper_modes(tl_pert.shape[3])
    drop_mask = (mode_numbers[None, :] > cutoffs[:, None]).astype(jnp.float32)
    operators = jnp.stack([phys_op, jnp.swapaxes(phys_op, 1, 2)])
    row_counts = column_cost[:, 0]
    adj_columns = to_columns(adj_in[None])
    tl_advected = tangent_advect(tl_pert, zonal_wind, merid_wind, vert_wind)
    tl_filtered = polar_filter(tl_advected, drop_mask, modes)
    tl_columns = to_columns(tl_filtered[None])
    tl_remapped = jnp.einsum("fkl,sflix->sfkix", remap, tl_columns, precision=HIGHEST)
    fields_all = jnp.concatenate([tl_remapped, adj_columns], axis=0)
    physics_done = column_physics(operators, phys_state, fields_all, row_counts)
    tl_finished = physics_done[0:1]
    adj_remapped = jnp.einsum("flk,sflix->sfkix", remap, physics_done[1:2], precision=HIGHEST)
    tl_result = to_bands(tl_finished)[0]
    adj_bands = to_bands(adj_remapped)[0]
    adj_filtered = polar_filter(adj_bands, drop_mask, modes)
    adj_result = adjoint_advect(adj_filtered, zonal_wind, merid_wind, vert_wind)
    return (tl_result, adj_result)

BF16 = jnp.bfloat16
F32 = jnp.float32
LANES = 128
MODES = 256
MESH_IDS = pl.DeviceIdType.MESH


def mode_tables(length, half, padded):
    nyquist = length // 2
    lowest = 3 * length // 8 + 1
    forward = np.zeros((2, 2, padded, MODES), ml_dtypes.bfloat16)
    backward = np.zeros((2, 2, MODES, padded), ml_dtypes.bfloat16)
    layout = []
    sample = np.arange(half)
    for parity in range(2):
        cosines = [m for m in range(lowest, nyquist + 1) if m % 2 == parity]
        sines = [m for m in range(lowest, nyquist) if m % 2 == parity]
        waves = np.array(cosines + sines)
        count = len(waves)
        angles = 2.0 * np.pi / length * ((sample[:, None] * waves[None, :]) % length)
        is_cosine = (np.arange(count) < len(cosines))[None, :]
        weight = np.where(waves == nyquist, length**-0.5, (2.0 / length) ** 0.5)
        table = np.where(is_cosine, np.cos(angles), np.sin(angles)) * weight[None, :]
        high = table.astype(ml_dtypes.bfloat16)
        low = (table - high.astype(np.float64)).astype(ml_dtypes.bfloat16)
        for part, piece in enumerate((high, low)):
            forward[parity, part, :half, :count] = piece
            backward[parity, part, :count, :half] = piece.T
        layout.append((cosines[0], len(cosines), count))
    return forward, backward, tuple(layout)


def split_dot(rows, high, low):
    count = rows.shape[0]
    top = rows.astype(BF16)
    rest = (rows - top.astype(F32)).astype(BF16)
    both = jnp.dot(jnp.concatenate([top, rest], axis=0), high, preferred_element_type=F32)
    cross = jnp.dot(top, low, preferred_element_type=F32)
    return both[:count] + both[count:] + cross


def filter_in_place(buf, levels, mask, fwd, bwd):
    width = buf.shape[-1]
    rows = levels * 16
    first = buf[0].reshape(rows, width)
    second = buf[1].reshape(rows, width)
    dropped = []
    for parity, folded in enumerate((first + second, first - second)):
        coeffs = split_dot(folded, fwd[parity, 0], fwd[parity, 1])
        kept = coeffs.reshape(levels, 2, 8, MODES) * mask[parity][None]
        dropped.append(split_dot(kept.reshape(rows, MODES), bwd[parity, 0], bwd[parity, 1]))
    even, odd = dropped
    buf[0] = (first - (even + odd)).reshape(levels, 2, 8, width)
    buf[1] = (second - (even - odd)).reshape(levels, 2, 8, width)


def step_kernel(
    half,
    bands,
    layout,
    cutoffs,
    cost,
    tl_hbm,
    adj_hbm,
    zonal_hbm,
    merid_hbm,
    vert_hbm,
    state_hbm,
    op_hbm,
    remap_hbm,
    fwd_hbm,
    bwd_hbm,
    tl_done,
    adj_done,
    tl,
    adj,
    zonal_raw,
    merid_raw,
    vert_raw,
    state_raw,
    op_raw,
    remap_raw,
    fwd,
    bwd,
    winds,
    qx,
    wext,
    ah,
    acols,
    tbuf,
    tcols,
    aback,
    tback,
    tband,
    out_tl,
    out_adj,
    abuf,
    mx,
    vx,
    part,
    spread,
    mats,
    mask,
    send_sem,
    recv_sem,
    load_sem,
):
    width = qx.shape[-1]
    tiles = width // LANES
    lev = lax.axis_index("lev")
    lat = lax.axis_index("lat")
    other = 1 - lev
    has_up = lat < bands - 1
    has_down = lat > 0

    loads = [
        pltpu.make_async_copy(src, dst, load_sem.at[number])
        for number, (src, dst) in enumerate(
            [
                (tl_hbm, tl),
                (adj_hbm, adj),
                (zonal_hbm, zonal_raw),
                (merid_hbm, merid_raw),
                (vert_hbm, vert_raw),
                (state_hbm, state_raw),
                (op_hbm, op_raw),
                (remap_hbm, remap_raw),
                (fwd_hbm, fwd),
                (bwd_hbm, bwd),
            ]
        )
    ]
    for load in loads:
        load.start()

    barrier = pltpu.get_barrier_semaphore()
    pl.semaphore_signal(barrier, inc=1, device_id=(other, lat), device_id_type=MESH_IDS)

    @pl.when(has_up)
    def _():
        pl.semaphore_signal(barrier, inc=1, device_id=(lev, lat + 1), device_id_type=MESH_IDS)

    @pl.when(has_down)
    def _():
        pl.semaphore_signal(barrier, inc=1, device_id=(lev, lat - 1), device_id_type=MESH_IDS)

    inner = jnp.logical_and(has_up, has_down)

    @pl.when(inner)
    def _():
        pl.semaphore_wait(barrier, 3)

    @pl.when(jnp.logical_not(inner))
    def _():
        pl.semaphore_wait(barrier, 2)

    def remote(number, src, dst, to_lev, to_lat):
        return pltpu.make_async_remote_copy(
            src_ref=src,
            dst_ref=dst,
            send_sem=send_sem.at[number],
            recv_sem=recv_sem.at[number],
            device_id=(to_lev, to_lat),
            device_id_type=MESH_IDS,
        )

    edge = 3 * other
    lat_up = remote(1, qx.at[:, pl.ds(1, 4), 2], qx.at[:, pl.ds(1, 4), 0], lev, lat + 1)
    lat_down = remote(2, qx.at[:, pl.ds(1, 4), 1], qx.at[:, pl.ds(1, 4), 3], lev, lat - 1)
    wind_halo = remote(3, winds.at[edge, pl.ds(8, 8)], wext, other, lat)
    mine = pl.ds(4 * lev, 4)
    theirs = pl.ds(4 * other, 4)
    adj_out_cols = [
        remote(4 + i, ah.at[other, :, i], acols.at[mine, i], other, lat) for i in range(2)
    ]
    adj_in_bands = [
        remote(6 + i, aback.at[pl.ds(3 * other, 5), i], abuf.at[lev, :, i], other, lat)
        for i in range(2)
    ]
    tl_out_cols = [
        remote(8 + i, tbuf.at[other, :, i], tcols.at[lev, :, i], other, lat) for i in range(2)
    ]
    tl_in_bands = [
        remote(10 + i, tback.at[theirs, i], tband.at[lev, :, i], other, lat) for i in range(2)
    ]
    merid_up = remote(12, mx.at[:, :, 2], mx.at[:, :, 0], lev, lat + 1)
    merid_down = remote(13, mx.at[:, :, 1], mx.at[:, :, 3], lev, lat - 1)

    def halves(row):
        first = jnp.concatenate([row[:, :half], jnp.zeros((8, width - half), F32)], axis=1)
        second = jnp.concatenate([row[:, half:], jnp.zeros((8, width - half), F32)], axis=1)
        return first, second

    loads[1].wait()
    for i in range(2):
        for k in range(4):
            for h, block in enumerate(halves(adj[:, k, i, :])):
                ah[h, k, i] = block
        adj_out_cols[i].start()

    loads[0].wait()

    def to_halves(i):
        for k in range(4):
            for h, block in enumerate(halves(tl[:, k, i, :])):
                qx[h, 1 + k, 1 + i] = block

    to_halves(1)

    @pl.when(has_up)
    def _():
        lat_up.start()

    to_halves(0)

    @pl.when(has_down)
    def _():
        lat_down.start()

    for load in loads[2:6]:
        load.wait()
    blank = jnp.zeros((4, width - half), F32)
    for k in range(4):
        for first, raw in ((0, zonal_raw), (4, merid_raw), (8, vert_raw)):
            for h in range(2):
                for i in range(2):
                    winds[k, first + 2 * h + i : first + 2 * h + i + 1, :half] = raw[
                        k, i : i + 1, h * half : (h + 1) * half
                    ]
            winds[k, first : first + 4, half:] = blank
        for l in range(2):
            winds[k, 12 + 2 * l : 14 + 2 * l, :half] = state_raw[2 * k + l]
        winds[k, 12:16, half:] = blank
    wind_halo.start()
    acols[mine] = ah[lev]

    zeros = jnp.zeros((8, width), F32)

    @pl.when(jnp.logical_not(has_down))
    def _():
        for h in range(2):
            for k in range(4):
                qx[h, 1 + k, 0] = zeros
                mx[h, k, 0] = zeros

    @pl.when(jnp.logical_not(has_up))
    def _():
        for h in range(2):
            for k in range(4):
                qx[h, 1 + k, 3] = zeros
                mx[h, k, 3] = zeros

    for h in range(2):
        for i in range(2):
            qx[h, 0, 1 + i] = zeros
            qx[h, 5, 1 + i] = zeros
            vx[h, 5 * lev, i] = zeros

    for load in loads[6:8]:
        load.wait()
    for base, raw in ((0, op_raw), (64, remap_raw)):
        for f in range(8):
            table = raw[f]
            for l in range(8):
                at = (f * 8 + l) * 8
                spread[at : at + 8, :] = jnp.broadcast_to(table[:, l : l + 1], (8, LANES))
        for k in range(8):
            for l in range(8):
                mats[base + 8 * k + l] = spread[pl.ds(8 * l + k, 8, stride=64), :]

    column = lax.broadcasted_iota(jnp.int32, (8, MODES), 1)
    for parity, (first, cosines, count) in enumerate(layout):
        number = first + 2 * jnp.where(column < cosines, column, column - cosines)
        for i in range(2):
            drop = jnp.logical_and(number > cutoffs[i], column < count)
            mask[parity, i] = jnp.where(drop, 1.0, 0.0).astype(F32)

    lane = lax.broadcasted_iota(jnp.int32, (8, width), 1)

    def wind(ref_row):
        return jnp.broadcast_to(ref_row, (8, width))

    def lon_diff(z, across):
        after = jnp.where(lane == half - 1, across[:, 0:1], pltpu.roll(z, width - 1, 1))
        before = jnp.where(lane == 0, across[:, half - 1 : half], pltpu.roll(z, 1, 1))
        return after - before

    def product(base, transposed, vec):
        result = []
        for k in range(8):
            terms = [
                mats[base + (8 * l + k if transposed else 8 * k + l)] * vec[l] for l in range(8)
            ]
            while len(terms) > 1:
                terms = [a + b for a, b in zip(terms[::2], terms[1::2])]
            result.append(terms[0])
        return result

    def physics(src, dst, i, adjoint):
        steps = jnp.full((8, LANES), cost[i], jnp.int32)

        def tile(t, carry):
            cols = pl.ds(pl.multiple_of(t * LANES, LANES), LANES)
            state = [
                jnp.broadcast_to(
                    winds[l // 2, 12 + 2 * (l % 2) + i : 13 + 2 * (l % 2) + i, cols], (8, LANES)
                )
                for l in range(8)
            ]
            if adjoint:
                vec = [src[l, i, :, cols] for l in range(8)]
            else:
                low = [src[0, l, i, :, cols] for l in range(5)]
                high = [src[1, l, i, :, cols] for l in range(5)]
                both = [low[3] + high[0], low[4] + high[1]]
                vec = product(64, False, low[:3] + both + high[2:])

            def sub_step(s, vec):
                if adjoint:
                    new = [d * v for d, v in zip(state, product(0, True, vec))]
                else:
                    new = product(0, False, [d * v for d, v in zip(state, vec)])
                active = s < steps
                return [jnp.where(active, n, v) for n, v in zip(new, vec)]

            vec = lax.fori_loop(0, SUBS, sub_step, vec)
            if adjoint:
                vec = product(64, True, vec)
            for k in range(8):
                dst[k, i, :, cols] = vec[k]
            return carry

        lax.fori_loop(0, tiles, tile, 0)

    for i in range(2):
        adj_out_cols[i].wait_recv()
        physics(acols, aback, i, True)
        adj_in_bands[i].start()
    abuf[lev] = aback[pl.ds(3 * lev, 5)]

    @pl.when(has_down)
    def _():
        lat_up.wait_recv()

    @pl.when(has_up)
    def _():
        lat_down.wait_recv()

    def advect(k, carry):
        for h in range(2):
            for i in range(2):
                row = 2 * h + i
                q = qx[h, k + 1, i + 1]
                zonal = wind(winds[k, row : row + 1]) * lon_diff(q, qx[1 - h, k + 1, i + 1])
                merid = wind(winds[k, 4 + row : 5 + row]) * (
                    qx[h, k + 1, i + 2] - qx[h, k + 1, i]
                )
                vert = wind(winds[k, 8 + row : 9 + row]) * (
                    qx[h, k + 2, i + 1] - qx[h, k, i + 1]
                )
                tbuf[h, k + lev, i] = q - 0.5 * (zonal + merid + vert)
        return carry

    lax.fori_loop(0, 4, advect, 0)

    wind_halo.wait_recv()
    sign = 0.5 - lev.astype(F32)
    for h in range(2):
        for i in range(2):
            row = 2 * h + i
            tbuf[h, 4 * other, i] = sign * (wind(wext[row : row + 1]) * qx[h, 1 + edge, 1 + i])
    for load in loads[8:]:
        load.wait()
    filter_in_place(tbuf, 5, mask, fwd, bwd)
    for copy in tl_out_cols:
        copy.start()
    tcols[lev] = tbuf[lev]

    for i in range(2):
        adj_in_bands[i].wait_recv()
    filter_in_place(abuf, 5, mask, fwd, bwd)

    def merid_parts(k, carry):
        for h in range(2):
            for i in range(2):
                row = 2 * h + i
                mx[h, k, i + 1] = wind(winds[k, 4 + row : 5 + row]) * abuf[h, k + lev, i]
        return carry

    lax.fori_loop(0, 4, merid_parts, 0)

    @pl.when(has_up)
    def _():
        merid_up.start()

    @pl.when(has_down)
    def _():
        merid_down.start()

    def vert_parts(k, carry):
        for h in range(2):
            for i in range(2):
                row = 2 * h + i
                vx[h, k + 1, i] = wind(winds[k, 8 + row : 9 + row]) * abuf[h, k + lev, i]
        return carry

    lax.fori_loop(0, 4, vert_parts, 0)
    for h in range(2):
        for i in range(2):
            row = 2 * h + i
            vx[h, 5 * other, i] = wind(wext[row : row + 1]) * abuf[h, 4 * other, i]

    def zonal_parts(k, carry):
        for i in range(2):
            p = [abuf[h, k + lev, i] for h in range(2)]
            z = [wind(winds[k, 2 * h + i : 2 * h + i + 1]) * p[h] for h in range(2)]
            for h in range(2):
                total = lon_diff(z[h], z[1 - h]) + (vx[h, k + 2, i] - vx[h, k, i])
                part[h, k, i] = p[h] + 0.5 * total
        return carry

    lax.fori_loop(0, 4, zonal_parts, 0)

    for i in range(2):
        tl_out_cols[i].wait_recv()
        physics(tcols, tback, i, False)
        tl_in_bands[i].start()
    tband[lev] = tback[mine]

    def join(pair):
        return jnp.concatenate([block[:, :half] for block in pair], axis=1)

    @pl.when(has_down)
    def _():
        merid_up.wait_recv()

    @pl.when(has_up)
    def _():
        merid_down.wait_recv()

    for k in range(4):
        for i in range(2):
            out_adj[:, k, i, :] = join(
                [
                    part[h, k, i] + 0.5 * (mx[h, k, i + 2] - mx[h, k, i])
                    for h in range(2)
                ]
            )
    adj_store = pltpu.make_async_copy(out_adj, adj_done, load_sem.at[10])
    adj_store.start()

    for copy in tl_in_bands:
        copy.wait_recv()
    for k in range(4):
        for i in range(2):
            out_tl[:, k, i, :] = join([tband[h, k, i] for h in range(2)])
    tl_store = pltpu.make_async_copy(out_tl, tl_done, load_sem.at[11])
    tl_store.start()

    for copy in [wind_halo] + adj_out_cols + adj_in_bands + tl_out_cols + tl_in_bands:
        copy.wait_send()

    @pl.when(has_up)
    def _():
        lat_up.wait_send()
        merid_up.wait_send()

    @pl.when(has_down)
    def _():
        lat_down.wait_send()
        merid_down.wait_send()

    adj_store.wait()
    tl_store.wait()


def hand_over(first, second, first_out, second_out, sems):
    copies = [
        pltpu.make_async_copy(first, first_out, sems.at[0]),
        pltpu.make_async_copy(second, second_out, sems.at[1]),
    ]
    for copy in copies:
        copy.start()
    for copy in copies:
        copy.wait()


def one_kernel(
    tl_pert,
    adj_in,
    zonal_wind,
    merid_wind,
    vert_wind,
    cutoffs,
    remap,
    phys_op,
    phys_state,
    column_cost,
):
    length = tl_pert.shape[3]
    half = length // 2
    padded = -(-half // LANES) * LANES
    bands = lax.axis_size("lat")
    forward, backward, layout = mode_tables(length, half, padded)
    smem = pl.BlockSpec(memory_space=pltpu.SMEM)
    hbm = pl.BlockSpec(memory_space=pl.ANY)
    band_shape = (2, 4, 2, 8, padded)
    edged_shape = (2, 5, 2, 8, padded)
    column_shape = (8, 2, 8, padded)
    fields = [tl_pert, adj_in, zonal_wind, merid_wind, vert_wind, phys_state, phys_op, remap]
    done = pl.pallas_call(
        functools.partial(step_kernel, half, bands, layout),
        out_shape=[jax.ShapeDtypeStruct(tl_pert.shape, F32)] * 2,
        in_specs=[smem] * 2 + [hbm] * 10,
        out_specs=[hbm] * 2,
        scratch_shapes=[pltpu.VMEM(field.shape, F32) for field in fields]
        + [
            pltpu.VMEM(forward.shape, BF16),
            pltpu.VMEM(backward.shape, BF16),
            pltpu.VMEM((4, 16, padded), F32),
            pltpu.VMEM((2, 6, 4, 8, padded), F32),
            pltpu.VMEM((8, padded), F32),
            pltpu.VMEM(band_shape, F32),
            pltpu.VMEM(column_shape, F32),
            pltpu.VMEM(edged_shape, F32),
            pltpu.VMEM(edged_shape, F32),
            pltpu.VMEM(column_shape, F32),
            pltpu.VMEM(column_shape, F32),
            pltpu.VMEM(band_shape, F32),
            pltpu.VMEM(tl_pert.shape, F32),
            pltpu.VMEM(tl_pert.shape, F32),
            pltpu.VMEM(edged_shape, F32),
            pltpu.VMEM((2, 4, 4, 8, padded), F32),
            pltpu.VMEM((2, 6, 2, 8, padded), F32),
            pltpu.VMEM(band_shape, F32),
            pltpu.VMEM((512, LANES), F32),
            pltpu.VMEM((128, 8, LANES), F32),
            pltpu.VMEM((2, 2, 8, MODES), F32),
            pltpu.SemaphoreType.DMA((14,)),
            pltpu.SemaphoreType.DMA((14,)),
            pltpu.SemaphoreType.DMA((12,)),
        ],
        compiler_params=pltpu.CompilerParams(
            collective_id=0, has_side_effects=True, vmem_limit_bytes=56 * 1024 * 1024
        ),
        cost_estimate=pl.CostEstimate(
            flops=10**9, bytes_accessed=8 * 10**6, transcendentals=0
        ),
    )(cutoffs, column_cost[:, 0], *fields, jnp.asarray(forward), jnp.asarray(backward))
    return pl.pallas_call(
        hand_over,
        out_shape=[jax.ShapeDtypeStruct(tl_pert.shape, F32)] * 2,
        in_specs=[hbm] * 2,
        out_specs=[hbm] * 2,
        scratch_shapes=[pltpu.SemaphoreType.DMA((2,))],
        compiler_params=pltpu.CompilerParams(vmem_limit_bytes=56 * 1024 * 1024),
    )(*done)


def fits_kernel(mesh):
    return mesh.shape["lev"] == 2 and mesh.shape["lat"] > 1


def solution(mesh):
    placed = (
        P(None, "lev", "lat", None),
        P(None, "lev", "lat", None),
        P("lev", "lat", None),
        P("lev", "lat", None),
        P("lev", "lat", None),
        P("lat"),
        P(),
        P(),
        P(None, "lat", "lev"),
        P("lat", "lev"),
    )
    return jax.shard_map(
        one_kernel if fits_kernel(mesh) else local,
        mesh=mesh,
        in_specs=placed,
        out_specs=(P(None, "lev", "lat", None), P(None, "lev", "lat", None)),
        check_vma=False,
    )
```

```python
import functools
import math

import jax
import jax.numpy as jnp
import ml_dtypes
import numpy as np
from jax import lax
from jax.experimental import pallas as pl
from jax.experimental.pallas import tpu as pltpu
from jax.sharding import PartitionSpec as P

SUBS = 8


HIGHEST = lax.Precision.HIGHEST


def with_halo(cells, sides, width):
    for axis, dim in sides:
        count = lax.axis_size(axis)
        ends = count - 1
        head = lax.slice_in_dim(cells, 0, width, axis=dim)
        tail = lax.slice_in_dim(cells, cells.shape[dim] - width, cells.shape[dim], axis=dim)
        cells = jnp.concatenate(
            [
                lax.ppermute(tail, axis, [(i, (i + 1) % count) for i in range(ends)]),
                cells,
                lax.ppermute(head, axis, [((i + 1) % count, i) for i in range(ends)]),
            ],
            axis=dim,
        )
    return cells


def fourier_basis(length):
    sample = jnp.arange(length, dtype=jnp.int32)[:, None]
    column = jnp.arange(length, dtype=jnp.int32)[None, :]
    nyquist = length // 2
    wavenumber = jnp.where(column <= nyquist, column, column - nyquist)
    angles = (sample * wavenumber % length).astype(jnp.float32) * (2.0 * math.pi / length)
    weights = jnp.where(
        (wavenumber == 0) | (wavenumber == nyquist),
        1.0 / math.sqrt(length),
        math.sqrt(2.0 / length),
    )
    basis_table = jnp.where(column <= nyquist, jnp.cos(angles), jnp.sin(angles)) * weights
    return (basis_table, wavenumber[0])


def upper_modes(length):
    basis_table, wavenumber = fourier_basis(length)
    nyquist = length // 2
    lowest = 3 * length // 8 + 1
    cosine_part = basis_table[:, lowest : nyquist + 1]
    sine_part = basis_table[:, nyquist + lowest :]
    modes = jnp.concatenate([cosine_part, sine_part], axis=1)
    mode_numbers = jnp.concatenate(
        [wavenumber[lowest : nyquist + 1], wavenumber[nyquist + lowest :]]
    )
    return (modes, mode_numbers)


def polar_filter(grid_field, drop_mask, modes):
    coeffs = jnp.einsum("fkix,xc->fkic", grid_field, modes, precision=HIGHEST)
    return grid_field - jnp.einsum("fkic,xc->fkix", coeffs * drop_mask, modes, precision=HIGHEST)


def tangent_advect(grid_field, zonal_wind, merid_wind, vert_wind):
    padded = with_halo(grid_field, (("lev", 1), ("lat", 2)), 1)
    lat_diff = padded[:, 1:-1, 2:] - padded[:, 1:-1, :-2]
    lev_diff = padded[:, 2:, 1:-1] - padded[:, :-2, 1:-1]
    lon_diff = jnp.roll(grid_field, -1, axis=3) - jnp.roll(grid_field, 1, axis=3)
    return grid_field - 0.5 * (zonal_wind * lon_diff + merid_wind * lat_diff + vert_wind * lev_diff)


def adjoint_advect(grid_field, zonal_wind, merid_wind, vert_wind):
    merid_padded = with_halo(merid_wind * grid_field, (("lat", 2),), 1)
    vert_padded = with_halo(vert_wind * grid_field, (("lev", 1),), 1)
    zonal_part = zonal_wind * grid_field
    lon_term = jnp.roll(zonal_part, -1, axis=3) - jnp.roll(zonal_part, 1, axis=3)
    lat_term = merid_padded[:, :, 2:] - merid_padded[:, :, :-2]
    lev_term = vert_padded[:, 2:] - vert_padded[:, :-2]
    return grid_field + 0.5 * (lon_term + lat_term + lev_term)


def to_columns(stacked):
    return lax.all_to_all(stacked, "lev", split_axis=4, concat_axis=2, tiled=True)


def to_bands(stacked):
    return lax.all_to_all(stacked, "lev", split_axis=2, concat_axis=4, tiled=True)


def column_physics(operators, state_rows, fields_all, row_counts):
    unit_rows = jnp.ones_like(state_rows)
    before = jnp.stack([state_rows, unit_rows])[:, None]
    after = jnp.stack([unit_rows, state_rows])[:, None]
    counts_view = row_counts[None, None, None, :, None]
    current = fields_all
    for sub_step in range(SUBS):
        advanced = after * jnp.einsum(
            "sfkl,sflix->sfkix", operators, before * current, precision=HIGHEST
        )
        current = jnp.where(sub_step < counts_view, advanced, current)
    return current


def local(
    tl_pert,
    adj_in,
    zonal_wind,
    merid_wind,
    vert_wind,
    cutoffs,
    remap,
    phys_op,
    phys_state,
    column_cost,
):
    modes, mode_numbers = upper_modes(tl_pert.shape[3])
    drop_mask = (mode_numbers[None, :] > cutoffs[:, None]).astype(jnp.float32)
    operators = jnp.stack([phys_op, jnp.swapaxes(phys_op, 1, 2)])
    row_counts = column_cost[:, 0]
    adj_columns = to_columns(adj_in[None])
    tl_advected = tangent_advect(tl_pert, zonal_wind, merid_wind, vert_wind)
    tl_filtered = polar_filter(tl_advected, drop_mask, modes)
    tl_columns = to_columns(tl_filtered[None])
    tl_remapped = jnp.einsum("fkl,sflix->sfkix", remap, tl_columns, precision=HIGHEST)
    fields_all = jnp.concatenate([tl_remapped, adj_columns], axis=0)
    physics_done = column_physics(operators, phys_state, fields_all, row_counts)
    tl_finished = physics_done[0:1]
    adj_remapped = jnp.einsum("flk,sflix->sfkix", remap, physics_done[1:2], precision=HIGHEST)
    tl_result = to_bands(tl_finished)[0]
    adj_bands = to_bands(adj_remapped)[0]
    adj_filtered = polar_filter(adj_bands, drop_mask, modes)
    adj_result = adjoint_advect(adj_filtered, zonal_wind, merid_wind, vert_wind)
    return (tl_result, adj_result)

BF16 = jnp.bfloat16
F32 = jnp.float32
LANES = 128
MODES = 256
MESH_IDS = pl.DeviceIdType.MESH


def mode_tables(length, half, padded):
    nyquist = length // 2
    lowest = 3 * length // 8 + 1
    forward = np.zeros((2, 2, padded, MODES), ml_dtypes.bfloat16)
    backward = np.zeros((2, 2, MODES, padded), ml_dtypes.bfloat16)
    layout = []
    sample = np.arange(half)
    for parity in range(2):
        cosines = [m for m in range(lowest, nyquist + 1) if m % 2 == parity]
        sines = [m for m in range(lowest, nyquist) if m % 2 == parity]
        waves = np.array(cosines + sines)
        count = len(waves)
        angles = 2.0 * np.pi / length * ((sample[:, None] * waves[None, :]) % length)
        is_cosine = (np.arange(count) < len(cosines))[None, :]
        weight = np.where(waves == nyquist, length**-0.5, (2.0 / length) ** 0.5)
        table = np.where(is_cosine, np.cos(angles), np.sin(angles)) * weight[None, :]
        high = table.astype(ml_dtypes.bfloat16)
        low = (table - high.astype(np.float64)).astype(ml_dtypes.bfloat16)
        for part, piece in enumerate((high, low)):
            forward[parity, part, :half, :count] = piece
            backward[parity, part, :count, :half] = piece.T
        layout.append((cosines[0], len(cosines), count))
    return forward, backward, tuple(layout)


def split_dot(rows, high, low):
    count = rows.shape[0]
    top = rows.astype(BF16)
    rest = (rows - top.astype(F32)).astype(BF16)
    both = jnp.dot(jnp.concatenate([top, rest], axis=0), high, preferred_element_type=F32)
    cross = jnp.dot(top, low, preferred_element_type=F32)
    return both[:count] + both[count:] + cross


def filter_in_place(buf, levels, mask, fwd, bwd):
    width = buf.shape[-1]
    rows = levels * 16
    first = buf[0].reshape(rows, width)
    second = buf[1].reshape(rows, width)
    dropped = []
    for parity, folded in enumerate((first + second, first - second)):
        coeffs = split_dot(folded, fwd[parity, 0], fwd[parity, 1])
        kept = coeffs.reshape(levels, 2, 8, MODES) * mask[parity][None]
        dropped.append(split_dot(kept.reshape(rows, MODES), bwd[parity, 0], bwd[parity, 1]))
    even, odd = dropped
    buf[0] = (first - (even + odd)).reshape(levels, 2, 8, width)
    buf[1] = (second - (even - odd)).reshape(levels, 2, 8, width)


def step_kernel(
    half,
    bands,
    layout,
    cutoffs,
    cost,
    tl_hbm,
    adj_hbm,
    zonal_hbm,
    merid_hbm,
    vert_hbm,
    state_hbm,
    op_hbm,
    remap_hbm,
    fwd_hbm,
    bwd_hbm,
    tl_done,
    adj_done,
    tl,
    adj,
    zonal_raw,
    merid_raw,
    vert_raw,
    state_raw,
    op_raw,
    remap_raw,
    fwd,
    bwd,
    winds,
    qx,
    wext,
    ah,
    acols,
    tbuf,
    tcols,
    aback,
    tback,
    tband,
    out_tl,
    out_adj,
    abuf,
    mx,
    vx,
    part,
    spread,
    mats,
    mask,
    send_sem,
    recv_sem,
    load_sem,
):
    width = qx.shape[-1]
    tiles = width // LANES
    lev = lax.axis_index("lev")
    lat = lax.axis_index("lat")
    other = 1 - lev
    has_up = lat < bands - 1
    has_down = lat > 0

    loads = [
        pltpu.make_async_copy(src, dst, load_sem.at[number])
        for number, (src, dst) in enumerate(
            [
                (tl_hbm, tl),
                (adj_hbm, adj),
                (zonal_hbm, zonal_raw),
                (merid_hbm, merid_raw),
                (vert_hbm, vert_raw),
                (state_hbm, state_raw),
                (op_hbm, op_raw),
                (remap_hbm, remap_raw),
                (fwd_hbm, fwd),
                (bwd_hbm, bwd),
            ]
        )
    ]
    for load in loads:
        load.start()

    barrier = pltpu.get_barrier_semaphore()
    pl.semaphore_signal(barrier, inc=1, device_id=(other, lat), device_id_type=MESH_IDS)

    @pl.when(has_up)
    def _():
        pl.semaphore_signal(barrier, inc=1, device_id=(lev, lat + 1), device_id_type=MESH_IDS)

    @pl.when(has_down)
    def _():
        pl.semaphore_signal(barrier, inc=1, device_id=(lev, lat - 1), device_id_type=MESH_IDS)

    inner = jnp.logical_and(has_up, has_down)

    @pl.when(inner)
    def _():
        pl.semaphore_wait(barrier, 3)

    @pl.when(jnp.logical_not(inner))
    def _():
        pl.semaphore_wait(barrier, 2)

    def remote(number, src, dst, to_lev, to_lat):
        return pltpu.make_async_remote_copy(
            src_ref=src,
            dst_ref=dst,
            send_sem=send_sem.at[number],
            recv_sem=recv_sem.at[number],
            device_id=(to_lev, to_lat),
            device_id_type=MESH_IDS,
        )

    edge = 3 * other
    lat_up = remote(1, qx.at[:, pl.ds(1, 4), 2], qx.at[:, pl.ds(1, 4), 0], lev, lat + 1)
    lat_down = remote(2, qx.at[:, pl.ds(1, 4), 1], qx.at[:, pl.ds(1, 4), 3], lev, lat - 1)
    wind_halo = remote(3, winds.at[edge, pl.ds(8, 8)], wext, other, lat)
    mine = pl.ds(4 * lev, 4)
    theirs = pl.ds(4 * other, 4)
    adj_out_cols = [
        remote(4 + i, ah.at[other, :, i], acols.at[mine, i], other, lat) for i in range(2)
    ]
    adj_in_bands = [
        remote(6 + i, aback.at[pl.ds(3 * other, 5), i], abuf.at[lev, :, i], other, lat)
        for i in range(2)
    ]
    tl_out_cols = [
        remote(8 + i, tbuf.at[other, :, i], tcols.at[lev, :, i], other, lat) for i in range(2)
    ]
    tl_in_bands = [
        remote(10 + i, tback.at[theirs, i], tband.at[lev, :, i], other, lat) for i in range(2)
    ]
    merid_up = remote(12, mx.at[:, :, 2], mx.at[:, :, 0], lev, lat + 1)
    merid_down = remote(13, mx.at[:, :, 1], mx.at[:, :, 3], lev, lat - 1)

    def halves(row):
        first = jnp.concatenate([row[:, :half], jnp.zeros((8, width - half), F32)], axis=1)
        second = jnp.concatenate([row[:, half:], jnp.zeros((8, width - half), F32)], axis=1)
        return first, second

    loads[1].wait()
    for i in range(2):
        for k in range(4):
            for h, block in enumerate(halves(adj[:, k, i, :])):
                ah[h, k, i] = block
        adj_out_cols[i].start()

    loads[0].wait()

    def to_halves(i):
        for k in range(4):
            for h, block in enumerate(halves(tl[:, k, i, :])):
                qx[h, 1 + k, 1 + i] = block

    to_halves(1)

    @pl.when(has_up)
    def _():
        lat_up.start()

    to_halves(0)

    @pl.when(has_down)
    def _():
        lat_down.start()

    for load in loads[2:6]:
        load.wait()
    blank = jnp.zeros((4, width - half), F32)
    for k in range(4):
        for first, raw in ((0, zonal_raw), (4, merid_raw), (8, vert_raw)):
            for h in range(2):
                for i in range(2):
                    winds[k, first + 2 * h + i : first + 2 * h + i + 1, :half] = raw[
                        k, i : i + 1, h * half : (h + 1) * half
                    ]
            winds[k, first : first + 4, half:] = blank
        for l in range(2):
            winds[k, 12 + 2 * l : 14 + 2 * l, :half] = state_raw[2 * k + l]
        winds[k, 12:16, half:] = blank
    wind_halo.start()
    acols[mine] = ah[lev]

    zeros = jnp.zeros((8, width), F32)

    @pl.when(jnp.logical_not(has_down))
    def _():
        for h in range(2):
            for k in range(4):
                qx[h, 1 + k, 0] = zeros
                mx[h, k, 0] = zeros

    @pl.when(jnp.logical_not(has_up))
    def _():
        for h in range(2):
            for k in range(4):
                qx[h, 1 + k, 3] = zeros
                mx[h, k, 3] = zeros

    for h in range(2):
        for i in range(2):
            qx[h, 0, 1 + i] = zeros
            qx[h, 5, 1 + i] = zeros
            vx[h, 5 * lev, i] = zeros

    for load in loads[6:8]:
        load.wait()
    for base, raw in ((0, op_raw), (64, remap_raw)):
        for f in range(8):
            table = raw[f]
            for l in range(8):
                at = (f * 8 + l) * 8
                spread[at : at + 8, :] = jnp.broadcast_to(table[:, l : l + 1], (8, LANES))
        for k in range(8):
            for l in range(8):
                mats[base + 8 * k + l] = spread[pl.ds(8 * l + k, 8, stride=64), :]

    column = lax.broadcasted_iota(jnp.int32, (8, MODES), 1)
    for parity, (first, cosines, count) in enumerate(layout):
        number = first + 2 * jnp.where(column < cosines, column, column - cosines)
        for i in range(2):
            drop = jnp.logical_and(number > cutoffs[i], column < count)
            mask[parity, i] = jnp.where(drop, 1.0, 0.0).astype(F32)

    lane = lax.broadcasted_iota(jnp.int32, (8, width), 1)

    def wind(ref_row):
        return jnp.broadcast_to(ref_row, (8, width))

    def lon_diff(z, across):
        after = jnp.where(lane == half - 1, across[:, 0:1], pltpu.roll(z, width - 1, 1))
        before = jnp.where(lane == 0, across[:, half - 1 : half], pltpu.roll(z, 1, 1))
        return after - before

    def product(base, transposed, vec):
        result = []
        for k in range(8):
            terms = [
                mats[base + (8 * l + k if transposed else 8 * k + l)] * vec[l] for l in range(8)
            ]
            while len(terms) > 1:
                terms = [a + b for a, b in zip(terms[::2], terms[1::2])]
            result.append(terms[0])
        return result

    def physics(src, dst, i, adjoint):
        steps = jnp.full((8, LANES), cost[i], jnp.int32)

        def tile(t, carry):
            cols = pl.ds(pl.multiple_of(t * LANES, LANES), LANES)
            state = [
                jnp.broadcast_to(
                    winds[l // 2, 12 + 2 * (l % 2) + i : 13 + 2 * (l % 2) + i, cols], (8, LANES)
                )
                for l in range(8)
            ]
            if adjoint:
                vec = [src[l, i, :, cols] for l in range(8)]
            else:
                low = [src[0, l, i, :, cols] for l in range(5)]
                high = [src[1, l, i, :, cols] for l in range(5)]
                both = [low[3] + high[0], low[4] + high[1]]
                vec = product(64, False, low[:3] + both + high[2:])

            def sub_step(s, vec):
                if adjoint:
                    new = [d * v for d, v in zip(state, product(0, True, vec))]
                else:
                    new = product(0, False, [d * v for d, v in zip(state, vec)])
                active = s < steps
                return [jnp.where(active, n, v) for n, v in zip(new, vec)]

            vec = lax.fori_loop(0, SUBS, sub_step, vec)
            if adjoint:
                vec = product(64, True, vec)
            for k in range(8):
                dst[k, i, :, cols] = vec[k]
            return carry

        lax.fori_loop(0, tiles, tile, 0)

    for i in range(2):
        adj_out_cols[i].wait_recv()
        physics(acols, aback, i, True)
        adj_in_bands[i].start()
    abuf[lev] = aback[pl.ds(3 * lev, 5)]

    @pl.when(has_down)
    def _():
        lat_up.wait_recv()

    @pl.when(has_up)
    def _():
        lat_down.wait_recv()

    def advect(k, carry):
        for h in range(2):
            for i in range(2):
                row = 2 * h + i
                q = qx[h, k + 1, i + 1]
                zonal = wind(winds[k, row : row + 1]) * lon_diff(q, qx[1 - h, k + 1, i + 1])
                merid = wind(winds[k, 4 + row : 5 + row]) * (
                    qx[h, k + 1, i + 2] - qx[h, k + 1, i]
                )
                vert = wind(winds[k, 8 + row : 9 + row]) * (
                    qx[h, k + 2, i + 1] - qx[h, k, i + 1]
                )
                tbuf[h, k + lev, i] = q - 0.5 * (zonal + merid + vert)
        return carry

    lax.fori_loop(0, 4, advect, 0)

    wind_halo.wait_recv()
    sign = 0.5 - lev.astype(F32)
    for h in range(2):
        for i in range(2):
            row = 2 * h + i
            tbuf[h, 4 * other, i] = sign * (wind(wext[row : row + 1]) * qx[h, 1 + edge, 1 + i])
    for load in loads[8:]:
        load.wait()
    filter_in_place(tbuf, 5, mask, fwd, bwd)
    for copy in tl_out_cols:
        copy.start()
    tcols[lev] = tbuf[lev]

    for i in range(2):
        adj_in_bands[i].wait_recv()
    filter_in_place(abuf, 5, mask, fwd, bwd)

    def merid_parts(k, carry):
        for h in range(2):
            for i in range(2):
                row = 2 * h + i
                mx[h, k, i + 1] = wind(winds[k, 4 + row : 5 + row]) * abuf[h, k + lev, i]
        return carry

    lax.fori_loop(0, 4, merid_parts, 0)

    @pl.when(has_up)
    def _():
        merid_up.start()

    @pl.when(has_down)
    def _():
        merid_down.start()

    def vert_parts(k, carry):
        for h in range(2):
            for i in range(2):
                row = 2 * h + i
                vx[h, k + 1, i] = wind(winds[k, 8 + row : 9 + row]) * abuf[h, k + lev, i]
        return carry

    lax.fori_loop(0, 4, vert_parts, 0)
    for h in range(2):
        for i in range(2):
            row = 2 * h + i
            vx[h, 5 * other, i] = wind(wext[row : row + 1]) * abuf[h, 4 * other, i]

    def zonal_parts(k, carry):
        for i in range(2):
            p = [abuf[h, k + lev, i] for h in range(2)]
            z = [wind(winds[k, 2 * h + i : 2 * h + i + 1]) * p[h] for h in range(2)]
            for h in range(2):
                total = lon_diff(z[h], z[1 - h]) + (vx[h, k + 2, i] - vx[h, k, i])
                part[h, k, i] = p[h] + 0.5 * total
        return carry

    lax.fori_loop(0, 4, zonal_parts, 0)

    for i in range(2):
        tl_out_cols[i].wait_recv()
        physics(tcols, tback, i, False)
        tl_in_bands[i].start()
    tband[lev] = tback[mine]

    def join(pair):
        return jnp.concatenate([block[:, :half] for block in pair], axis=1)

    @pl.when(has_down)
    def _():
        merid_up.wait_recv()

    @pl.when(has_up)
    def _():
        merid_down.wait_recv()

    for k in range(4):
        for i in range(2):
            out_adj[:, k, i, :] = join(
                [
                    part[h, k, i] + 0.5 * (mx[h, k, i + 2] - mx[h, k, i])
                    for h in range(2)
                ]
            )
    adj_store = pltpu.make_async_copy(out_adj, adj_done, load_sem.at[10])
    adj_store.start()

    for copy in tl_in_bands:
        copy.wait_recv()
    for k in range(4):
        for i in range(2):
            out_tl[:, k, i, :] = join([tband[h, k, i] for h in range(2)])
    tl_store = pltpu.make_async_copy(out_tl, tl_done, load_sem.at[11])
    tl_store.start()

    for copy in [wind_halo] + adj_out_cols + adj_in_bands + tl_out_cols + tl_in_bands:
        copy.wait_send()

    @pl.when(has_up)
    def _():
        lat_up.wait_send()
        merid_up.wait_send()

    @pl.when(has_down)
    def _():
        lat_down.wait_send()
        merid_down.wait_send()

    adj_store.wait()
    tl_store.wait()


def hand_over(first, second, first_out, second_out, first_held, second_held, sems):
    pairs = ((first, first_held, first_out), (second, second_held, second_out))
    inward = [pltpu.make_async_copy(src, held, sems.at[n]) for n, (src, held, _) in enumerate(pairs)]
    outward = [
        pltpu.make_async_copy(held, dst, sems.at[2 + n]) for n, (_, held, dst) in enumerate(pairs)
    ]
    for copy in inward:
        copy.start()
    for arrived, copy in zip(inward, outward):
        arrived.wait()
        copy.start()
    for copy in outward:
        copy.wait()


def one_kernel(
    tl_pert,
    adj_in,
    zonal_wind,
    merid_wind,
    vert_wind,
    cutoffs,
    remap,
    phys_op,
    phys_state,
    column_cost,
):
    length = tl_pert.shape[3]
    half = length // 2
    padded = -(-half // LANES) * LANES
    bands = lax.axis_size("lat")
    forward, backward, layout = mode_tables(length, half, padded)
    smem = pl.BlockSpec(memory_space=pltpu.SMEM)
    hbm = pl.BlockSpec(memory_space=pl.ANY)
    band_shape = (2, 4, 2, 8, padded)
    edged_shape = (2, 5, 2, 8, padded)
    column_shape = (8, 2, 8, padded)
    fields = [tl_pert, adj_in, zonal_wind, merid_wind, vert_wind, phys_state, phys_op, remap]
    done = pl.pallas_call(
        functools.partial(step_kernel, half, bands, layout),
        out_shape=[jax.ShapeDtypeStruct(tl_pert.shape, F32)] * 2,
        in_specs=[smem] * 2 + [hbm] * 10,
        out_specs=[hbm] * 2,
        scratch_shapes=[pltpu.VMEM(field.shape, F32) for field in fields]
        + [
            pltpu.VMEM(forward.shape, BF16),
            pltpu.VMEM(backward.shape, BF16),
            pltpu.VMEM((4, 16, padded), F32),
            pltpu.VMEM((2, 6, 4, 8, padded), F32),
            pltpu.VMEM((8, padded), F32),
            pltpu.VMEM(band_shape, F32),
            pltpu.VMEM(column_shape, F32),
            pltpu.VMEM(edged_shape, F32),
            pltpu.VMEM(edged_shape, F32),
            pltpu.VMEM(column_shape, F32),
            pltpu.VMEM(column_shape, F32),
            pltpu.VMEM(band_shape, F32),
            pltpu.VMEM(tl_pert.shape, F32),
            pltpu.VMEM(tl_pert.shape, F32),
            pltpu.VMEM(edged_shape, F32),
            pltpu.VMEM((2, 4, 4, 8, padded), F32),
            pltpu.VMEM((2, 6, 2, 8, padded), F32),
            pltpu.VMEM(band_shape, F32),
            pltpu.VMEM((512, LANES), F32),
            pltpu.VMEM((128, 8, LANES), F32),
            pltpu.VMEM((2, 2, 8, MODES), F32),
            pltpu.SemaphoreType.DMA((14,)),
            pltpu.SemaphoreType.DMA((14,)),
            pltpu.SemaphoreType.DMA((12,)),
        ],
        compiler_params=pltpu.CompilerParams(
            collective_id=0, has_side_effects=True, vmem_limit_bytes=56 * 1024 * 1024
        ),
        cost_estimate=pl.CostEstimate(
            flops=10**9, bytes_accessed=8 * 10**6, transcendentals=0
        ),
    )(cutoffs, column_cost[:, 0], *fields, jnp.asarray(forward), jnp.asarray(backward))
    return pl.pallas_call(
        hand_over,
        out_shape=[jax.ShapeDtypeStruct(tl_pert.shape, F32)] * 2,
        in_specs=[hbm] * 2,
        out_specs=[hbm] * 2,
        scratch_shapes=[pltpu.VMEM(tl_pert.shape, F32)] * 2 + [pltpu.SemaphoreType.DMA((4,))],
        compiler_params=pltpu.CompilerParams(vmem_limit_bytes=56 * 1024 * 1024),
    )(*done)


def fits_kernel(mesh):
    return mesh.shape["lev"] == 2 and mesh.shape["lat"] > 1


def solution(mesh):
    placed = (
        P(None, "lev", "lat", None),
        P(None, "lev", "lat", None),
        P("lev", "lat", None),
        P("lev", "lat", None),
        P("lev", "lat", None),
        P("lat"),
        P(),
        P(),
        P(None, "lat", "lev"),
        P("lat", "lev"),
    )
    return jax.shard_map(
        one_kernel if fits_kernel(mesh) else local,
        mesh=mesh,
        in_specs=placed,
        out_specs=(P(None, "lev", "lat", None), P(None, "lev", "lat", None)),
        check_vma=False,
    )
```

```python
import functools
import math

import jax
import jax.numpy as jnp
import ml_dtypes
import numpy as np
from jax import lax
from jax.experimental import pallas as pl
from jax.experimental.pallas import tpu as pltpu
from jax.sharding import PartitionSpec as P

SUBS = 8


HIGHEST = lax.Precision.HIGHEST


def with_halo(cells, sides, width):
    for axis, dim in sides:
        count = lax.axis_size(axis)
        ends = count - 1
        head = lax.slice_in_dim(cells, 0, width, axis=dim)
        tail = lax.slice_in_dim(cells, cells.shape[dim] - width, cells.shape[dim], axis=dim)
        cells = jnp.concatenate(
            [
                lax.ppermute(tail, axis, [(i, (i + 1) % count) for i in range(ends)]),
                cells,
                lax.ppermute(head, axis, [((i + 1) % count, i) for i in range(ends)]),
            ],
            axis=dim,
        )
    return cells


def fourier_basis(length):
    sample = jnp.arange(length, dtype=jnp.int32)[:, None]
    column = jnp.arange(length, dtype=jnp.int32)[None, :]
    nyquist = length // 2
    wavenumber = jnp.where(column <= nyquist, column, column - nyquist)
    angles = (sample * wavenumber % length).astype(jnp.float32) * (2.0 * math.pi / length)
    weights = jnp.where(
        (wavenumber == 0) | (wavenumber == nyquist),
        1.0 / math.sqrt(length),
        math.sqrt(2.0 / length),
    )
    basis_table = jnp.where(column <= nyquist, jnp.cos(angles), jnp.sin(angles)) * weights
    return (basis_table, wavenumber[0])


def upper_modes(length):
    basis_table, wavenumber = fourier_basis(length)
    nyquist = length // 2
    lowest = 3 * length // 8 + 1
    cosine_part = basis_table[:, lowest : nyquist + 1]
    sine_part = basis_table[:, nyquist + lowest :]
    modes = jnp.concatenate([cosine_part, sine_part], axis=1)
    mode_numbers = jnp.concatenate(
        [wavenumber[lowest : nyquist + 1], wavenumber[nyquist + lowest :]]
    )
    return (modes, mode_numbers)


def polar_filter(grid_field, drop_mask, modes):
    coeffs = jnp.einsum("fkix,xc->fkic", grid_field, modes, precision=HIGHEST)
    return grid_field - jnp.einsum("fkic,xc->fkix", coeffs * drop_mask, modes, precision=HIGHEST)


def tangent_advect(grid_field, zonal_wind, merid_wind, vert_wind):
    padded = with_halo(grid_field, (("lev", 1), ("lat", 2)), 1)
    lat_diff = padded[:, 1:-1, 2:] - padded[:, 1:-1, :-2]
    lev_diff = padded[:, 2:, 1:-1] - padded[:, :-2, 1:-1]
    lon_diff = jnp.roll(grid_field, -1, axis=3) - jnp.roll(grid_field, 1, axis=3)
    return grid_field - 0.5 * (zonal_wind * lon_diff + merid_wind * lat_diff + vert_wind * lev_diff)


def adjoint_advect(grid_field, zonal_wind, merid_wind, vert_wind):
    merid_padded = with_halo(merid_wind * grid_field, (("lat", 2),), 1)
    vert_padded = with_halo(vert_wind * grid_field, (("lev", 1),), 1)
    zonal_part = zonal_wind * grid_field
    lon_term = jnp.roll(zonal_part, -1, axis=3) - jnp.roll(zonal_part, 1, axis=3)
    lat_term = merid_padded[:, :, 2:] - merid_padded[:, :, :-2]
    lev_term = vert_padded[:, 2:] - vert_padded[:, :-2]
    return grid_field + 0.5 * (lon_term + lat_term + lev_term)


def to_columns(stacked):
    return lax.all_to_all(stacked, "lev", split_axis=4, concat_axis=2, tiled=True)


def to_bands(stacked):
    return lax.all_to_all(stacked, "lev", split_axis=2, concat_axis=4, tiled=True)


def column_physics(operators, state_rows, fields_all, row_counts):
    unit_rows = jnp.ones_like(state_rows)
    before = jnp.stack([state_rows, unit_rows])[:, None]
    after = jnp.stack([unit_rows, state_rows])[:, None]
    counts_view = row_counts[None, None, None, :, None]
    current = fields_all
    for sub_step in range(SUBS):
        advanced = after * jnp.einsum(
            "sfkl,sflix->sfkix", operators, before * current, precision=HIGHEST
        )
        current = jnp.where(sub_step < counts_view, advanced, current)
    return current


def local(
    tl_pert,
    adj_in,
    zonal_wind,
    merid_wind,
    vert_wind,
    cutoffs,
    remap,
    phys_op,
    phys_state,
    column_cost,
):
    modes, mode_numbers = upper_modes(tl_pert.shape[3])
    drop_mask = (mode_numbers[None, :] > cutoffs[:, None]).astype(jnp.float32)
    operators = jnp.stack([phys_op, jnp.swapaxes(phys_op, 1, 2)])
    row_counts = column_cost[:, 0]
    adj_columns = to_columns(adj_in[None])
    tl_advected = tangent_advect(tl_pert, zonal_wind, merid_wind, vert_wind)
    tl_filtered = polar_filter(tl_advected, drop_mask, modes)
    tl_columns = to_columns(tl_filtered[None])
    tl_remapped = jnp.einsum("fkl,sflix->sfkix", remap, tl_columns, precision=HIGHEST)
    fields_all = jnp.concatenate([tl_remapped, adj_columns], axis=0)
    physics_done = column_physics(operators, phys_state, fields_all, row_counts)
    tl_finished = physics_done[0:1]
    adj_remapped = jnp.einsum("flk,sflix->sfkix", remap, physics_done[1:2], precision=HIGHEST)
    tl_result = to_bands(tl_finished)[0]
    adj_bands = to_bands(adj_remapped)[0]
    adj_filtered = polar_filter(adj_bands, drop_mask, modes)
    adj_result = adjoint_advect(adj_filtered, zonal_wind, merid_wind, vert_wind)
    return (tl_result, adj_result)

BF16 = jnp.bfloat16
F32 = jnp.float32
LANES = 128
MODES = 256
MESH_IDS = pl.DeviceIdType.MESH


def mode_tables(length, half, padded):
    nyquist = length // 2
    lowest = 3 * length // 8 + 1
    forward = np.zeros((2, 2, padded, MODES), ml_dtypes.bfloat16)
    backward = np.zeros((2, 2, MODES, padded), ml_dtypes.bfloat16)
    layout = []
    sample = np.arange(half)
    for parity in range(2):
        cosines = [m for m in range(lowest, nyquist + 1) if m % 2 == parity]
        sines = [m for m in range(lowest, nyquist) if m % 2 == parity]
        waves = np.array(cosines + sines)
        count = len(waves)
        angles = 2.0 * np.pi / length * ((sample[:, None] * waves[None, :]) % length)
        is_cosine = (np.arange(count) < len(cosines))[None, :]
        weight = np.where(waves == nyquist, length**-0.5, (2.0 / length) ** 0.5)
        table = np.where(is_cosine, np.cos(angles), np.sin(angles)) * weight[None, :]
        high = table.astype(ml_dtypes.bfloat16)
        low = (table - high.astype(np.float64)).astype(ml_dtypes.bfloat16)
        for part, piece in enumerate((high, low)):
            forward[parity, part, :half, :count] = piece
            backward[parity, part, :count, :half] = piece.T
        layout.append((cosines[0], len(cosines), count))
    return forward, backward, tuple(layout)


def split_dot(rows, high, low):
    count = rows.shape[0]
    top = rows.astype(BF16)
    rest = (rows - top.astype(F32)).astype(BF16)
    both = jnp.dot(jnp.concatenate([top, rest], axis=0), high, preferred_element_type=F32)
    cross = jnp.dot(top, low, preferred_element_type=F32)
    return both[:count] + both[count:] + cross


def filter_in_place(buf, levels, mask, fwd, bwd):
    width = buf.shape[-1]
    rows = levels * 16
    first = buf[0].reshape(rows, width)
    second = buf[1].reshape(rows, width)
    dropped = []
    for parity, folded in enumerate((first + second, first - second)):
        coeffs = split_dot(folded, fwd[parity, 0], fwd[parity, 1])
        kept = coeffs.reshape(levels, 2, 8, MODES) * mask[parity][None]
        dropped.append(split_dot(kept.reshape(rows, MODES), bwd[parity, 0], bwd[parity, 1]))
    even, odd = dropped
    buf[0] = (first - (even + odd)).reshape(levels, 2, 8, width)
    buf[1] = (second - (even - odd)).reshape(levels, 2, 8, width)


def step_kernel(
    half,
    bands,
    layout,
    cutoffs,
    cost,
    tl_hbm,
    adj_hbm,
    zonal_hbm,
    merid_hbm,
    vert_hbm,
    state_hbm,
    op_hbm,
    remap_hbm,
    fwd_hbm,
    bwd_hbm,
    out_tl,
    out_adj,
    tl,
    adj,
    zonal_raw,
    merid_raw,
    vert_raw,
    state_raw,
    op_raw,
    remap_raw,
    fwd,
    bwd,
    winds,
    qx,
    wext,
    ah,
    acols,
    tbuf,
    tcols,
    aback,
    tback,
    tband,
    abuf,
    mx,
    vx,
    partial,
    spread,
    mats,
    mask,
    send_sem,
    recv_sem,
    load_sem,
):
    width = qx.shape[-1]
    tiles = width // LANES
    lev = lax.axis_index("lev")
    lat = lax.axis_index("lat")
    other = 1 - lev
    has_up = lat < bands - 1
    has_down = lat > 0

    loads = [
        pltpu.make_async_copy(src, dst, load_sem.at[number])
        for number, (src, dst) in enumerate(
            [
                (tl_hbm, tl),
                (adj_hbm, adj),
                (zonal_hbm, zonal_raw),
                (merid_hbm, merid_raw),
                (vert_hbm, vert_raw),
                (state_hbm, state_raw),
                (op_hbm, op_raw),
                (remap_hbm, remap_raw),
                (fwd_hbm, fwd),
                (bwd_hbm, bwd),
            ]
        )
    ]
    for number in (1, 0, 2, 3, 4, 5, 6, 7):
        loads[number].start()

    barrier = pltpu.get_barrier_semaphore()
    pl.semaphore_signal(barrier, inc=1, device_id=(other, lat), device_id_type=MESH_IDS)

    @pl.when(has_up)
    def _():
        pl.semaphore_signal(barrier, inc=1, device_id=(lev, lat + 1), device_id_type=MESH_IDS)

    @pl.when(has_down)
    def _():
        pl.semaphore_signal(barrier, inc=1, device_id=(lev, lat - 1), device_id_type=MESH_IDS)

    inner = jnp.logical_and(has_up, has_down)

    @pl.when(inner)
    def _():
        pl.semaphore_wait(barrier, 3)

    @pl.when(jnp.logical_not(inner))
    def _():
        pl.semaphore_wait(barrier, 2)

    def remote(number, src, dst, to_lev, to_lat):
        return pltpu.make_async_remote_copy(
            src_ref=src,
            dst_ref=dst,
            send_sem=send_sem.at[number],
            recv_sem=recv_sem.at[number],
            device_id=(to_lev, to_lat),
            device_id_type=MESH_IDS,
        )

    edge = 3 * other
    lat_up = remote(1, qx.at[:, pl.ds(1, 4), 2], qx.at[:, pl.ds(1, 4), 0], lev, lat + 1)
    lat_down = remote(2, qx.at[:, pl.ds(1, 4), 1], qx.at[:, pl.ds(1, 4), 3], lev, lat - 1)
    wind_halo = remote(3, winds.at[edge, pl.ds(8, 8)], wext, other, lat)
    mine = pl.ds(4 * lev, 4)
    theirs = pl.ds(4 * other, 4)
    adj_out_cols = [
        remote(14 + i, ah.at[other, :, i], acols.at[mine, i], other, lat) for i in range(2)
    ]
    pieces = [(i, pl.ds(part * width // 2, width // 2)) for i in range(2) for part in range(2)]
    adj_in_bands = [
        remote(
            4 + number,
            aback.at[pl.ds(3 * other, 5), i, :, cols],
            abuf.at[lev, :, i, :, cols],
            other,
            lat,
        )
        for number, (i, cols) in enumerate(pieces)
    ]
    tl_out_cols = [
        remote(8 + i, tbuf.at[other, :, i], tcols.at[lev, :, i], other, lat) for i in range(2)
    ]
    tl_in_bands = [
        remote(
            10 + number, tback.at[theirs, i, :, cols], tband.at[lev, :, i, :, cols], other, lat
        )
        for number, (i, cols) in enumerate(pieces)
    ]
    merid_up = remote(0, mx.at[:, :, 2], mx.at[:, :, 0], lev, lat + 1)
    merid_down = remote(16, mx.at[:, :, 1], mx.at[:, :, 3], lev, lat - 1)

    def halves(row):
        first = jnp.concatenate([row[:, :half], jnp.zeros((8, width - half), F32)], axis=1)
        second = jnp.concatenate([row[:, half:], jnp.zeros((8, width - half), F32)], axis=1)
        return first, second

    loads[1].wait()
    for i in range(2):
        for k in range(4):
            for h, block in enumerate(halves(adj[:, k, i, :])):
                ah[h, k, i] = block
        adj_out_cols[i].start()

    loads[0].wait()
    for load in loads[8:]:
        load.start()

    def to_halves(i):
        for k in range(4):
            for h, block in enumerate(halves(tl[:, k, i, :])):
                qx[h, 1 + k, 1 + i] = block

    to_halves(1)

    @pl.when(has_up)
    def _():
        lat_up.start()

    to_halves(0)

    @pl.when(has_down)
    def _():
        lat_down.start()

    for load in loads[2:6]:
        load.wait()
    blank = jnp.zeros((4, width - half), F32)
    for k in range(4):
        for first, raw in ((0, zonal_raw), (4, merid_raw), (8, vert_raw)):
            for h in range(2):
                for i in range(2):
                    winds[k, first + 2 * h + i : first + 2 * h + i + 1, :half] = raw[
                        k, i : i + 1, h * half : (h + 1) * half
                    ]
            winds[k, first : first + 4, half:] = blank
        for l in range(2):
            winds[k, 12 + 2 * l : 14 + 2 * l, :half] = state_raw[2 * k + l]
        winds[k, 12:16, half:] = blank
    wind_halo.start()
    acols[mine] = ah[lev]

    zeros = jnp.zeros((8, width), F32)

    @pl.when(jnp.logical_not(has_down))
    def _():
        for h in range(2):
            for k in range(4):
                qx[h, 1 + k, 0] = zeros
                mx[h, k, 0] = zeros

    @pl.when(jnp.logical_not(has_up))
    def _():
        for h in range(2):
            for k in range(4):
                qx[h, 1 + k, 3] = zeros
                mx[h, k, 3] = zeros

    for h in range(2):
        for i in range(2):
            qx[h, 0, 1 + i] = zeros
            qx[h, 5, 1 + i] = zeros
            vx[h, 5 * lev, i] = zeros

    for load in loads[6:8]:
        load.wait()
    for base, raw in ((0, op_raw), (64, remap_raw)):
        for f in range(8):
            table = raw[f]
            for l in range(8):
                at = (f * 8 + l) * 8
                spread[at : at + 8, :] = jnp.broadcast_to(table[:, l : l + 1], (8, LANES))
        for k in range(8):
            for l in range(8):
                mats[base + 8 * k + l] = spread[pl.ds(8 * l + k, 8, stride=64), :]

    column = lax.broadcasted_iota(jnp.int32, (8, MODES), 1)
    for parity, (first, cosines, count) in enumerate(layout):
        number = first + 2 * jnp.where(column < cosines, column, column - cosines)
        for i in range(2):
            drop = jnp.logical_and(number > cutoffs[i], column < count)
            mask[parity, i] = jnp.where(drop, 1.0, 0.0).astype(F32)

    lane = lax.broadcasted_iota(jnp.int32, (8, width), 1)

    def wind(ref_row):
        return jnp.broadcast_to(ref_row, (8, width))

    def lon_diff(z, across):
        after = jnp.where(lane == half - 1, across[:, 0:1], pltpu.roll(z, width - 1, 1))
        before = jnp.where(lane == 0, across[:, half - 1 : half], pltpu.roll(z, 1, 1))
        return after - before

    def product(base, transposed, vec):
        result = []
        for k in range(8):
            terms = [
                mats[base + (8 * l + k if transposed else 8 * k + l)] * vec[l] for l in range(8)
            ]
            while len(terms) > 1:
                terms = [a + b for a, b in zip(terms[::2], terms[1::2])]
            result.append(terms[0])
        return result

    def physics(src, dst, i, part, adjoint):
        steps = jnp.full((8, LANES), cost[i], jnp.int32)

        def tile(t, carry):
            cols = pl.ds(pl.multiple_of(t * LANES, LANES), LANES)
            state = [
                jnp.broadcast_to(
                    winds[l // 2, 12 + 2 * (l % 2) + i : 13 + 2 * (l % 2) + i, cols], (8, LANES)
                )
                for l in range(8)
            ]
            if adjoint:
                vec = [src[l, i, :, cols] for l in range(8)]
            else:
                low = [src[0, l, i, :, cols] for l in range(5)]
                high = [src[1, l, i, :, cols] for l in range(5)]
                both = [low[3] + high[0], low[4] + high[1]]
                vec = product(64, False, low[:3] + both + high[2:])

            def sub_step(s, vec):
                if adjoint:
                    new = [d * v for d, v in zip(state, product(0, True, vec))]
                else:
                    new = product(0, False, [d * v for d, v in zip(state, vec)])
                active = s < steps
                return [jnp.where(active, n, v) for n, v in zip(new, vec)]

            vec = lax.fori_loop(0, SUBS, sub_step, vec)
            if adjoint:
                vec = product(64, True, vec)
            for k in range(8):
                dst[k, i, :, cols] = vec[k]
            return carry

        lax.fori_loop(part * tiles // 2, (part + 1) * tiles // 2, tile, 0)

    for i in range(2):
        adj_out_cols[i].wait_recv()
        for part in range(2):
            physics(acols, aback, i, part, True)
            adj_in_bands[2 * i + part].start()
    abuf[lev] = aback[pl.ds(3 * lev, 5)]

    @pl.when(has_down)
    def _():
        lat_up.wait_recv()

    @pl.when(has_up)
    def _():
        lat_down.wait_recv()

    def advect(k, carry):
        for h in range(2):
            for i in range(2):
                row = 2 * h + i
                q = qx[h, k + 1, i + 1]
                zonal = wind(winds[k, row : row + 1]) * lon_diff(q, qx[1 - h, k + 1, i + 1])
                merid = wind(winds[k, 4 + row : 5 + row]) * (
                    qx[h, k + 1, i + 2] - qx[h, k + 1, i]
                )
                vert = wind(winds[k, 8 + row : 9 + row]) * (
                    qx[h, k + 2, i + 1] - qx[h, k, i + 1]
                )
                tbuf[h, k + lev, i] = q - 0.5 * (zonal + merid + vert)
        return carry

    lax.fori_loop(0, 4, advect, 0)

    wind_halo.wait_recv()
    sign = 0.5 - lev.astype(F32)
    for h in range(2):
        for i in range(2):
            row = 2 * h + i
            tbuf[h, 4 * other, i] = sign * (wind(wext[row : row + 1]) * qx[h, 1 + edge, 1 + i])
    for load in loads[8:]:
        load.wait()
    filter_in_place(tbuf, 5, mask, fwd, bwd)
    for copy in tl_out_cols:
        copy.start()
    tcols[lev] = tbuf[lev]

    for copy in adj_in_bands:
        copy.wait_recv()
    filter_in_place(abuf, 5, mask, fwd, bwd)

    def merid_parts(k, carry):
        for h in range(2):
            for i in range(2):
                row = 2 * h + i
                mx[h, k, i + 1] = wind(winds[k, 4 + row : 5 + row]) * abuf[h, k + lev, i]
        return carry

    lax.fori_loop(0, 4, merid_parts, 0)

    @pl.when(has_up)
    def _():
        merid_up.start()

    @pl.when(has_down)
    def _():
        merid_down.start()

    def vert_parts(k, carry):
        for h in range(2):
            for i in range(2):
                row = 2 * h + i
                vx[h, k + 1, i] = wind(winds[k, 8 + row : 9 + row]) * abuf[h, k + lev, i]
        return carry

    lax.fori_loop(0, 4, vert_parts, 0)
    for h in range(2):
        for i in range(2):
            row = 2 * h + i
            vx[h, 5 * other, i] = wind(wext[row : row + 1]) * abuf[h, 4 * other, i]

    def zonal_parts(k, carry):
        for i in range(2):
            p = [abuf[h, k + lev, i] for h in range(2)]
            z = [wind(winds[k, 2 * h + i : 2 * h + i + 1]) * p[h] for h in range(2)]
            for h in range(2):
                total = lon_diff(z[h], z[1 - h]) + (vx[h, k + 2, i] - vx[h, k, i])
                partial[h, k, i] = p[h] + 0.5 * total
        return carry

    lax.fori_loop(0, 4, zonal_parts, 0)

    for i in range(2):
        tl_out_cols[i].wait_recv()
        for part in range(2):
            physics(tcols, tback, i, part, False)
            tl_in_bands[2 * i + part].start()
    tband[lev] = tback[mine]

    def join(pair):
        return jnp.concatenate([block[:, :half] for block in pair], axis=1)

    @pl.when(has_down)
    def _():
        merid_up.wait_recv()

    @pl.when(has_up)
    def _():
        merid_down.wait_recv()

    for k in range(4):
        for i in range(2):
            out_adj[:, k, i, :] = join(
                [
                    partial[h, k, i] + 0.5 * (mx[h, k, i + 2] - mx[h, k, i])
                    for h in range(2)
                ]
            )

    for i in range(2):
        for copy in tl_in_bands[2 * i : 2 * i + 2]:
            copy.wait_recv()
        for k in range(4):
            out_tl[:, k, i, :] = join([tband[h, k, i] for h in range(2)])

    for copy in [wind_halo] + adj_out_cols + adj_in_bands + tl_out_cols + tl_in_bands:
        copy.wait_send()

    @pl.when(has_up)
    def _():
        lat_up.wait_send()
        merid_up.wait_send()

    @pl.when(has_down)
    def _():
        lat_down.wait_send()
        merid_down.wait_send()


def hand_over(first, second, first_out, second_out, sems):
    copies = [
        pltpu.make_async_copy(first, first_out, sems.at[0]),
        pltpu.make_async_copy(second, second_out, sems.at[1]),
    ]
    for copy in copies:
        copy.start()
    for copy in copies:
        copy.wait()


def one_kernel(
    tl_pert,
    adj_in,
    zonal_wind,
    merid_wind,
    vert_wind,
    cutoffs,
    remap,
    phys_op,
    phys_state,
    column_cost,
):
    length = tl_pert.shape[3]
    half = length // 2
    padded = -(-half // LANES) * LANES
    bands = lax.axis_size("lat")
    forward, backward, layout = mode_tables(length, half, padded)
    vmem = pl.BlockSpec(memory_space=pltpu.VMEM)
    smem = pl.BlockSpec(memory_space=pltpu.SMEM)
    hbm = pl.BlockSpec(memory_space=pl.ANY)
    band_shape = (2, 4, 2, 8, padded)
    edged_shape = (2, 5, 2, 8, padded)
    column_shape = (8, 2, 8, padded)
    fields = [tl_pert, adj_in, zonal_wind, merid_wind, vert_wind, phys_state, phys_op, remap]
    done = pl.pallas_call(
        functools.partial(step_kernel, half, bands, layout),
        out_shape=[pltpu.VMEM(tl_pert.shape, F32)] * 2,
        in_specs=[smem] * 2 + [hbm] * 10,
        out_specs=[vmem] * 2,
        scratch_shapes=[pltpu.VMEM(field.shape, F32) for field in fields]
        + [
            pltpu.VMEM(forward.shape, BF16),
            pltpu.VMEM(backward.shape, BF16),
            pltpu.VMEM((4, 16, padded), F32),
            pltpu.VMEM((2, 6, 4, 8, padded), F32),
            pltpu.VMEM((8, padded), F32),
            pltpu.VMEM(band_shape, F32),
            pltpu.VMEM(column_shape, F32),
            pltpu.VMEM(edged_shape, F32),
            pltpu.VMEM(edged_shape, F32),
            pltpu.VMEM(column_shape, F32),
            pltpu.VMEM(column_shape, F32),
            pltpu.VMEM(band_shape, F32),
            pltpu.VMEM(edged_shape, F32),
            pltpu.VMEM((2, 4, 4, 8, padded), F32),
            pltpu.VMEM((2, 6, 2, 8, padded), F32),
            pltpu.VMEM(band_shape, F32),
            pltpu.VMEM((512, LANES), F32),
            pltpu.VMEM((128, 8, LANES), F32),
            pltpu.VMEM((2, 2, 8, MODES), F32),
            pltpu.SemaphoreType.DMA((17,)),
            pltpu.SemaphoreType.DMA((17,)),
            pltpu.SemaphoreType.DMA((10,)),
        ],
        compiler_params=pltpu.CompilerParams(
            collective_id=0, has_side_effects=True, vmem_limit_bytes=56 * 1024 * 1024
        ),
        cost_estimate=pl.CostEstimate(
            flops=10**9, bytes_accessed=8 * 10**6, transcendentals=0
        ),
    )(cutoffs, column_cost[:, 0], *fields, jnp.asarray(forward), jnp.asarray(backward))
    return pl.pallas_call(
        hand_over,
        out_shape=[jax.ShapeDtypeStruct(tl_pert.shape, F32)] * 2,
        in_specs=[vmem] * 2,
        out_specs=[hbm] * 2,
        scratch_shapes=[pltpu.SemaphoreType.DMA((2,))],
    )(*done)


def fits_kernel(mesh):
    return mesh.shape["lev"] == 2 and mesh.shape["lat"] > 1


def solution(mesh):
    placed = (
        P(None, "lev", "lat", None),
        P(None, "lev", "lat", None),
        P("lev", "lat", None),
        P("lev", "lat", None),
        P("lev", "lat", None),
        P("lat"),
        P(),
        P(),
        P(None, "lat", "lev"),
        P("lat", "lev"),
    )
    return jax.shard_map(
        one_kernel if fits_kernel(mesh) else local,
        mesh=mesh,
        in_specs=placed,
        out_specs=(P(None, "lev", "lat", None), P(None, "lev", "lat", None)),
        check_vma=False,
    )
```

```python
import functools
import math

import jax
import jax.numpy as jnp
import ml_dtypes
import numpy as np
from jax import lax
from jax.experimental import pallas as pl
from jax.experimental.pallas import tpu as pltpu
from jax.sharding import PartitionSpec as P

SUBS = 8


HIGHEST = lax.Precision.HIGHEST


def with_halo(cells, sides, width):
    for axis, dim in sides:
        count = lax.axis_size(axis)
        ends = count - 1
        head = lax.slice_in_dim(cells, 0, width, axis=dim)
        tail = lax.slice_in_dim(cells, cells.shape[dim] - width, cells.shape[dim], axis=dim)
        cells = jnp.concatenate(
            [
                lax.ppermute(tail, axis, [(i, (i + 1) % count) for i in range(ends)]),
                cells,
                lax.ppermute(head, axis, [((i + 1) % count, i) for i in range(ends)]),
            ],
            axis=dim,
        )
    return cells


def fourier_basis(length):
    sample = jnp.arange(length, dtype=jnp.int32)[:, None]
    column = jnp.arange(length, dtype=jnp.int32)[None, :]
    nyquist = length // 2
    wavenumber = jnp.where(column <= nyquist, column, column - nyquist)
    angles = (sample * wavenumber % length).astype(jnp.float32) * (2.0 * math.pi / length)
    weights = jnp.where(
        (wavenumber == 0) | (wavenumber == nyquist),
        1.0 / math.sqrt(length),
        math.sqrt(2.0 / length),
    )
    basis_table = jnp.where(column <= nyquist, jnp.cos(angles), jnp.sin(angles)) * weights
    return (basis_table, wavenumber[0])


def upper_modes(length):
    basis_table, wavenumber = fourier_basis(length)
    nyquist = length // 2
    lowest = 3 * length // 8 + 1
    cosine_part = basis_table[:, lowest : nyquist + 1]
    sine_part = basis_table[:, nyquist + lowest :]
    modes = jnp.concatenate([cosine_part, sine_part], axis=1)
    mode_numbers = jnp.concatenate(
        [wavenumber[lowest : nyquist + 1], wavenumber[nyquist + lowest :]]
    )
    return (modes, mode_numbers)


def polar_filter(grid_field, drop_mask, modes):
    coeffs = jnp.einsum("fkix,xc->fkic", grid_field, modes, precision=HIGHEST)
    return grid_field - jnp.einsum("fkic,xc->fkix", coeffs * drop_mask, modes, precision=HIGHEST)


def tangent_advect(grid_field, zonal_wind, merid_wind, vert_wind):
    padded = with_halo(grid_field, (("lev", 1), ("lat", 2)), 1)
    lat_diff = padded[:, 1:-1, 2:] - padded[:, 1:-1, :-2]
    lev_diff = padded[:, 2:, 1:-1] - padded[:, :-2, 1:-1]
    lon_diff = jnp.roll(grid_field, -1, axis=3) - jnp.roll(grid_field, 1, axis=3)
    return grid_field - 0.5 * (zonal_wind * lon_diff + merid_wind * lat_diff + vert_wind * lev_diff)


def adjoint_advect(grid_field, zonal_wind, merid_wind, vert_wind):
    merid_padded = with_halo(merid_wind * grid_field, (("lat", 2),), 1)
    vert_padded = with_halo(vert_wind * grid_field, (("lev", 1),), 1)
    zonal_part = zonal_wind * grid_field
    lon_term = jnp.roll(zonal_part, -1, axis=3) - jnp.roll(zonal_part, 1, axis=3)
    lat_term = merid_padded[:, :, 2:] - merid_padded[:, :, :-2]
    lev_term = vert_padded[:, 2:] - vert_padded[:, :-2]
    return grid_field + 0.5 * (lon_term + lat_term + lev_term)


def to_columns(stacked):
    return lax.all_to_all(stacked, "lev", split_axis=4, concat_axis=2, tiled=True)


def to_bands(stacked):
    return lax.all_to_all(stacked, "lev", split_axis=2, concat_axis=4, tiled=True)


def column_physics(operators, state_rows, fields_all, row_counts):
    unit_rows = jnp.ones_like(state_rows)
    before = jnp.stack([state_rows, unit_rows])[:, None]
    after = jnp.stack([unit_rows, state_rows])[:, None]
    counts_view = row_counts[None, None, None, :, None]
    current = fields_all
    for sub_step in range(SUBS):
        advanced = after * jnp.einsum(
            "sfkl,sflix->sfkix", operators, before * current, precision=HIGHEST
        )
        current = jnp.where(sub_step < counts_view, advanced, current)
    return current


def local(
    tl_pert,
    adj_in,
    zonal_wind,
    merid_wind,
    vert_wind,
    cutoffs,
    remap,
    phys_op,
    phys_state,
    column_cost,
):
    modes, mode_numbers = upper_modes(tl_pert.shape[3])
    drop_mask = (mode_numbers[None, :] > cutoffs[:, None]).astype(jnp.float32)
    operators = jnp.stack([phys_op, jnp.swapaxes(phys_op, 1, 2)])
    row_counts = column_cost[:, 0]
    adj_columns = to_columns(adj_in[None])
    tl_advected = tangent_advect(tl_pert, zonal_wind, merid_wind, vert_wind)
    tl_filtered = polar_filter(tl_advected, drop_mask, modes)
    tl_columns = to_columns(tl_filtered[None])
    tl_remapped = jnp.einsum("fkl,sflix->sfkix", remap, tl_columns, precision=HIGHEST)
    fields_all = jnp.concatenate([tl_remapped, adj_columns], axis=0)
    physics_done = column_physics(operators, phys_state, fields_all, row_counts)
    tl_finished = physics_done[0:1]
    adj_remapped = jnp.einsum("flk,sflix->sfkix", remap, physics_done[1:2], precision=HIGHEST)
    tl_result = to_bands(tl_finished)[0]
    adj_bands = to_bands(adj_remapped)[0]
    adj_filtered = polar_filter(adj_bands, drop_mask, modes)
    adj_result = adjoint_advect(adj_filtered, zonal_wind, merid_wind, vert_wind)
    return (tl_result, adj_result)

BF16 = jnp.bfloat16
F32 = jnp.float32
LANES = 128
MODES = 256
MESH_IDS = pl.DeviceIdType.MESH


def mode_tables(length, half, padded):
    nyquist = length // 2
    lowest = 3 * length // 8 + 1
    forward = np.zeros((2, 2, padded, MODES), ml_dtypes.bfloat16)
    backward = np.zeros((2, 2, MODES, padded), ml_dtypes.bfloat16)
    layout = []
    sample = np.arange(half)
    for parity in range(2):
        cosines = [m for m in range(lowest, nyquist + 1) if m % 2 == parity]
        sines = [m for m in range(lowest, nyquist) if m % 2 == parity]
        waves = np.array(cosines + sines)
        count = len(waves)
        angles = 2.0 * np.pi / length * ((sample[:, None] * waves[None, :]) % length)
        is_cosine = (np.arange(count) < len(cosines))[None, :]
        weight = np.where(waves == nyquist, length**-0.5, (2.0 / length) ** 0.5)
        table = np.where(is_cosine, np.cos(angles), np.sin(angles)) * weight[None, :]
        high = table.astype(ml_dtypes.bfloat16)
        low = (table - high.astype(np.float64)).astype(ml_dtypes.bfloat16)
        for part, piece in enumerate((high, low)):
            forward[parity, part, :half, :count] = piece
            backward[parity, part, :count, :half] = piece.T
        layout.append((cosines[0], len(cosines), count))
    return forward, backward, tuple(layout)


def split_dot(rows, high, low):
    count = rows.shape[0]
    top = rows.astype(BF16)
    rest = (rows - top.astype(F32)).astype(BF16)
    both = jnp.dot(jnp.concatenate([top, rest], axis=0), high, preferred_element_type=F32)
    cross = jnp.dot(top, low, preferred_element_type=F32)
    return both[:count] + both[count:] + cross


def filter_in_place(buf, levels, mask, fwd, bwd):
    width = buf.shape[-1]
    rows = levels * 16
    first = buf[0].reshape(rows, width)
    second = buf[1].reshape(rows, width)
    dropped = []
    for parity, folded in enumerate((first + second, first - second)):
        coeffs = split_dot(folded, fwd[parity, 0], fwd[parity, 1])
        kept = coeffs.reshape(levels, 2, 8, MODES) * mask[parity][None]
        dropped.append(split_dot(kept.reshape(rows, MODES), bwd[parity, 0], bwd[parity, 1]))
    even, odd = dropped
    buf[0] = (first - (even + odd)).reshape(levels, 2, 8, width)
    buf[1] = (second - (even - odd)).reshape(levels, 2, 8, width)


def step_kernel(
    half,
    bands,
    layout,
    cutoffs,
    cost,
    tl_hbm,
    adj_hbm,
    zonal_hbm,
    merid_hbm,
    vert_hbm,
    state_hbm,
    op_hbm,
    remap_hbm,
    fwd_hbm,
    bwd_hbm,
    out_tl,
    out_adj,
    tl,
    adj,
    zonal_raw,
    merid_raw,
    vert_raw,
    state_raw,
    op_raw,
    remap_raw,
    fwd,
    bwd,
    winds,
    qx,
    wext,
    ah,
    acols,
    tbuf,
    tcols,
    aback,
    tback,
    tband,
    abuf,
    mx,
    vx,
    partial,
    spread,
    mats,
    mask,
    send_sem,
    recv_sem,
    load_sem,
):
    width = qx.shape[-1]
    tiles = width // LANES
    lev = lax.axis_index("lev")
    lat = lax.axis_index("lat")
    other = 1 - lev
    has_up = lat < bands - 1
    has_down = lat > 0

    loads = [
        pltpu.make_async_copy(src, dst, load_sem.at[number])
        for number, (src, dst) in enumerate(
            [
                (tl_hbm, tl),
                (adj_hbm, adj),
                (zonal_hbm, zonal_raw),
                (merid_hbm, merid_raw),
                (vert_hbm, vert_raw),
                (state_hbm, state_raw),
                (op_hbm, op_raw),
                (remap_hbm, remap_raw),
                (fwd_hbm, fwd),
                (bwd_hbm, bwd),
            ]
        )
    ]
    for number in (1, 0, 2, 3, 4, 5, 6, 7):
        loads[number].start()

    barrier = pltpu.get_barrier_semaphore()
    pl.semaphore_signal(barrier, inc=1, device_id=(other, lat), device_id_type=MESH_IDS)

    @pl.when(has_up)
    def _():
        pl.semaphore_signal(barrier, inc=1, device_id=(lev, lat + 1), device_id_type=MESH_IDS)

    @pl.when(has_down)
    def _():
        pl.semaphore_signal(barrier, inc=1, device_id=(lev, lat - 1), device_id_type=MESH_IDS)

    inner = jnp.logical_and(has_up, has_down)

    @pl.when(inner)
    def _():
        pl.semaphore_wait(barrier, 3)

    @pl.when(jnp.logical_not(inner))
    def _():
        pl.semaphore_wait(barrier, 2)

    def remote(number, src, dst, to_lev, to_lat):
        return pltpu.make_async_remote_copy(
            src_ref=src,
            dst_ref=dst,
            send_sem=send_sem.at[number],
            recv_sem=recv_sem.at[number],
            device_id=(to_lev, to_lat),
            device_id_type=MESH_IDS,
        )

    edge = 3 * other
    lat_up = remote(1, qx.at[:, pl.ds(1, 4), 2], qx.at[:, pl.ds(1, 4), 0], lev, lat + 1)
    lat_down = remote(2, qx.at[:, pl.ds(1, 4), 1], qx.at[:, pl.ds(1, 4), 3], lev, lat - 1)
    wind_halo = remote(3, winds.at[edge, pl.ds(8, 8)], wext, other, lat)
    mine = pl.ds(4 * lev, 4)
    theirs = pl.ds(4 * other, 4)
    adj_out_cols = [
        remote(14 + i, ah.at[other, :, i], acols.at[mine, i], other, lat) for i in range(2)
    ]
    pieces = [(i, pl.ds(part * width // 2, width // 2)) for i in range(2) for part in range(2)]
    adj_in_bands = [
        remote(
            4 + number,
            aback.at[pl.ds(3 * other, 5), i, :, cols],
            abuf.at[lev, :, i, :, cols],
            other,
            lat,
        )
        for number, (i, cols) in enumerate(pieces)
    ]
    tl_out_cols = [
        remote(8 + i, tbuf.at[other, :, i], tcols.at[lev, :, i], other, lat) for i in range(2)
    ]
    tl_in_bands = [
        remote(
            10 + number, tback.at[theirs, i, :, cols], tband.at[lev, :, i, :, cols], other, lat
        )
        for number, (i, cols) in enumerate(pieces)
    ]
    merid_up = remote(0, mx.at[:, :, 2], mx.at[:, :, 0], lev, lat + 1)
    merid_down = remote(16, mx.at[:, :, 1], mx.at[:, :, 3], lev, lat - 1)

    def halves(row):
        first = jnp.concatenate([row[:, :half], jnp.zeros((8, width - half), F32)], axis=1)
        second = jnp.concatenate([row[:, half:], jnp.zeros((8, width - half), F32)], axis=1)
        return first, second

    loads[1].wait()
    for i in range(2):
        for k in range(4):
            for h, block in enumerate(halves(adj[:, k, i, :])):
                ah[h, k, i] = block
        adj_out_cols[i].start()

    loads[0].wait()
    for load in loads[8:]:
        load.start()

    def to_halves(i):
        for k in range(4):
            for h, block in enumerate(halves(tl[:, k, i, :])):
                qx[h, 1 + k, 1 + i] = block

    to_halves(1)

    @pl.when(has_up)
    def _():
        lat_up.start()

    to_halves(0)

    @pl.when(has_down)
    def _():
        lat_down.start()

    for load in loads[2:6]:
        load.wait()
    blank = jnp.zeros((4, width - half), F32)
    for k in range(4):
        for first, raw in ((0, zonal_raw), (4, merid_raw), (8, vert_raw)):
            for h in range(2):
                for i in range(2):
                    winds[k, first + 2 * h + i : first + 2 * h + i + 1, :half] = raw[
                        k, i : i + 1, h * half : (h + 1) * half
                    ]
            winds[k, first : first + 4, half:] = blank
        for l in range(2):
            winds[k, 12 + 2 * l : 14 + 2 * l, :half] = state_raw[2 * k + l]
        winds[k, 12:16, half:] = blank
    wind_halo.start()
    acols[mine] = ah[lev]

    zeros = jnp.zeros((8, width), F32)

    @pl.when(jnp.logical_not(has_down))
    def _():
        for h in range(2):
            for k in range(4):
                qx[h, 1 + k, 0] = zeros
                mx[h, k, 0] = zeros

    @pl.when(jnp.logical_not(has_up))
    def _():
        for h in range(2):
            for k in range(4):
                qx[h, 1 + k, 3] = zeros
                mx[h, k, 3] = zeros

    for h in range(2):
        for i in range(2):
            qx[h, 0, 1 + i] = zeros
            qx[h, 5, 1 + i] = zeros
            vx[h, 5 * lev, i] = zeros

    for load in loads[6:8]:
        load.wait()
    for base, raw in ((0, op_raw), (64, remap_raw)):
        for f in range(8):
            table = raw[f]
            for l in range(8):
                at = (f * 8 + l) * 8
                spread[at : at + 8, :] = jnp.broadcast_to(table[:, l : l + 1], (8, LANES))
        for k in range(8):
            for l in range(8):
                mats[base + 8 * k + l] = spread[pl.ds(8 * l + k, 8, stride=64), :]

    column = lax.broadcasted_iota(jnp.int32, (8, MODES), 1)
    for parity, (first, cosines, count) in enumerate(layout):
        number = first + 2 * jnp.where(column < cosines, column, column - cosines)
        for i in range(2):
            drop = jnp.logical_and(number > cutoffs[i], column < count)
            mask[parity, i] = jnp.where(drop, 1.0, 0.0).astype(F32)

    lane = lax.broadcasted_iota(jnp.int32, (8, width), 1)

    def wind(ref_row):
        return jnp.broadcast_to(ref_row, (8, width))

    def lon_diff(z, across):
        after = jnp.where(lane == half - 1, across[:, 0:1], pltpu.roll(z, width - 1, 1))
        before = jnp.where(lane == 0, across[:, half - 1 : half], pltpu.roll(z, 1, 1))
        return after - before

    def product(base, transposed, vec):
        result = []
        for k in range(8):
            terms = [
                mats[base + (8 * l + k if transposed else 8 * k + l)] * vec[l] for l in range(8)
            ]
            while len(terms) > 1:
                terms = [a + b for a, b in zip(terms[::2], terms[1::2])]
            result.append(terms[0])
        return result

    def physics(src, dst, i, part, adjoint):
        steps = jnp.full((8, LANES), cost[i], jnp.int32)

        def tile(t, carry):
            cols = pl.ds(pl.multiple_of(t * LANES, LANES), LANES)
            state = [
                jnp.broadcast_to(
                    winds[l // 2, 12 + 2 * (l % 2) + i : 13 + 2 * (l % 2) + i, cols], (8, LANES)
                )
                for l in range(8)
            ]
            if adjoint:
                vec = [src[l, i, :, cols] for l in range(8)]
            else:
                low = [src[0, l, i, :, cols] for l in range(5)]
                high = [src[1, l, i, :, cols] for l in range(5)]
                both = [low[3] + high[0], low[4] + high[1]]
                vec = product(64, False, low[:3] + both + high[2:])

            def sub_step(s, vec):
                if adjoint:
                    new = [d * v for d, v in zip(state, product(0, True, vec))]
                else:
                    new = product(0, False, [d * v for d, v in zip(state, vec)])
                active = s < steps
                return [jnp.where(active, n, v) for n, v in zip(new, vec)]

            vec = lax.fori_loop(0, SUBS, sub_step, vec)
            if adjoint:
                vec = product(64, True, vec)
            for k in range(8):
                dst[k, i, :, cols] = vec[k]
            return carry

        lax.fori_loop(part * tiles // 2, (part + 1) * tiles // 2, tile, 0)

    for i in range(2):
        adj_out_cols[i].wait_recv()
        for part in range(2):
            physics(acols, aback, i, part, True)
            adj_in_bands[2 * i + part].start()
    abuf[lev] = aback[pl.ds(3 * lev, 5)]

    @pl.when(has_down)
    def _():
        lat_up.wait_recv()

    @pl.when(has_up)
    def _():
        lat_down.wait_recv()

    def advect(k, carry):
        for h in range(2):
            for i in range(2):
                row = 2 * h + i
                q = qx[h, k + 1, i + 1]
                zonal = wind(winds[k, row : row + 1]) * lon_diff(q, qx[1 - h, k + 1, i + 1])
                merid = wind(winds[k, 4 + row : 5 + row]) * (
                    qx[h, k + 1, i + 2] - qx[h, k + 1, i]
                )
                vert = wind(winds[k, 8 + row : 9 + row]) * (
                    qx[h, k + 2, i + 1] - qx[h, k, i + 1]
                )
                tbuf[h, k + lev, i] = q - 0.5 * (zonal + merid + vert)
        return carry

    lax.fori_loop(0, 4, advect, 0)

    wind_halo.wait_recv()
    sign = 0.5 - lev.astype(F32)
    for h in range(2):
        for i in range(2):
            row = 2 * h + i
            tbuf[h, 4 * other, i] = sign * (wind(wext[row : row + 1]) * qx[h, 1 + edge, 1 + i])
    for load in loads[8:]:
        load.wait()
    filter_in_place(tbuf, 5, mask, fwd, bwd)
    for copy in tl_out_cols:
        copy.start()
    tcols[lev] = tbuf[lev]

    for copy in adj_in_bands:
        copy.wait_recv()
    filter_in_place(abuf, 5, mask, fwd, bwd)

    def merid_parts(k, carry):
        for h in range(2):
            for i in range(2):
                row = 2 * h + i
                mx[h, k, i + 1] = wind(winds[k, 4 + row : 5 + row]) * abuf[h, k + lev, i]
        return carry

    lax.fori_loop(0, 4, merid_parts, 0)

    @pl.when(has_up)
    def _():
        merid_up.start()

    @pl.when(has_down)
    def _():
        merid_down.start()

    def vert_parts(k, carry):
        for h in range(2):
            for i in range(2):
                row = 2 * h + i
                vx[h, k + 1, i] = wind(winds[k, 8 + row : 9 + row]) * abuf[h, k + lev, i]
        return carry

    lax.fori_loop(0, 4, vert_parts, 0)
    for h in range(2):
        for i in range(2):
            row = 2 * h + i
            vx[h, 5 * other, i] = wind(wext[row : row + 1]) * abuf[h, 4 * other, i]

    def zonal_parts(k, carry):
        for i in range(2):
            p = [abuf[h, k + lev, i] for h in range(2)]
            z = [wind(winds[k, 2 * h + i : 2 * h + i + 1]) * p[h] for h in range(2)]
            for h in range(2):
                total = lon_diff(z[h], z[1 - h]) + (vx[h, k + 2, i] - vx[h, k, i])
                partial[h, k, i] = p[h] + 0.5 * total
        return carry

    lax.fori_loop(0, 4, zonal_parts, 0)

    for i in range(2):
        tl_out_cols[i].wait_recv()
        for part in range(2):
            physics(tcols, tback, i, part, False)
            tl_in_bands[2 * i + part].start()
    tband[lev] = tback[mine]

    def join(pair):
        return jnp.concatenate([block[:, :half] for block in pair], axis=1)

    @pl.when(has_down)
    def _():
        merid_up.wait_recv()

    @pl.when(has_up)
    def _():
        merid_down.wait_recv()

    for k in range(4):
        for i in range(2):
            out_adj[:, k, i, :] = join(
                [
                    partial[h, k, i] + 0.5 * (mx[h, k, i + 2] - mx[h, k, i])
                    for h in range(2)
                ]
            )

    for i in range(2):
        for copy in tl_in_bands[2 * i : 2 * i + 2]:
            copy.wait_recv()
        for k in range(4):
            out_tl[:, k, i, :] = join([tband[h, k, i] for h in range(2)])

    for copy in [wind_halo] + adj_out_cols + adj_in_bands + tl_out_cols + tl_in_bands:
        copy.wait_send()

    @pl.when(has_up)
    def _():
        lat_up.wait_send()
        merid_up.wait_send()

    @pl.when(has_down)
    def _():
        lat_down.wait_send()
        merid_down.wait_send()


def hand_over(first, second, first_out, second_out, sems):
    copies = [
        pltpu.make_async_copy(first, first_out, sems.at[0]),
        pltpu.make_async_copy(second, second_out, sems.at[1]),
    ]
    for copy in copies:
        copy.start()
    for copy in copies:
        copy.wait()


def one_kernel(
    tl_pert,
    adj_in,
    zonal_wind,
    merid_wind,
    vert_wind,
    cutoffs,
    remap,
    phys_op,
    phys_state,
    column_cost,
):
    length = tl_pert.shape[3]
    half = length // 2
    padded = -(-half // LANES) * LANES
    bands = lax.axis_size("lat")
    forward, backward, layout = mode_tables(length, half, padded)
    vmem = pl.BlockSpec(memory_space=pltpu.VMEM)
    smem = pl.BlockSpec(memory_space=pltpu.SMEM)
    hbm = pl.BlockSpec(memory_space=pl.ANY)
    band_shape = (2, 4, 2, 8, padded)
    edged_shape = (2, 5, 2, 8, padded)
    column_shape = (8, 2, 8, padded)
    fields = [tl_pert, adj_in, zonal_wind, merid_wind, vert_wind, phys_state, phys_op, remap]
    done = pl.pallas_call(
        functools.partial(step_kernel, half, bands, layout),
        out_shape=[pltpu.VMEM(tl_pert.shape, F32)] * 2,
        in_specs=[smem] * 2 + [hbm] * 10,
        out_specs=[vmem] * 2,
        scratch_shapes=[pltpu.VMEM(field.shape, F32) for field in fields]
        + [
            pltpu.VMEM(forward.shape, BF16),
            pltpu.VMEM(backward.shape, BF16),
            pltpu.VMEM((4, 16, padded), F32),
            pltpu.VMEM((2, 6, 4, 8, padded), F32),
            pltpu.VMEM((8, padded), F32),
            pltpu.VMEM(band_shape, F32),
            pltpu.VMEM(column_shape, F32),
            pltpu.VMEM(edged_shape, F32),
            pltpu.VMEM(edged_shape, F32),
            pltpu.VMEM(column_shape, F32),
            pltpu.VMEM(column_shape, F32),
            pltpu.VMEM(band_shape, F32),
            pltpu.VMEM(edged_shape, F32),
            pltpu.VMEM((2, 4, 4, 8, padded), F32),
            pltpu.VMEM((2, 6, 2, 8, padded), F32),
            pltpu.VMEM(band_shape, F32),
            pltpu.VMEM((512, LANES), F32),
            pltpu.VMEM((128, 8, LANES), F32),
            pltpu.VMEM((2, 2, 8, MODES), F32),
            pltpu.SemaphoreType.DMA((17,)),
            pltpu.SemaphoreType.DMA((17,)),
            pltpu.SemaphoreType.DMA((10,)),
        ],
        compiler_params=pltpu.CompilerParams(
            collective_id=0, has_side_effects=True, vmem_limit_bytes=48 * 1024 * 1024
        ),
        cost_estimate=pl.CostEstimate(
            flops=10**9, bytes_accessed=8 * 10**6, transcendentals=0
        ),
    )(cutoffs, column_cost[:, 0], *fields, jnp.asarray(forward), jnp.asarray(backward))
    return pl.pallas_call(
        hand_over,
        out_shape=[jax.ShapeDtypeStruct(tl_pert.shape, F32)] * 2,
        in_specs=[hbm] * 2,
        out_specs=[hbm] * 2,
        scratch_shapes=[pltpu.SemaphoreType.DMA((2,))],
        compiler_params=pltpu.CompilerParams(vmem_limit_bytes=1024 * 1024),
    )(*done)


def fits_kernel(mesh):
    return mesh.shape["lev"] == 2 and mesh.shape["lat"] > 1


def solution(mesh):
    placed = (
        P(None, "lev", "lat", None),
        P(None, "lev", "lat", None),
        P("lev", "lat", None),
        P("lev", "lat", None),
        P("lev", "lat", None),
        P("lat"),
        P(),
        P(),
        P(None, "lat", "lev"),
        P("lat", "lev"),
    )
    return jax.shard_map(
        one_kernel if fits_kernel(mesh) else local,
        mesh=mesh,
        in_specs=placed,
        out_specs=(P(None, "lev", "lat", None), P(None, "lev", "lat", None)),
        check_vma=False,
    )
```

```python
import functools
import math

import jax
import jax.numpy as jnp
import ml_dtypes
import numpy as np
from jax import lax
from jax.experimental import pallas as pl
from jax.experimental.pallas import tpu as pltpu
from jax.sharding import PartitionSpec as P

SUBS = 8


HIGHEST = lax.Precision.HIGHEST


def with_halo(cells, sides, width):
    for axis, dim in sides:
        count = lax.axis_size(axis)
        ends = count - 1
        head = lax.slice_in_dim(cells, 0, width, axis=dim)
        tail = lax.slice_in_dim(cells, cells.shape[dim] - width, cells.shape[dim], axis=dim)
        cells = jnp.concatenate(
            [
                lax.ppermute(tail, axis, [(i, (i + 1) % count) for i in range(ends)]),
                cells,
                lax.ppermute(head, axis, [((i + 1) % count, i) for i in range(ends)]),
            ],
            axis=dim,
        )
    return cells


def fourier_basis(length):
    sample = jnp.arange(length, dtype=jnp.int32)[:, None]
    column = jnp.arange(length, dtype=jnp.int32)[None, :]
    nyquist = length // 2
    wavenumber = jnp.where(column <= nyquist, column, column - nyquist)
    angles = (sample * wavenumber % length).astype(jnp.float32) * (2.0 * math.pi / length)
    weights = jnp.where(
        (wavenumber == 0) | (wavenumber == nyquist),
        1.0 / math.sqrt(length),
        math.sqrt(2.0 / length),
    )
    basis_table = jnp.where(column <= nyquist, jnp.cos(angles), jnp.sin(angles)) * weights
    return (basis_table, wavenumber[0])


def upper_modes(length):
    basis_table, wavenumber = fourier_basis(length)
    nyquist = length // 2
    lowest = 3 * length // 8 + 1
    cosine_part = basis_table[:, lowest : nyquist + 1]
    sine_part = basis_table[:, nyquist + lowest :]
    modes = jnp.concatenate([cosine_part, sine_part], axis=1)
    mode_numbers = jnp.concatenate(
        [wavenumber[lowest : nyquist + 1], wavenumber[nyquist + lowest :]]
    )
    return (modes, mode_numbers)


def polar_filter(grid_field, drop_mask, modes):
    coeffs = jnp.einsum("fkix,xc->fkic", grid_field, modes, precision=HIGHEST)
    return grid_field - jnp.einsum("fkic,xc->fkix", coeffs * drop_mask, modes, precision=HIGHEST)


def tangent_advect(grid_field, zonal_wind, merid_wind, vert_wind):
    padded = with_halo(grid_field, (("lev", 1), ("lat", 2)), 1)
    lat_diff = padded[:, 1:-1, 2:] - padded[:, 1:-1, :-2]
    lev_diff = padded[:, 2:, 1:-1] - padded[:, :-2, 1:-1]
    lon_diff = jnp.roll(grid_field, -1, axis=3) - jnp.roll(grid_field, 1, axis=3)
    return grid_field - 0.5 * (zonal_wind * lon_diff + merid_wind * lat_diff + vert_wind * lev_diff)


def adjoint_advect(grid_field, zonal_wind, merid_wind, vert_wind):
    merid_padded = with_halo(merid_wind * grid_field, (("lat", 2),), 1)
    vert_padded = with_halo(vert_wind * grid_field, (("lev", 1),), 1)
    zonal_part = zonal_wind * grid_field
    lon_term = jnp.roll(zonal_part, -1, axis=3) - jnp.roll(zonal_part, 1, axis=3)
    lat_term = merid_padded[:, :, 2:] - merid_padded[:, :, :-2]
    lev_term = vert_padded[:, 2:] - vert_padded[:, :-2]
    return grid_field + 0.5 * (lon_term + lat_term + lev_term)


def to_columns(stacked):
    return lax.all_to_all(stacked, "lev", split_axis=4, concat_axis=2, tiled=True)


def to_bands(stacked):
    return lax.all_to_all(stacked, "lev", split_axis=2, concat_axis=4, tiled=True)


def column_physics(operators, state_rows, fields_all, row_counts):
    unit_rows = jnp.ones_like(state_rows)
    before = jnp.stack([state_rows, unit_rows])[:, None]
    after = jnp.stack([unit_rows, state_rows])[:, None]
    counts_view = row_counts[None, None, None, :, None]
    current = fields_all
    for sub_step in range(SUBS):
        advanced = after * jnp.einsum(
            "sfkl,sflix->sfkix", operators, before * current, precision=HIGHEST
        )
        current = jnp.where(sub_step < counts_view, advanced, current)
    return current


def local(
    tl_pert,
    adj_in,
    zonal_wind,
    merid_wind,
    vert_wind,
    cutoffs,
    remap,
    phys_op,
    phys_state,
    column_cost,
):
    modes, mode_numbers = upper_modes(tl_pert.shape[3])
    drop_mask = (mode_numbers[None, :] > cutoffs[:, None]).astype(jnp.float32)
    operators = jnp.stack([phys_op, jnp.swapaxes(phys_op, 1, 2)])
    row_counts = column_cost[:, 0]
    adj_columns = to_columns(adj_in[None])
    tl_advected = tangent_advect(tl_pert, zonal_wind, merid_wind, vert_wind)
    tl_filtered = polar_filter(tl_advected, drop_mask, modes)
    tl_columns = to_columns(tl_filtered[None])
    tl_remapped = jnp.einsum("fkl,sflix->sfkix", remap, tl_columns, precision=HIGHEST)
    fields_all = jnp.concatenate([tl_remapped, adj_columns], axis=0)
    physics_done = column_physics(operators, phys_state, fields_all, row_counts)
    tl_finished = physics_done[0:1]
    adj_remapped = jnp.einsum("flk,sflix->sfkix", remap, physics_done[1:2], precision=HIGHEST)
    tl_result = to_bands(tl_finished)[0]
    adj_bands = to_bands(adj_remapped)[0]
    adj_filtered = polar_filter(adj_bands, drop_mask, modes)
    adj_result = adjoint_advect(adj_filtered, zonal_wind, merid_wind, vert_wind)
    return (tl_result, adj_result)

BF16 = jnp.bfloat16
F32 = jnp.float32
LANES = 128
MODES = 256
MESH_IDS = pl.DeviceIdType.MESH


def mode_tables(length, half, padded):
    nyquist = length // 2
    lowest = 3 * length // 8 + 1
    forward = np.zeros((2, 2, padded, MODES), ml_dtypes.bfloat16)
    backward = np.zeros((2, 2, MODES, padded), ml_dtypes.bfloat16)
    layout = []
    sample = np.arange(half)
    for parity in range(2):
        cosines = [m for m in range(lowest, nyquist + 1) if m % 2 == parity]
        sines = [m for m in range(lowest, nyquist) if m % 2 == parity]
        waves = np.array(cosines + sines)
        count = len(waves)
        angles = 2.0 * np.pi / length * ((sample[:, None] * waves[None, :]) % length)
        is_cosine = (np.arange(count) < len(cosines))[None, :]
        weight = np.where(waves == nyquist, length**-0.5, (2.0 / length) ** 0.5)
        table = np.where(is_cosine, np.cos(angles), np.sin(angles)) * weight[None, :]
        high = table.astype(ml_dtypes.bfloat16)
        low = (table - high.astype(np.float64)).astype(ml_dtypes.bfloat16)
        for part, piece in enumerate((high, low)):
            forward[parity, part, :half, :count] = piece
            backward[parity, part, :count, :half] = piece.T
        layout.append((cosines[0], len(cosines), count))
    return forward, backward, tuple(layout)


def split_dot(rows, high, low):
    count = rows.shape[0]
    top = rows.astype(BF16)
    rest = (rows - top.astype(F32)).astype(BF16)
    both = jnp.dot(jnp.concatenate([top, rest], axis=0), high, preferred_element_type=F32)
    cross = jnp.dot(top, low, preferred_element_type=F32)
    return both[:count] + both[count:] + cross


def filter_in_place(buf, levels, mask, fwd, bwd):
    width = buf.shape[-1]
    rows = levels * 16
    first = buf[0].reshape(rows, width)
    second = buf[1].reshape(rows, width)
    dropped = []
    for parity, folded in enumerate((first + second, first - second)):
        coeffs = split_dot(folded, fwd[parity, 0], fwd[parity, 1])
        kept = coeffs.reshape(levels, 2, 8, MODES) * mask[parity][None]
        dropped.append(split_dot(kept.reshape(rows, MODES), bwd[parity, 0], bwd[parity, 1]))
    even, odd = dropped
    buf[0] = (first - (even + odd)).reshape(levels, 2, 8, width)
    buf[1] = (second - (even - odd)).reshape(levels, 2, 8, width)


def step_kernel(
    half,
    bands,
    layout,
    cutoffs,
    cost,
    tl_hbm,
    adj_hbm,
    zonal_hbm,
    merid_hbm,
    vert_hbm,
    state_hbm,
    op_hbm,
    remap_hbm,
    fwd_hbm,
    bwd_hbm,
    out_tl,
    out_adj,
    tl,
    adj,
    zonal_raw,
    merid_raw,
    vert_raw,
    state_raw,
    op_raw,
    remap_raw,
    fwd,
    bwd,
    winds,
    qx,
    wext,
    ah,
    acols,
    tbuf,
    tcols,
    aback,
    tback,
    tband,
    abuf,
    mx,
    vx,
    partial,
    spread,
    mats,
    mask,
    send_sem,
    recv_sem,
    load_sem,
):
    width = qx.shape[-1]
    tiles = width // LANES
    lev = lax.axis_index("lev")
    lat = lax.axis_index("lat")
    other = 1 - lev
    has_up = lat < bands - 1
    has_down = lat > 0

    loads = [
        pltpu.make_async_copy(src, dst, load_sem.at[number])
        for number, (src, dst) in enumerate(
            [
                (tl_hbm, tl),
                (adj_hbm, adj),
                (zonal_hbm, zonal_raw),
                (merid_hbm, merid_raw),
                (vert_hbm, vert_raw),
                (state_hbm, state_raw),
                (op_hbm, op_raw),
                (remap_hbm, remap_raw),
                (fwd_hbm, fwd),
                (bwd_hbm, bwd),
            ]
        )
    ]
    for number in (1, 0, 2, 3, 4, 5, 6, 7):
        loads[number].start()

    barrier = pltpu.get_barrier_semaphore()
    pl.semaphore_signal(barrier, inc=1, device_id=(other, lat), device_id_type=MESH_IDS)

    @pl.when(has_up)
    def _():
        pl.semaphore_signal(barrier, inc=1, device_id=(lev, lat + 1), device_id_type=MESH_IDS)

    @pl.when(has_down)
    def _():
        pl.semaphore_signal(barrier, inc=1, device_id=(lev, lat - 1), device_id_type=MESH_IDS)

    inner = jnp.logical_and(has_up, has_down)

    @pl.when(inner)
    def _():
        pl.semaphore_wait(barrier, 3)

    @pl.when(jnp.logical_not(inner))
    def _():
        pl.semaphore_wait(barrier, 2)

    def remote(number, src, dst, to_lev, to_lat):
        return pltpu.make_async_remote_copy(
            src_ref=src,
            dst_ref=dst,
            send_sem=send_sem.at[number],
            recv_sem=recv_sem.at[number],
            device_id=(to_lev, to_lat),
            device_id_type=MESH_IDS,
        )

    edge = 3 * other
    lat_up = remote(1, qx.at[:, pl.ds(1, 4), 2], qx.at[:, pl.ds(1, 4), 0], lev, lat + 1)
    lat_down = remote(2, qx.at[:, pl.ds(1, 4), 1], qx.at[:, pl.ds(1, 4), 3], lev, lat - 1)
    wind_halo = remote(3, winds.at[edge, pl.ds(8, 8)], wext, other, lat)
    mine = pl.ds(4 * lev, 4)
    theirs = pl.ds(4 * other, 4)
    adj_out_cols = [
        remote(14 + i, ah.at[other, :, i], acols.at[mine, i], other, lat) for i in range(2)
    ]
    pieces = [(i, pl.ds(part * width // 2, width // 2)) for i in range(2) for part in range(2)]
    adj_in_bands = [
        remote(
            4 + number,
            aback.at[pl.ds(3 * other, 5), i, :, cols],
            abuf.at[lev, :, i, :, cols],
            other,
            lat,
        )
        for number, (i, cols) in enumerate(pieces)
    ]
    tl_out_cols = [
        remote(8 + i, tbuf.at[other, :, i], tcols.at[lev, :, i], other, lat) for i in range(2)
    ]
    tl_in_bands = [
        remote(
            10 + number, tback.at[theirs, i, :, cols], tband.at[lev, :, i, :, cols], other, lat
        )
        for number, (i, cols) in enumerate(pieces)
    ]
    merid_up = remote(0, mx.at[:, :, 2], mx.at[:, :, 0], lev, lat + 1)
    merid_down = remote(16, mx.at[:, :, 1], mx.at[:, :, 3], lev, lat - 1)

    def halves(row):
        first = jnp.concatenate([row[:, :half], jnp.zeros((8, width - half), F32)], axis=1)
        second = jnp.concatenate([row[:, half:], jnp.zeros((8, width - half), F32)], axis=1)
        return first, second

    loads[1].wait()
    for i in range(2):
        for k in range(4):
            for h, block in enumerate(halves(adj[:, k, i, :])):
                ah[h, k, i] = block
        adj_out_cols[i].start()

    loads[0].wait()
    for load in loads[8:]:
        load.start()

    def to_halves(i):
        for k in range(4):
            for h, block in enumerate(halves(tl[:, k, i, :])):
                qx[h, 1 + k, 1 + i] = block

    to_halves(1)

    @pl.when(has_up)
    def _():
        lat_up.start()

    to_halves(0)

    @pl.when(has_down)
    def _():
        lat_down.start()

    for load in loads[2:6]:
        load.wait()
    blank = jnp.zeros((4, width - half), F32)
    for k in range(4):
        for first, raw in ((0, zonal_raw), (4, merid_raw), (8, vert_raw)):
            for h in range(2):
                for i in range(2):
                    winds[k, first + 2 * h + i : first + 2 * h + i + 1, :half] = raw[
                        k, i : i + 1, h * half : (h + 1) * half
                    ]
            winds[k, first : first + 4, half:] = blank
        for l in range(2):
            winds[k, 12 + 2 * l : 14 + 2 * l, :half] = state_raw[2 * k + l]
        winds[k, 12:16, half:] = blank
    wind_halo.start()
    acols[mine] = ah[lev]

    zeros = jnp.zeros((8, width), F32)

    @pl.when(jnp.logical_not(has_down))
    def _():
        for h in range(2):
            for k in range(4):
                qx[h, 1 + k, 0] = zeros
                mx[h, k, 0] = zeros

    @pl.when(jnp.logical_not(has_up))
    def _():
        for h in range(2):
            for k in range(4):
                qx[h, 1 + k, 3] = zeros
                mx[h, k, 3] = zeros

    for h in range(2):
        for i in range(2):
            qx[h, 0, 1 + i] = zeros
            qx[h, 5, 1 + i] = zeros
            vx[h, 5 * lev, i] = zeros

    for load in loads[6:8]:
        load.wait()
    for base, raw in ((0, op_raw), (64, remap_raw)):
        for f in range(8):
            table = raw[f]
            for l in range(8):
                at = (f * 8 + l) * 8
                spread[at : at + 8, :] = jnp.broadcast_to(table[:, l : l + 1], (8, LANES))
        for k in range(8):
            for l in range(8):
                mats[base + 8 * k + l] = spread[pl.ds(8 * l + k, 8, stride=64), :]

    column = lax.broadcasted_iota(jnp.int32, (8, MODES), 1)
    for parity, (first, cosines, count) in enumerate(layout):
        number = first + 2 * jnp.where(column < cosines, column, column - cosines)
        for i in range(2):
            drop = jnp.logical_and(number > cutoffs[i], column < count)
            mask[parity, i] = jnp.where(drop, 1.0, 0.0).astype(F32)

    lane = lax.broadcasted_iota(jnp.int32, (8, width), 1)

    def wind(ref_row):
        return jnp.broadcast_to(ref_row, (8, width))

    def lon_diff(z, across):
        after = jnp.where(lane == half - 1, across[:, 0:1], pltpu.roll(z, width - 1, 1))
        before = jnp.where(lane == 0, across[:, half - 1 : half], pltpu.roll(z, 1, 1))
        return after - before

    spots = tiles // 2

    def product(base, transposed, vec):
        result = []
        for k in range(8):
            total = [None] * spots
            for l in range(8):
                weight = mats[base + (8 * l + k if transposed else 8 * k + l)]
                for t in range(spots):
                    term = weight * vec[l][t]
                    total[t] = term if l == 0 else total[t] + term
            result.append(total)
        return result

    def physics(src, dst, i, part, adjoint):
        steps = jnp.full((8, LANES), cost[i], jnp.int32)
        cols = [pl.ds((part * spots + t) * LANES, LANES) for t in range(spots)]

        def scale(vec):
            result = []
            for l in range(8):
                row = 12 + 2 * (l % 2) + i
                result.append(
                    [
                        jnp.broadcast_to(winds[l // 2, row : row + 1, cols[t]], (8, LANES))
                        * vec[l][t]
                        for t in range(spots)
                    ]
                )
            return result

        def sub_step(s, vec):
            new = scale(product(0, adjoint, vec))
            active = s < steps
            return [
                [jnp.where(active, n, v) for n, v in zip(news, olds)]
                for news, olds in zip(new, vec)
            ]

        if adjoint:
            vec = [[src[l, i, :, at] for at in cols] for l in range(8)]
            vec = scale(product(0, True, vec))
        else:
            vec = []
            for l in range(8):
                if l < 3:
                    vec.append([src[0, l, i, :, at] for at in cols])
                elif l > 4:
                    vec.append([src[1, l - 3, i, :, at] for at in cols])
                else:
                    vec.append([src[0, l, i, :, at] + src[1, l - 3, i, :, at] for at in cols])
            vec = scale(product(64, False, vec))
        vec = lax.fori_loop(1, SUBS, sub_step, vec)
        vec = product(64, True, vec) if adjoint else product(0, False, vec)
        for k in range(8):
            for t in range(spots):
                dst[k, i, :, cols[t]] = vec[k][t]

    for i in range(2):
        adj_out_cols[i].wait_recv()
        for part in range(2):
            physics(acols, aback, i, part, True)
            adj_in_bands[2 * i + part].start()
    abuf[lev] = aback[pl.ds(3 * lev, 5)]

    @pl.when(has_down)
    def _():
        lat_up.wait_recv()

    @pl.when(has_up)
    def _():
        lat_down.wait_recv()

    def advect(k, carry):
        for h in range(2):
            for i in range(2):
                row = 2 * h + i
                q = qx[h, k + 1, i + 1]
                zonal = wind(winds[k, row : row + 1]) * lon_diff(q, qx[1 - h, k + 1, i + 1])
                merid = wind(winds[k, 4 + row : 5 + row]) * (
                    qx[h, k + 1, i + 2] - qx[h, k + 1, i]
                )
                vert = wind(winds[k, 8 + row : 9 + row]) * (
                    qx[h, k + 2, i + 1] - qx[h, k, i + 1]
                )
                tbuf[h, k + lev, i] = q - 0.5 * (zonal + merid + vert)
        return carry

    lax.fori_loop(0, 4, advect, 0)

    wind_halo.wait_recv()
    sign = 0.5 - lev.astype(F32)
    for h in range(2):
        for i in range(2):
            row = 2 * h + i
            tbuf[h, 4 * other, i] = sign * (wind(wext[row : row + 1]) * qx[h, 1 + edge, 1 + i])
    for load in loads[8:]:
        load.wait()
    filter_in_place(tbuf, 5, mask, fwd, bwd)
    for copy in tl_out_cols:
        copy.start()
    tcols[lev] = tbuf[lev]

    for copy in adj_in_bands:
        copy.wait_recv()
    filter_in_place(abuf, 5, mask, fwd, bwd)

    def merid_parts(k, carry):
        for h in range(2):
            for i in range(2):
                row = 2 * h + i
                mx[h, k, i + 1] = wind(winds[k, 4 + row : 5 + row]) * abuf[h, k + lev, i]
        return carry

    lax.fori_loop(0, 4, merid_parts, 0)

    @pl.when(has_up)
    def _():
        merid_up.start()

    @pl.when(has_down)
    def _():
        merid_down.start()

    def vert_parts(k, carry):
        for h in range(2):
            for i in range(2):
                row = 2 * h + i
                vx[h, k + 1, i] = wind(winds[k, 8 + row : 9 + row]) * abuf[h, k + lev, i]
        return carry

    lax.fori_loop(0, 4, vert_parts, 0)
    for h in range(2):
        for i in range(2):
            row = 2 * h + i
            vx[h, 5 * other, i] = wind(wext[row : row + 1]) * abuf[h, 4 * other, i]

    def zonal_parts(k, carry):
        for i in range(2):
            p = [abuf[h, k + lev, i] for h in range(2)]
            z = [wind(winds[k, 2 * h + i : 2 * h + i + 1]) * p[h] for h in range(2)]
            for h in range(2):
                total = lon_diff(z[h], z[1 - h]) + (vx[h, k + 2, i] - vx[h, k, i])
                partial[h, k, i] = p[h] + 0.5 * total
        return carry

    lax.fori_loop(0, 4, zonal_parts, 0)

    for i in range(2):
        tl_out_cols[i].wait_recv()
        for part in range(2):
            physics(tcols, tback, i, part, False)
            tl_in_bands[2 * i + part].start()
    tband[lev] = tback[mine]

    def join(pair):
        return jnp.concatenate([block[:, :half] for block in pair], axis=1)

    @pl.when(has_down)
    def _():
        merid_up.wait_recv()

    @pl.when(has_up)
    def _():
        merid_down.wait_recv()

    for k in range(4):
        for i in range(2):
            out_adj[:, k, i, :] = join(
                [
                    partial[h, k, i] + 0.5 * (mx[h, k, i + 2] - mx[h, k, i])
                    for h in range(2)
                ]
            )

    for i in range(2):
        for copy in tl_in_bands[2 * i : 2 * i + 2]:
            copy.wait_recv()
        for k in range(4):
            out_tl[:, k, i, :] = join([tband[h, k, i] for h in range(2)])

    for copy in [wind_halo] + adj_out_cols + adj_in_bands + tl_out_cols + tl_in_bands:
        copy.wait_send()

    @pl.when(has_up)
    def _():
        lat_up.wait_send()
        merid_up.wait_send()

    @pl.when(has_down)
    def _():
        lat_down.wait_send()
        merid_down.wait_send()


def hand_over(first, second, first_out, second_out, sems):
    copies = [
        pltpu.make_async_copy(first, first_out, sems.at[0]),
        pltpu.make_async_copy(second, second_out, sems.at[1]),
    ]
    for copy in copies:
        copy.start()
    for copy in copies:
        copy.wait()


def one_kernel(
    tl_pert,
    adj_in,
    zonal_wind,
    merid_wind,
    vert_wind,
    cutoffs,
    remap,
    phys_op,
    phys_state,
    column_cost,
):
    length = tl_pert.shape[3]
    half = length // 2
    padded = -(-half // LANES) * LANES
    bands = lax.axis_size("lat")
    forward, backward, layout = mode_tables(length, half, padded)
    vmem = pl.BlockSpec(memory_space=pltpu.VMEM)
    smem = pl.BlockSpec(memory_space=pltpu.SMEM)
    hbm = pl.BlockSpec(memory_space=pl.ANY)
    band_shape = (2, 4, 2, 8, padded)
    edged_shape = (2, 5, 2, 8, padded)
    column_shape = (8, 2, 8, padded)
    fields = [tl_pert, adj_in, zonal_wind, merid_wind, vert_wind, phys_state, phys_op, remap]
    done = pl.pallas_call(
        functools.partial(step_kernel, half, bands, layout),
        out_shape=[pltpu.VMEM(tl_pert.shape, F32)] * 2,
        in_specs=[smem] * 2 + [hbm] * 10,
        out_specs=[vmem] * 2,
        scratch_shapes=[pltpu.VMEM(field.shape, F32) for field in fields]
        + [
            pltpu.VMEM(forward.shape, BF16),
            pltpu.VMEM(backward.shape, BF16),
            pltpu.VMEM((4, 16, padded), F32),
            pltpu.VMEM((2, 6, 4, 8, padded), F32),
            pltpu.VMEM((8, padded), F32),
            pltpu.VMEM(band_shape, F32),
            pltpu.VMEM(column_shape, F32),
            pltpu.VMEM(edged_shape, F32),
            pltpu.VMEM(edged_shape, F32),
            pltpu.VMEM(column_shape, F32),
            pltpu.VMEM(column_shape, F32),
            pltpu.VMEM(band_shape, F32),
            pltpu.VMEM(edged_shape, F32),
            pltpu.VMEM((2, 4, 4, 8, padded), F32),
            pltpu.VMEM((2, 6, 2, 8, padded), F32),
            pltpu.VMEM(band_shape, F32),
            pltpu.VMEM((512, LANES), F32),
            pltpu.VMEM((128, 8, LANES), F32),
            pltpu.VMEM((2, 2, 8, MODES), F32),
            pltpu.SemaphoreType.DMA((17,)),
            pltpu.SemaphoreType.DMA((17,)),
            pltpu.SemaphoreType.DMA((10,)),
        ],
        compiler_params=pltpu.CompilerParams(
            collective_id=0, has_side_effects=True, vmem_limit_bytes=56 * 1024 * 1024
        ),
        cost_estimate=pl.CostEstimate(
            flops=10**9, bytes_accessed=8 * 10**6, transcendentals=0
        ),
    )(cutoffs, column_cost[:, 0], *fields, jnp.asarray(forward), jnp.asarray(backward))
    return pl.pallas_call(
        hand_over,
        out_shape=[jax.ShapeDtypeStruct(tl_pert.shape, F32)] * 2,
        in_specs=[hbm] * 2,
        out_specs=[hbm] * 2,
        scratch_shapes=[pltpu.SemaphoreType.DMA((2,))],
        compiler_params=pltpu.CompilerParams(vmem_limit_bytes=1024 * 1024),
    )(*done)


def fits_kernel(mesh):
    return mesh.shape["lev"] == 2 and mesh.shape["lat"] > 1


def solution(mesh):
    placed = (
        P(None, "lev", "lat", None),
        P(None, "lev", "lat", None),
        P("lev", "lat", None),
        P("lev", "lat", None),
        P("lev", "lat", None),
        P("lat"),
        P(),
        P(),
        P(None, "lat", "lev"),
        P("lat", "lev"),
    )
    return jax.shard_map(
        one_kernel if fits_kernel(mesh) else local,
        mesh=mesh,
        in_specs=placed,
        out_specs=(P(None, "lev", "lat", None), P(None, "lev", "lat", None)),
        check_vma=False,
    )
```

```python
import functools
import math

import jax
import jax.numpy as jnp
import ml_dtypes
import numpy as np
from jax import lax
from jax.experimental import pallas as pl
from jax.experimental.pallas import tpu as pltpu
from jax.sharding import PartitionSpec as P

SUBS = 8


HIGHEST = lax.Precision.HIGHEST


def with_halo(cells, sides, width):
    for axis, dim in sides:
        count = lax.axis_size(axis)
        ends = count - 1
        head = lax.slice_in_dim(cells, 0, width, axis=dim)
        tail = lax.slice_in_dim(cells, cells.shape[dim] - width, cells.shape[dim], axis=dim)
        cells = jnp.concatenate(
            [
                lax.ppermute(tail, axis, [(i, (i + 1) % count) for i in range(ends)]),
                cells,
                lax.ppermute(head, axis, [((i + 1) % count, i) for i in range(ends)]),
            ],
            axis=dim,
        )
    return cells


def fourier_basis(length):
    sample = jnp.arange(length, dtype=jnp.int32)[:, None]
    column = jnp.arange(length, dtype=jnp.int32)[None, :]
    nyquist = length // 2
    wavenumber = jnp.where(column <= nyquist, column, column - nyquist)
    angles = (sample * wavenumber % length).astype(jnp.float32) * (2.0 * math.pi / length)
    weights = jnp.where(
        (wavenumber == 0) | (wavenumber == nyquist),
        1.0 / math.sqrt(length),
        math.sqrt(2.0 / length),
    )
    basis_table = jnp.where(column <= nyquist, jnp.cos(angles), jnp.sin(angles)) * weights
    return (basis_table, wavenumber[0])


def upper_modes(length):
    basis_table, wavenumber = fourier_basis(length)
    nyquist = length // 2
    lowest = 3 * length // 8 + 1
    cosine_part = basis_table[:, lowest : nyquist + 1]
    sine_part = basis_table[:, nyquist + lowest :]
    modes = jnp.concatenate([cosine_part, sine_part], axis=1)
    mode_numbers = jnp.concatenate(
        [wavenumber[lowest : nyquist + 1], wavenumber[nyquist + lowest :]]
    )
    return (modes, mode_numbers)


def polar_filter(grid_field, drop_mask, modes):
    coeffs = jnp.einsum("fkix,xc->fkic", grid_field, modes, precision=HIGHEST)
    return grid_field - jnp.einsum("fkic,xc->fkix", coeffs * drop_mask, modes, precision=HIGHEST)


def tangent_advect(grid_field, zonal_wind, merid_wind, vert_wind):
    padded = with_halo(grid_field, (("lev", 1), ("lat", 2)), 1)
    lat_diff = padded[:, 1:-1, 2:] - padded[:, 1:-1, :-2]
    lev_diff = padded[:, 2:, 1:-1] - padded[:, :-2, 1:-1]
    lon_diff = jnp.roll(grid_field, -1, axis=3) - jnp.roll(grid_field, 1, axis=3)
    return grid_field - 0.5 * (zonal_wind * lon_diff + merid_wind * lat_diff + vert_wind * lev_diff)


def adjoint_advect(grid_field, zonal_wind, merid_wind, vert_wind):
    merid_padded = with_halo(merid_wind * grid_field, (("lat", 2),), 1)
    vert_padded = with_halo(vert_wind * grid_field, (("lev", 1),), 1)
    zonal_part = zonal_wind * grid_field
    lon_term = jnp.roll(zonal_part, -1, axis=3) - jnp.roll(zonal_part, 1, axis=3)
    lat_term = merid_padded[:, :, 2:] - merid_padded[:, :, :-2]
    lev_term = vert_padded[:, 2:] - vert_padded[:, :-2]
    return grid_field + 0.5 * (lon_term + lat_term + lev_term)


def to_columns(stacked):
    return lax.all_to_all(stacked, "lev", split_axis=4, concat_axis=2, tiled=True)


def to_bands(stacked):
    return lax.all_to_all(stacked, "lev", split_axis=2, concat_axis=4, tiled=True)


def column_physics(operators, state_rows, fields_all, row_counts):
    unit_rows = jnp.ones_like(state_rows)
    before = jnp.stack([state_rows, unit_rows])[:, None]
    after = jnp.stack([unit_rows, state_rows])[:, None]
    counts_view = row_counts[None, None, None, :, None]
    current = fields_all
    for sub_step in range(SUBS):
        advanced = after * jnp.einsum(
            "sfkl,sflix->sfkix", operators, before * current, precision=HIGHEST
        )
        current = jnp.where(sub_step < counts_view, advanced, current)
    return current


def local(
    tl_pert,
    adj_in,
    zonal_wind,
    merid_wind,
    vert_wind,
    cutoffs,
    remap,
    phys_op,
    phys_state,
    column_cost,
):
    modes, mode_numbers = upper_modes(tl_pert.shape[3])
    drop_mask = (mode_numbers[None, :] > cutoffs[:, None]).astype(jnp.float32)
    operators = jnp.stack([phys_op, jnp.swapaxes(phys_op, 1, 2)])
    row_counts = column_cost[:, 0]
    adj_columns = to_columns(adj_in[None])
    tl_advected = tangent_advect(tl_pert, zonal_wind, merid_wind, vert_wind)
    tl_filtered = polar_filter(tl_advected, drop_mask, modes)
    tl_columns = to_columns(tl_filtered[None])
    tl_remapped = jnp.einsum("fkl,sflix->sfkix", remap, tl_columns, precision=HIGHEST)
    fields_all = jnp.concatenate([tl_remapped, adj_columns], axis=0)
    physics_done = column_physics(operators, phys_state, fields_all, row_counts)
    tl_finished = physics_done[0:1]
    adj_remapped = jnp.einsum("flk,sflix->sfkix", remap, physics_done[1:2], precision=HIGHEST)
    tl_result = to_bands(tl_finished)[0]
    adj_bands = to_bands(adj_remapped)[0]
    adj_filtered = polar_filter(adj_bands, drop_mask, modes)
    adj_result = adjoint_advect(adj_filtered, zonal_wind, merid_wind, vert_wind)
    return (tl_result, adj_result)

BF16 = jnp.bfloat16
F32 = jnp.float32
LANES = 128
MODES = 256
MESH_IDS = pl.DeviceIdType.MESH


def mode_tables(length, half, padded):
    nyquist = length // 2
    lowest = 3 * length // 8 + 1
    forward = np.zeros((2, 2, padded, MODES), ml_dtypes.bfloat16)
    backward = np.zeros((2, 2, MODES, padded), ml_dtypes.bfloat16)
    layout = []
    sample = np.arange(half)
    for parity in range(2):
        cosines = [m for m in range(lowest, nyquist + 1) if m % 2 == parity]
        sines = [m for m in range(lowest, nyquist) if m % 2 == parity]
        waves = np.array(cosines + sines)
        count = len(waves)
        angles = 2.0 * np.pi / length * ((sample[:, None] * waves[None, :]) % length)
        is_cosine = (np.arange(count) < len(cosines))[None, :]
        weight = np.where(waves == nyquist, length**-0.5, (2.0 / length) ** 0.5)
        table = np.where(is_cosine, np.cos(angles), np.sin(angles)) * weight[None, :]
        high = table.astype(ml_dtypes.bfloat16)
        low = (table - high.astype(np.float64)).astype(ml_dtypes.bfloat16)
        for part, piece in enumerate((high, low)):
            forward[parity, part, :half, :count] = piece
            backward[parity, part, :count, :half] = piece.T
        layout.append((cosines[0], len(cosines), count))
    return forward, backward, tuple(layout)


def split_dot(rows, high, low):
    count = rows.shape[0]
    top = rows.astype(BF16)
    rest = (rows - top.astype(F32)).astype(BF16)
    both = jnp.dot(jnp.concatenate([top, rest], axis=0), high, preferred_element_type=F32)
    cross = jnp.dot(top, low, preferred_element_type=F32)
    return both[:count] + both[count:] + cross


def filter_in_place(buf, levels, mask, fwd, bwd):
    width = buf.shape[-1]
    rows = levels * 16
    first = buf[0].reshape(rows, width)
    second = buf[1].reshape(rows, width)
    dropped = []
    for parity, folded in enumerate((first + second, first - second)):
        coeffs = split_dot(folded, fwd[parity, 0], fwd[parity, 1])
        kept = coeffs.reshape(levels, 2, 8, MODES) * mask[parity][None]
        dropped.append(split_dot(kept.reshape(rows, MODES), bwd[parity, 0], bwd[parity, 1]))
    even, odd = dropped
    buf[0] = (first - (even + odd)).reshape(levels, 2, 8, width)
    buf[1] = (second - (even - odd)).reshape(levels, 2, 8, width)


def step_kernel(
    half,
    bands,
    layout,
    cutoffs,
    cost,
    tl_hbm,
    adj_hbm,
    zonal_hbm,
    merid_hbm,
    vert_hbm,
    state_hbm,
    op_hbm,
    remap_hbm,
    fwd_hbm,
    bwd_hbm,
    out_tl,
    out_adj,
    tl,
    adj,
    zonal_raw,
    merid_raw,
    vert_raw,
    state_raw,
    op_raw,
    remap_raw,
    fwd,
    bwd,
    winds,
    qx,
    wext,
    ah,
    acols,
    tbuf,
    tcols,
    aback,
    tback,
    tband,
    abuf,
    mx,
    vx,
    partial,
    spread,
    mats,
    mask,
    send_sem,
    recv_sem,
    load_sem,
):
    width = qx.shape[-1]
    tiles = width // LANES
    lev = lax.axis_index("lev")
    lat = lax.axis_index("lat")
    other = 1 - lev
    has_up = lat < bands - 1
    has_down = lat > 0

    loads = [
        pltpu.make_async_copy(src, dst, load_sem.at[number])
        for number, (src, dst) in enumerate(
            [
                (tl_hbm, tl),
                (adj_hbm, adj),
                (zonal_hbm, zonal_raw),
                (merid_hbm, merid_raw),
                (vert_hbm, vert_raw),
                (state_hbm, state_raw),
                (op_hbm, op_raw),
                (remap_hbm, remap_raw),
                (fwd_hbm, fwd),
                (bwd_hbm, bwd),
            ]
        )
    ]
    for number in (1, 0, 2, 3, 4, 5, 6, 7):
        loads[number].start()

    barrier = pltpu.get_barrier_semaphore()
    pl.semaphore_signal(barrier, inc=1, device_id=(other, lat), device_id_type=MESH_IDS)

    @pl.when(has_up)
    def _():
        pl.semaphore_signal(barrier, inc=1, device_id=(lev, lat + 1), device_id_type=MESH_IDS)

    @pl.when(has_down)
    def _():
        pl.semaphore_signal(barrier, inc=1, device_id=(lev, lat - 1), device_id_type=MESH_IDS)

    inner = jnp.logical_and(has_up, has_down)

    @pl.when(inner)
    def _():
        pl.semaphore_wait(barrier, 3)

    @pl.when(jnp.logical_not(inner))
    def _():
        pl.semaphore_wait(barrier, 2)

    def remote(number, src, dst, to_lev, to_lat):
        return pltpu.make_async_remote_copy(
            src_ref=src,
            dst_ref=dst,
            send_sem=send_sem.at[number],
            recv_sem=recv_sem.at[number],
            device_id=(to_lev, to_lat),
            device_id_type=MESH_IDS,
        )

    edge = 3 * other
    lat_up = remote(1, qx.at[:, pl.ds(1, 4), 2], qx.at[:, pl.ds(1, 4), 0], lev, lat + 1)
    lat_down = remote(2, qx.at[:, pl.ds(1, 4), 1], qx.at[:, pl.ds(1, 4), 3], lev, lat - 1)
    wind_halo = remote(3, winds.at[edge, pl.ds(8, 8)], wext, other, lat)
    mine = pl.ds(4 * lev, 4)
    theirs = pl.ds(4 * other, 4)
    adj_out_cols = [
        remote(14 + i, ah.at[other, :, i], acols.at[mine, i], other, lat) for i in range(2)
    ]
    pieces = [(i, pl.ds(part * width // 2, width // 2)) for i in range(2) for part in range(2)]
    adj_in_bands = [
        remote(
            4 + number,
            aback.at[pl.ds(3 * other, 5), i, :, cols],
            abuf.at[lev, :, i, :, cols],
            other,
            lat,
        )
        for number, (i, cols) in enumerate(pieces)
    ]
    tl_out_cols = [
        remote(
            17 + number, tbuf.at[other, :, i, :, cols], tcols.at[lev, :, i, :, cols], other, lat
        )
        for number, (i, cols) in enumerate(pieces)
    ]
    tl_in_bands = [
        remote(
            10 + number, tback.at[theirs, i, :, cols], tband.at[lev, :, i, :, cols], other, lat
        )
        for number, (i, cols) in enumerate(pieces)
    ]
    merid_up = remote(0, mx.at[:, :, 2], mx.at[:, :, 0], lev, lat + 1)
    merid_down = remote(16, mx.at[:, :, 1], mx.at[:, :, 3], lev, lat - 1)

    def halves(row):
        first = jnp.concatenate([row[:, :half], jnp.zeros((8, width - half), F32)], axis=1)
        second = jnp.concatenate([row[:, half:], jnp.zeros((8, width - half), F32)], axis=1)
        return first, second

    loads[1].wait()
    for i in range(2):
        for k in range(4):
            for h, block in enumerate(halves(adj[:, k, i, :])):
                ah[h, k, i] = block
        adj_out_cols[i].start()

    loads[0].wait()
    for load in loads[8:]:
        load.start()

    def to_halves(i):
        for k in range(4):
            for h, block in enumerate(halves(tl[:, k, i, :])):
                qx[h, 1 + k, 1 + i] = block

    to_halves(1)

    @pl.when(has_up)
    def _():
        lat_up.start()

    to_halves(0)

    @pl.when(has_down)
    def _():
        lat_down.start()

    for load in loads[2:6]:
        load.wait()
    blank = jnp.zeros((4, width - half), F32)
    for k in range(4):
        for first, raw in ((0, zonal_raw), (4, merid_raw), (8, vert_raw)):
            for h in range(2):
                for i in range(2):
                    winds[k, first + 2 * h + i : first + 2 * h + i + 1, :half] = raw[
                        k, i : i + 1, h * half : (h + 1) * half
                    ]
            winds[k, first : first + 4, half:] = blank
        for l in range(2):
            winds[k, 12 + 2 * l : 14 + 2 * l, :half] = state_raw[2 * k + l]
        winds[k, 12:16, half:] = blank
    wind_halo.start()
    acols[mine] = ah[lev]

    zeros = jnp.zeros((8, width), F32)

    @pl.when(jnp.logical_not(has_down))
    def _():
        for h in range(2):
            for k in range(4):
                qx[h, 1 + k, 0] = zeros
                mx[h, k, 0] = zeros

    @pl.when(jnp.logical_not(has_up))
    def _():
        for h in range(2):
            for k in range(4):
                qx[h, 1 + k, 3] = zeros
                mx[h, k, 3] = zeros

    for h in range(2):
        for i in range(2):
            qx[h, 0, 1 + i] = zeros
            qx[h, 5, 1 + i] = zeros
            vx[h, 5 * lev, i] = zeros

    for load in loads[6:8]:
        load.wait()
    for base, raw in ((0, op_raw), (64, remap_raw)):
        for f in range(8):
            table = raw[f]
            for l in range(8):
                at = (f * 8 + l) * 8
                spread[at : at + 8, :] = jnp.broadcast_to(table[:, l : l + 1], (8, LANES))
        for k in range(8):
            for l in range(8):
                mats[base + 8 * k + l] = spread[pl.ds(8 * l + k, 8, stride=64), :]

    column = lax.broadcasted_iota(jnp.int32, (8, MODES), 1)
    for parity, (first, cosines, count) in enumerate(layout):
        number = first + 2 * jnp.where(column < cosines, column, column - cosines)
        for i in range(2):
            drop = jnp.logical_and(number > cutoffs[i], column < count)
            mask[parity, i] = jnp.where(drop, 1.0, 0.0).astype(F32)

    lane = lax.broadcasted_iota(jnp.int32, (8, width), 1)

    def wind(ref_row):
        return jnp.broadcast_to(ref_row, (8, width))

    def lon_diff(z, across):
        after = jnp.where(lane == half - 1, across[:, 0:1], pltpu.roll(z, width - 1, 1))
        before = jnp.where(lane == 0, across[:, half - 1 : half], pltpu.roll(z, 1, 1))
        return after - before

    spots = tiles // 2

    def product(base, transposed, vec):
        result = []
        for k in range(8):
            total = [None] * spots
            for l in range(8):
                weight = mats[base + (8 * l + k if transposed else 8 * k + l)]
                for t in range(spots):
                    term = weight * vec[l][t]
                    total[t] = term if l == 0 else total[t] + term
            result.append(total)
        return result

    def physics(src, dst, i, part, adjoint):
        steps = jnp.full((8, LANES), cost[i], jnp.int32)
        cols = [pl.ds((part * spots + t) * LANES, LANES) for t in range(spots)]

        def scale(vec):
            result = []
            for l in range(8):
                row = 12 + 2 * (l % 2) + i
                result.append(
                    [
                        jnp.broadcast_to(winds[l // 2, row : row + 1, cols[t]], (8, LANES))
                        * vec[l][t]
                        for t in range(spots)
                    ]
                )
            return result

        def sub_step(s, vec):
            new = scale(product(0, adjoint, vec))
            active = s < steps
            return [
                [jnp.where(active, n, v) for n, v in zip(news, olds)]
                for news, olds in zip(new, vec)
            ]

        if adjoint:
            vec = [[src[l, i, :, at] for at in cols] for l in range(8)]
            vec = scale(product(0, True, vec))
        else:
            vec = []
            for l in range(8):
                if l < 3:
                    vec.append([src[0, l, i, :, at] for at in cols])
                elif l > 4:
                    vec.append([src[1, l - 3, i, :, at] for at in cols])
                else:
                    vec.append([src[0, l, i, :, at] + src[1, l - 3, i, :, at] for at in cols])
            vec = scale(product(64, False, vec))
        vec = lax.fori_loop(1, SUBS, sub_step, vec)
        vec = product(64, True, vec) if adjoint else product(0, False, vec)
        for k in range(8):
            for t in range(spots):
                dst[k, i, :, cols[t]] = vec[k][t]

    for i in range(2):
        adj_out_cols[i].wait_recv()
        for part in range(2):
            physics(acols, aback, i, part, True)
            adj_in_bands[2 * i + part].start()
    abuf[lev] = aback[pl.ds(3 * lev, 5)]

    @pl.when(has_down)
    def _():
        lat_up.wait_recv()

    @pl.when(has_up)
    def _():
        lat_down.wait_recv()

    def advect(k, carry):
        for h in range(2):
            for i in range(2):
                row = 2 * h + i
                q = qx[h, k + 1, i + 1]
                zonal = wind(winds[k, row : row + 1]) * lon_diff(q, qx[1 - h, k + 1, i + 1])
                merid = wind(winds[k, 4 + row : 5 + row]) * (
                    qx[h, k + 1, i + 2] - qx[h, k + 1, i]
                )
                vert = wind(winds[k, 8 + row : 9 + row]) * (
                    qx[h, k + 2, i + 1] - qx[h, k, i + 1]
                )
                tbuf[h, k + lev, i] = q - 0.5 * (zonal + merid + vert)
        return carry

    lax.fori_loop(0, 4, advect, 0)

    wind_halo.wait_recv()
    sign = 0.5 - lev.astype(F32)
    for h in range(2):
        for i in range(2):
            row = 2 * h + i
            tbuf[h, 4 * other, i] = sign * (wind(wext[row : row + 1]) * qx[h, 1 + edge, 1 + i])
    for load in loads[8:]:
        load.wait()
    filter_in_place(tbuf, 5, mask, fwd, bwd)
    for copy in tl_out_cols:
        copy.start()
    tcols[lev] = tbuf[lev]

    for copy in adj_in_bands:
        copy.wait_recv()
    filter_in_place(abuf, 5, mask, fwd, bwd)

    def merid_parts(k, carry):
        for h in range(2):
            for i in range(2):
                row = 2 * h + i
                mx[h, k, i + 1] = wind(winds[k, 4 + row : 5 + row]) * abuf[h, k + lev, i]
        return carry

    lax.fori_loop(0, 4, merid_parts, 0)

    @pl.when(has_up)
    def _():
        merid_up.start()

    @pl.when(has_down)
    def _():
        merid_down.start()

    for i in range(2):
        for part in range(2):
            tl_out_cols[2 * i + part].wait_recv()
            physics(tcols, tback, i, part, False)
            tl_in_bands[2 * i + part].start()
    tband[lev] = tback[mine]

    def vert_parts(k, carry):
        for h in range(2):
            for i in range(2):
                row = 2 * h + i
                vx[h, k + 1, i] = wind(winds[k, 8 + row : 9 + row]) * abuf[h, k + lev, i]
        return carry

    lax.fori_loop(0, 4, vert_parts, 0)
    for h in range(2):
        for i in range(2):
            row = 2 * h + i
            vx[h, 5 * other, i] = wind(wext[row : row + 1]) * abuf[h, 4 * other, i]

    def zonal_parts(k, carry):
        for i in range(2):
            p = [abuf[h, k + lev, i] for h in range(2)]
            z = [wind(winds[k, 2 * h + i : 2 * h + i + 1]) * p[h] for h in range(2)]
            for h in range(2):
                total = lon_diff(z[h], z[1 - h]) + (vx[h, k + 2, i] - vx[h, k, i])
                partial[h, k, i] = p[h] + 0.5 * total
        return carry

    lax.fori_loop(0, 4, zonal_parts, 0)

    def join(pair):
        return jnp.concatenate([block[:, :half] for block in pair], axis=1)

    @pl.when(has_down)
    def _():
        merid_up.wait_recv()

    @pl.when(has_up)
    def _():
        merid_down.wait_recv()

    for k in range(4):
        for i in range(2):
            out_adj[:, k, i, :] = join(
                [
                    partial[h, k, i] + 0.5 * (mx[h, k, i + 2] - mx[h, k, i])
                    for h in range(2)
                ]
            )

    for i in range(2):
        for copy in tl_in_bands[2 * i : 2 * i + 2]:
            copy.wait_recv()
        for k in range(4):
            out_tl[:, k, i, :] = join([tband[h, k, i] for h in range(2)])

    for copy in [wind_halo] + adj_out_cols + adj_in_bands + tl_out_cols + tl_in_bands:
        copy.wait_send()

    @pl.when(has_up)
    def _():
        lat_up.wait_send()
        merid_up.wait_send()

    @pl.when(has_down)
    def _():
        lat_down.wait_send()
        merid_down.wait_send()


def hand_over(first, second, first_out, second_out, sems):
    copies = [
        pltpu.make_async_copy(first, first_out, sems.at[0]),
        pltpu.make_async_copy(second, second_out, sems.at[1]),
    ]
    for copy in copies:
        copy.start()
    for copy in copies:
        copy.wait()


def one_kernel(
    tl_pert,
    adj_in,
    zonal_wind,
    merid_wind,
    vert_wind,
    cutoffs,
    remap,
    phys_op,
    phys_state,
    column_cost,
):
    length = tl_pert.shape[3]
    half = length // 2
    padded = -(-half // LANES) * LANES
    bands = lax.axis_size("lat")
    forward, backward, layout = mode_tables(length, half, padded)
    vmem = pl.BlockSpec(memory_space=pltpu.VMEM)
    smem = pl.BlockSpec(memory_space=pltpu.SMEM)
    hbm = pl.BlockSpec(memory_space=pl.ANY)
    band_shape = (2, 4, 2, 8, padded)
    edged_shape = (2, 5, 2, 8, padded)
    column_shape = (8, 2, 8, padded)
    fields = [tl_pert, adj_in, zonal_wind, merid_wind, vert_wind, phys_state, phys_op, remap]
    done = pl.pallas_call(
        functools.partial(step_kernel, half, bands, layout),
        out_shape=[pltpu.VMEM(tl_pert.shape, F32)] * 2,
        in_specs=[smem] * 2 + [hbm] * 10,
        out_specs=[vmem] * 2,
        scratch_shapes=[pltpu.VMEM(field.shape, F32) for field in fields]
        + [
            pltpu.VMEM(forward.shape, BF16),
            pltpu.VMEM(backward.shape, BF16),
            pltpu.VMEM((4, 16, padded), F32),
            pltpu.VMEM((2, 6, 4, 8, padded), F32),
            pltpu.VMEM((8, padded), F32),
            pltpu.VMEM(band_shape, F32),
            pltpu.VMEM(column_shape, F32),
            pltpu.VMEM(edged_shape, F32),
            pltpu.VMEM(edged_shape, F32),
            pltpu.VMEM(column_shape, F32),
            pltpu.VMEM(column_shape, F32),
            pltpu.VMEM(band_shape, F32),
            pltpu.VMEM(edged_shape, F32),
            pltpu.VMEM((2, 4, 4, 8, padded), F32),
            pltpu.VMEM((2, 6, 2, 8, padded), F32),
            pltpu.VMEM(band_shape, F32),
            pltpu.VMEM((512, LANES), F32),
            pltpu.VMEM((128, 8, LANES), F32),
            pltpu.VMEM((2, 2, 8, MODES), F32),
            pltpu.SemaphoreType.DMA((21,)),
            pltpu.SemaphoreType.DMA((21,)),
            pltpu.SemaphoreType.DMA((10,)),
        ],
        compiler_params=pltpu.CompilerParams(
            collective_id=0, has_side_effects=True, vmem_limit_bytes=56 * 1024 * 1024
        ),
        cost_estimate=pl.CostEstimate(
            flops=10**9, bytes_accessed=8 * 10**6, transcendentals=0
        ),
    )(cutoffs, column_cost[:, 0], *fields, jnp.asarray(forward), jnp.asarray(backward))
    return pl.pallas_call(
        hand_over,
        out_shape=[jax.ShapeDtypeStruct(tl_pert.shape, F32)] * 2,
        in_specs=[hbm] * 2,
        out_specs=[hbm] * 2,
        scratch_shapes=[pltpu.SemaphoreType.DMA((2,))],
        compiler_params=pltpu.CompilerParams(vmem_limit_bytes=1024 * 1024),
    )(*done)


def fits_kernel(mesh):
    return mesh.shape["lev"] == 2 and mesh.shape["lat"] > 1


def solution(mesh):
    placed = (
        P(None, "lev", "lat", None),
        P(None, "lev", "lat", None),
        P("lev", "lat", None),
        P("lev", "lat", None),
        P("lev", "lat", None),
        P("lat"),
        P(),
        P(),
        P(None, "lat", "lev"),
        P("lat", "lev"),
    )
    return jax.shard_map(
        one_kernel if fits_kernel(mesh) else local,
        mesh=mesh,
        in_specs=placed,
        out_specs=(P(None, "lev", "lat", None), P(None, "lev", "lat", None)),
        check_vma=False,
    )
```
